32 devices in a mesh: seq: 8 (over z, x), tp: 4 (over y, core).
Axes of the slice: x: 2, y: 2, z: 4, core: 2. Of those that a mesh axis runs over, the one named last changes fastest.
Arguments:
- tokens: bfloat16 [2048, 4096], P('seq', 'tp'), may hold values from -6 to 6
- w_qkv: bfloat16 [3, 4096, 4096], P(None, None, 'tp'), may hold values from -0.09375 to 0.09375
- forget: float32 [2048, 32], P('seq', 'tp'), as said below
- out_grad: bfloat16 [2048, 4096], P('seq', 'tp'), may hold values from -6 to 6
- doc_lengths: int32 [16], replicated, may hold values from 1 to 1024, 2048 in all
Outputs:
- attn_out: float32 [2048, 4096], P('seq', 'tp')
- input_grad: float32 [2048, 4096], P('seq', 'tp')
The draws below stay inside these ranges and needn't reach their ends.
Inputs may be any that keep to these rules, and one draw needn't show every extreme that they name: `doc_lengths`: the documents' lengths in stream order; they sum to 2048, and the longest has exactly 1024 tokens. `forget`: log decay factors, all negative.
All inputs are finite; a program needn't handle non-finite values.
Results may differ from the reference program's by a relative error of at most 0.0046.
Values may be sent and summed in bfloat16 or wider, within the bound.
No kernel may reach another device: no remote copies, remote signals or barrier semaphores. Data moves between devices by JAX's collectives and lax.ppermute only.
A program may use at most 128 MiB of HBM per device.

```python
import math
import jax
import jax.numpy as jnp
import numpy as np
from jax import lax

D = 4096
ATTN_GROUPINGS = 32
DH = 128
TOK_DEV = 256
DOCS = 16
PACKED_LENGTH = 2048
MOST = 1024
BLOCK = 256


def draw_forget(key, part):
    sampling_rng_keys = jax.random.split(key, 7)
    fast_share = 0.5
    fast_heads = jax.random.uniform(sampling_rng_keys[0], (ATTN_GROUPINGS,)) < fast_share
    fast_rate = jnp.exp(jax.random.uniform(sampling_rng_keys[1], (ATTN_GROUPINGS,), minval=math.log(1.0 / 50.0), maxval=math.log(1.0 / 30.0)))
    slow_rate = jnp.exp(jax.random.uniform(sampling_rng_keys[2], (ATTN_GROUPINGS,), minval=math.log(0.05), maxval=math.log(0.4))) / PACKED_LENGTH
    forgetting_rate_param = jnp.where(fast_heads, fast_rate, slow_rate)
    segment_multiplier = jnp.exp(jax.random.uniform(sampling_rng_keys[3], (PACKED_LENGTH // TOK_DEV, 1), minval=math.log(0.5), maxval=0.0))
    segment_multiplier = jnp.repeat(segment_multiplier, TOK_DEV, axis=0)
    position_multiplier = jnp.exp(jax.random.uniform(sampling_rng_keys[4], (PACKED_LENGTH, ATTN_GROUPINGS), minval=-math.log(2.0), maxval=math.log(2.0)))
    document_spans = jax.random.uniform(sampling_rng_keys[5], (PACKED_LENGTH, ATTN_GROUPINGS)) < 2.0 / PACKED_LENGTH
    kept_fraction = jax.random.uniform(sampling_rng_keys[6], (PACKED_LENGTH, ATTN_GROUPINGS), minval=0.6, maxval=0.8)
    payload_vectors = -forgetting_rate_param[None, :] * segment_multiplier * position_multiplier + jnp.where(document_spans, jnp.log(kept_fraction), 0.0)
    return payload_vectors.astype(jnp.float32)


def steps_of(own_key, dims, pieces, smallest, top_value):
    def one(axis_at, parts):
        draws = jax.random.uniform(jax.random.fold_in(jax.random.fold_in(own_key, 6), axis_at), (parts,), jnp.float32, smallest / len(pieces), top_value / len(pieces))
        return jnp.repeat(jnp.exp(draws), dims[axis_at] // parts).reshape((-1,) + (1,) * (len(dims) - axis_at - 1))

    gain = one(*pieces[0])
    for cut in pieces[1:]:
        gain = gain * one(*cut)
    return gain


def profile(number_of, total, bound, skew):
    portions = [(1 << 20) // math.isqrt(rank ** skew) + 1 for rank in range(2, number_of + 1)]
    spare, counts = total - bound - (number_of - 1), [1] * (number_of - 1)
    while spare > 0:
        candidates = [i for i in range(number_of - 1) if counts[i] < bound]
        mass, budget = sum([portions[i] for i in candidates]), spare
        for i in candidates:
            extra = min(bound - counts[i], max(1, budget * portions[i] // mass), spare)
            counts[i] = counts[i] + extra
            spare = spare - extra
    return np.array([bound] + counts)


def ragged_sizes(stream_key, count, total, most, slope):
    if count == 2:
        one = jax.random.randint(stream_key, (), max(1, total - most), min(most, total - 1) + 1)
        return jnp.stack([one, total - one])
    sizes = jnp.asarray(profile(count, total, most, slope), jnp.int32)
    twos = (count - 1) // 2
    donor, sink = sizes[1:1 + 2 * twos:2], sizes[2:2 + 2 * twos:2]
    slack = jnp.minimum(donor - 1, most - sink)
    passed = jax.random.randint(jax.random.fold_in(stream_key, 1), (twos,), 0, 1 << 20) % (slack + 1)
    sizes = sizes.at[1:1 + 2 * twos:2].set(donor - passed).at[2:2 + 2 * twos:2].set(sink + passed)
    return sizes[jax.random.permutation(jax.random.fold_in(stream_key, 2), count)]


def gaussian(stream_key, shape, deviation, reach, shards=(), held_as=jnp.bfloat16):
    result = deviation * jax.random.normal(stream_key, shape, jnp.float32)
    if shards:
        result = result * steps_of(stream_key, shape, shards, -0.22, 0.18)
    return jnp.clip(result, -reach, reach).astype(held_as)


def setup_inputs(seed: int = 0) -> dict:
    streams_of = jax.random.split(jax.random.key(seed), 6)
    tokens = gaussian(streams_of[0], (PACKED_LENGTH, D), 1.0, 6.0, ((0, 8), (1, 4)))
    w_qkv = gaussian(streams_of[1], (3, D, ATTN_GROUPINGS * DH), D ** -0.5, 0.09375, ((2, 4),))
    forget = draw_forget(jax.random.fold_in(streams_of[5], 71), 0)
    out_grad = gaussian(streams_of[3], (PACKED_LENGTH, ATTN_GROUPINGS * DH), 1.0, 6.0, ((0, 8), (1, 4)))
    doc_lengths = ragged_sizes(streams_of[4], DOCS, PACKED_LENGTH, MOST, 2).astype(jnp.int32)
    return {"tokens": tokens, "w_qkv": w_qkv, "forget": forget, "out_grad": out_grad, "doc_lengths": doc_lengths}


HIGHEST = lax.Precision.HIGHEST

def document_ids(doc_lengths, positions):
    doc_ends = jnp.cumsum(doc_lengths).astype(jnp.int32)
    return lax.optimization_barrier(jnp.sum((positions[:, None] >= doc_ends[None, :]).astype(jnp.int32), axis=1)).astype(jnp.int32)

def head_forward(query_rows, key_rows, value_rows, log_decay, doc_ids):
    block_count = PACKED_LENGTH // BLOCK
    block_docs = doc_ids.reshape(block_count, BLOCK)
    prior_docs = jnp.concatenate([jnp.full((1,), -1, jnp.int32), block_docs[:-1, -1]]).astype(jnp.int32)
    lower = jnp.tril(jnp.ones((BLOCK, BLOCK), jnp.bool_))

    def advance(state_in, block_items):
        query_blk, key_blk, value_blk, decay_blk, docs_blk, prior_doc = block_items
        cumulative = jnp.cumsum(decay_blk)
        carried = docs_blk == prior_doc
        same_doc = (docs_blk[:, None] == docs_blk[None, :]) & lower
        log_gap = jnp.where(same_doc, cumulative[:, None] - cumulative[None, :], 0.0)
        weights = jnp.where(same_doc, jnp.exp(log_gap), 0.0)
        scores = jnp.dot(query_blk, key_blk.T, precision=HIGHEST) * weights
        intra_out = jnp.dot(scores, value_blk, precision=HIGHEST)
        lead_weight = jnp.where(carried, jnp.exp(cumulative), 0.0)
        inter_out = lead_weight[:, None] * jnp.dot(query_blk, state_in, precision=HIGHEST)
        tail_weight = jnp.where(docs_blk == docs_blk[-1], jnp.exp(cumulative[-1] - cumulative), 0.0)
        keep_state = jnp.where(carried[-1], jnp.exp(cumulative[-1]), 0.0)
        state_out = keep_state * state_in + jnp.dot((key_blk * tail_weight[:, None]).T, value_blk, precision=HIGHEST)
        return (state_out, (intra_out + inter_out) / DH)
    zero_state = jnp.zeros((DH, DH), jnp.float32)
    block_items = (query_rows.reshape(block_count, BLOCK, DH), key_rows.reshape(block_count, BLOCK, DH), value_rows.reshape(block_count, BLOCK, DH), log_decay.reshape(block_count, BLOCK), block_docs, prior_docs)
    outputs = lax.scan(advance, zero_state, block_items)[1]
    return outputs.reshape(PACKED_LENGTH, DH)

def reference(tokens, w_qkv, forget, out_grad, doc_lengths):
    positions = jnp.arange(PACKED_LENGTH, dtype=jnp.int32)
    doc_ids = document_ids(doc_lengths, positions)
    projected = [jnp.dot(tokens, w_qkv[proj_index], preferred_element_type=jnp.float32).astype(jnp.bfloat16) for proj_index in range(3)]

    def per_head(matrix):
        return matrix.astype(jnp.float32).reshape(PACKED_LENGTH, ATTN_GROUPINGS, DH).transpose(1, 0, 2)

    def head_pass(head_items):
        query_rows, key_rows, value_rows, log_decay, grad_rows = head_items

        def forward(query_in, key_in, value_in):
            return head_forward(query_in, key_in, value_in, log_decay, doc_ids)
        outputs, pullback = jax.vjp(forward, query_rows, key_rows, value_rows)
        grad_query, grad_key, grad_value = pullback(grad_rows)
        return (outputs, grad_query, grad_key, grad_value)
    outputs, grad_query, grad_key, grad_value = lax.map(head_pass, (per_head(projected[0]), per_head(projected[1]), per_head(projected[2]), forget.T, per_head(out_grad)))

    def merge_heads(stack):
        return stack.transpose(1, 0, 2).reshape(PACKED_LENGTH, ATTN_GROUPINGS * DH)
    grads_merged = [merge_heads(grad_stack).astype(jnp.bfloat16) for grad_stack in (grad_query, grad_key, grad_value)]
    attn_out = merge_heads(outputs).astype(jnp.float32)
    grad_terms = jnp.zeros((PACKED_LENGTH, D), jnp.float32)
    for proj_index in range(3):
        grad_terms = grad_terms + jnp.dot(grads_merged[proj_index], w_qkv[proj_index].T, preferred_element_type=jnp.float32)
    return (attn_out, grad_terms)
```

```python
import functools

import jax
import jax.numpy as jnp
from jax import lax
from jax.experimental import pallas as pl
from jax.experimental.pallas import tpu as pltpu
from jax.sharding import PartitionSpec as P

DH = 128
F32 = jnp.float32
BF16 = jnp.bfloat16
MIB = 1 << 20


def dot(a, b, ca, cb):
    return lax.dot_general(a, b, (((ca,), (cb,)), ((), ())), preferred_element_type=F32)


def split(a):
    high = a.astype(BF16)
    return high, (a - high.astype(F32)).astype(BF16)


def dot_split(a, b, ca, cb):
    high, low = split(a)
    return dot(high, b, ca, cb) + dot(low, b, ca, cb)


def call(kernel, name, outs, args, spaces=None, flops=0, nbytes=0, limit=16, scratch=()):
    spaces = spaces or ["v"] * len(args)
    kinds = {"v": pltpu.VMEM, "s": pltpu.SMEM, "a": pl.ANY}
    placed = [
        pltpu.with_memory_space_constraint(a, pltpu.VMEM) if s == "v" else a
        for a, s in zip(args, spaces)
    ]
    return pl.pallas_call(
        kernel,
        name=name,
        out_shape=[pltpu.VMEM(shape, dtype) for shape, dtype in outs],
        in_specs=[pl.BlockSpec(memory_space=kinds[s]) for s in spaces],
        out_specs=[pl.BlockSpec(memory_space=pltpu.VMEM)] * len(outs),
        scratch_shapes=scratch,
        compiler_params=pltpu.CompilerParams(vmem_limit_bytes=limit * MIB),
        cost_estimate=pl.CostEstimate(flops=flops, bytes_accessed=nbytes, transcendentals=0),
    )(*placed)


def tile_of(width):
    return 256 if width % 256 == 0 else 128


def load_and_project(starts, own, other, w, w_vm, acc, sems):
    part, count = own.shape[1], w.shape[1] // own.shape[1]
    width = w.shape[2]
    tile = tile_of(width)
    copies = []
    for j in range(count):
        rows = pl.ds(pl.multiple_of(starts[j] * part, part), part)
        copies.append(pltpu.make_async_copy(w.at[:, rows, :], w_vm.at[:, rows, :], sems.at[j]))
        copies[-1].start()
    for j, x in enumerate((own, other)):
        copies[j].wait()
        rows = pl.ds(pl.multiple_of(starts[j] * part, part), part)

        @pl.loop(0, 3 * (width // tile))
        def _(n):
            m, cols = n // (width // tile), pl.ds(pl.multiple_of(n % (width // tile) * tile, tile), tile)
            term = dot(x[...], w_vm[m, rows, cols], 1, 0)
            if j:
                acc[m, :, cols] += term
            else:
                acc[m, :, cols] = term

    for j in range(2, count):
        copies[j].wait()


def project_more(starts, x, w_vm, acc_in, acc):
    part, width = x.shape[1], w_vm.shape[2]
    tile = tile_of(width)
    rows = pl.ds(pl.multiple_of(starts[2] * part, part), part)

    @pl.loop(0, 3 * (width // tile))
    def _(n):
        m, cols = n // (width // tile), pl.ds(pl.multiple_of(n % (width // tile) * tile, tile), tile)
        acc[m, :, cols] = acc_in[m, :, cols] + dot(x[...], w_vm[m, rows, cols], 1, 0)


def project_last(starts, x, w_vm, acc_in, grads, cols_h, qkv, states):
    part, width = x.shape[1], w_vm.shape[2]
    tile = tile_of(width)
    rows = pl.ds(pl.multiple_of(starts[3] * part, part), part)

    @pl.loop(0, 3 * (width // tile))
    def _(n):
        m, cols = n // (width // tile), pl.ds(pl.multiple_of(n % (width // tile) * tile, tile), tile)
        qkv[m, :, cols] = (acc_in[m, :, cols] + dot(x[...], w_vm[m, rows, cols], 1, 0)).astype(BF16)

    own_states(qkv, grads, cols_h, states)


def own_states(qkv, grads, cols_h, states):
    @pl.loop(0, states.shape[1])
    def _(h):
        cols = pl.ds(pl.multiple_of(h * DH, DH), DH)
        col = cols_h[h]
        lead, tail = col[:, 1:2], col[:, 2:3]
        states[0, h] = dot_split(qkv[1, :, cols].astype(F32) * tail, qkv[2, :, cols], 0, 0)
        states[1, h] = dot_split(qkv[0, :, cols].astype(F32) * lead, grads[:, cols], 0, 0) * (1.0 / DH)


def project_whole(x, w, qkv):
    qkv[0] = dot(x[...], w[0], 1, 0).astype(BF16)


def intra(qkv, grads, cols_h, rows_h, first, out, gq, gk, gv):
    length = first.shape[0]
    t = lax.broadcasted_iota(jnp.int32, (length, length), 0)
    s = lax.broadcasted_iota(jnp.int32, (length, length), 1)
    mask = (s <= t) & (s >= first[...])

    @pl.loop(0, cols_h.shape[0])
    def _(h):
        cols = pl.ds(pl.multiple_of(h * DH, DH), DH)
        gap = jnp.where(mask, cols_h[h][:, 0:1] - rows_h[h], 0.0)
        weight = jnp.where(mask, jnp.exp(gap), 0.0)
        q, k, v, g = qkv[0, :, cols], qkv[1, :, cols], qkv[2, :, cols], grads[:, cols]
        scores = split(dot(q, k, 1, 1) * weight)
        dots = split(dot(g, v, 1, 1) * weight)
        out[:, cols] = dot(scores[0], v, 1, 0) + dot(scores[1], v, 1, 0)
        gq[:, cols] = dot(dots[0], k, 1, 0) + dot(dots[1], k, 1, 0)
        gk[:, cols] = dot(dots[0], q, 0, 0) + dot(dots[1], q, 0, 0)
        gv[:, cols] = dot(scores[0], g, 0, 0) + dot(scores[1], g, 0, 0)


def finish(qkv, grads, cols_h, out, gq, gk, gv, states, ends, attn, gstack):
    @pl.loop(0, cols_h.shape[0])
    def _(h):
        cols = pl.ds(pl.multiple_of(h * DH, DH), DH)
        col = cols_h[h]
        lead, tail = col[:, 1:2], col[:, 2:3]
        q, k, v, g = qkv[0, :, cols], qkv[1, :, cols], qkv[2, :, cols], grads[:, cols]
        state, end = states[h], ends[h]
        attn[:, cols] = (out[:, cols] + dot(q, state, 1, 0) * lead) * (1.0 / DH)
        gstack[0, :, cols] = ((gq[:, cols] + dot(g, state, 1, 1) * lead) * (1.0 / DH)).astype(BF16)
        gstack[1, :, cols] = (gk[:, cols] * (1.0 / DH) + dot(v, end, 1, 1) * tail).astype(BF16)
        gstack[2, :, cols] = (gv[:, cols] * (1.0 / DH) + dot(k, end, 1, 0) * tail).astype(BF16)


def back(starts, which, gstack, w_vm, out):
    part = out.shape[1]
    base = starts[which] * part
    tile = tile_of(part)

    @pl.loop(0, part // tile)
    def _(n):
        rows = pl.ds(pl.multiple_of(base + n * tile, tile), tile)
        total = dot(gstack[0], w_vm[0, rows, :], 1, 1)
        total += dot(gstack[1], w_vm[1, rows, :], 1, 1)
        total += dot(gstack[2], w_vm[2, rows, :], 1, 1)
        out[:, pl.ds(pl.multiple_of(n * tile, tile), tile)] = total.astype(out.dtype)


def back_first(starts, qkv, grads, cols_h, out, gq, gk, gv, states, ends, w_vm, attn, gstack, chunk):
    finish(qkv, grads, cols_h, out, gq, gk, gv, states, ends, attn, gstack)
    back(starts, 3, gstack, w_vm, chunk)


def back_second(starts, gstack, w_vm, chunk):
    back(starts, 2, gstack, w_vm, chunk)


def back_rest(starts, gstack, w_vm, chunk_other, chunk_own):
    back(starts, 1, gstack, w_vm, chunk_other)
    back(starts, 0, gstack, w_vm, chunk_own)


def per_head(scale, matrix):
    return scale[..., None, None] * matrix


def states_direct(own, through):
    heads = own.shape[1]
    half = heads // 2
    place = lax.axis_index("seq")
    x, z = place % 2, place // 2
    upper = x == 1
    mate = [(i, i ^ 1) for i in range(8)]
    near = [(i, i ^ 2) for i in range(8)]
    middle = [(2, 4), (4, 2), (3, 5), (5, 3)]
    far = [(i, i ^ 4) for i in range(8)]

    def shift(a, pairs):
        return lax.ppermute(a, "seq", pairs)

    mine = lax.dynamic_slice_in_dim(own, x * half, half, 1)
    theirs = lax.dynamic_slice_in_dim(own, (1 - x) * half, half, 1)
    mate_through = shift(through, mate)
    pair_through = through * mate_through
    near_through = shift(pair_through, near)
    middle_through = shift(pair_through, middle)
    next_through = jnp.where((z == 0) | (z == 3), near_through, middle_through)
    low_through = lax.dynamic_slice_in_dim(jnp.where(upper, mate_through, through), x * half, half, 0)
    high_through = lax.dynamic_slice_in_dim(jnp.where(upper, through, mate_through), x * half, half, 0)
    next_through = lax.dynamic_slice_in_dim(next_through, x * half, half, 0)

    got = shift(theirs.astype(BF16), mate).astype(F32)
    low, high = jnp.where(upper, got, mine), jnp.where(upper, mine, got)
    pair_state = high[0] + per_head(high_through, low[0])
    pair_grad = low[1] + per_head(low_through, high[1])
    to_near = jnp.where(z % 2 == 0, pair_state, pair_grad).astype(BF16)
    to_middle = jnp.where(z == 1, pair_state, pair_grad).astype(BF16)
    to_far = jnp.where(z < 2, pair_state, pair_grad).astype(BF16)
    from_near = shift(to_near, near).astype(F32)
    from_middle = shift(to_middle, middle).astype(F32)
    from_far = shift(to_far, far).astype(F32)
    from_far = per_head(next_through, from_far)
    zero = jnp.zeros_like(from_near)
    inner_far = from_middle + from_far
    state = jnp.where(z == 0, zero, jnp.where(z == 1, from_near, jnp.where(z == 2, inner_far, from_near + from_far)))
    grad = jnp.where(z == 3, zero, jnp.where(z == 2, from_near, jnp.where(z == 1, inner_far, from_near + from_far)))
    low_pair = jnp.stack([state, high[1] + per_head(high_through, grad)]).astype(BF16)
    high_pair = jnp.stack([low[0] + per_head(low_through, state), grad]).astype(BF16)
    kept = jnp.where(upper, high_pair, low_pair)
    passed = shift(jnp.where(upper, low_pair, high_pair), mate)
    both = jnp.where(
        upper, jnp.concatenate([passed, kept], axis=1), jnp.concatenate([kept, passed], axis=1)
    )
    return both[0], both[1]


def states_gathered(own, through):
    count = lax.axis_size("seq")
    place = lax.axis_index("seq")
    all_own = lax.all_gather(own, "seq")
    all_through = lax.all_gather(through, "seq")

    def pick(a, i):
        return lax.dynamic_index_in_dim(a, i, 0, False)

    def ahead(step, state):
        return per_head(pick(all_through, step), state) + pick(all_own, step)[0]

    def behind(step, state):
        source = count - 1 - step
        return per_head(pick(all_through, source), state) + pick(all_own, source)[1]

    zero = jnp.zeros_like(own[0])
    state = lax.fori_loop(0, place, ahead, zero)
    grad = lax.fori_loop(0, count - 1 - place, behind, zero)
    return state.astype(BF16), grad.astype(BF16)


def local(tokens, w_qkv, forget, out_grad, doc_lengths):
    length, part = tokens.shape
    width = w_qkv.shape[2]
    heads = width // DH
    depth = w_qkv.shape[1]
    tps = lax.axis_size("tp")
    tp = lax.axis_index("tp")
    seqs = lax.axis_size("seq")
    offset = lax.axis_index("seq") * length
    by_hand = tps == 4

    positions = offset + jnp.arange(length, dtype=jnp.int32)
    doc_ends = jnp.cumsum(doc_lengths)
    past = positions[:, None] >= doc_ends[None, :]
    first = jnp.max(jnp.where(past, doc_ends[None, :], 0), axis=1) - offset
    carried = first < 0
    total = jnp.cumsum(forget, axis=0)
    lead = jnp.where(carried[:, None], jnp.exp(total), 0.0)
    tail = jnp.where((first == first[-1])[:, None], jnp.exp(total[-1][None, :] - total), 0.0)
    through = jnp.where(carried[-1], jnp.exp(total[-1]), 0.0)
    cols_h = jnp.stack([total.T, lead.T, tail.T], axis=-1)
    rows_h = total.T[:, None, :]
    first = first[:, None]

    qkv_shape = ((3, length, width), BF16)
    states_shape = ((2, heads, DH, DH), F32)
    if by_hand:
        starts = jnp.stack([tp, tp ^ 1, tp ^ 2, tp ^ 3]).astype(jnp.int32)
        core = [(i, i ^ 1) for i in range(4)]
        chip = [(i, i ^ 2) for i in range(4)]
        step_flops = 2 * 3 * length * part * width
        across = lax.ppermute(tokens, "tp", chip)
        beside = lax.ppermute(tokens, "tp", core)
        across_beside = lax.ppermute(across, "tp", core)
        w_vm, acc = call(
            load_and_project,
            "load_and_project",
            [(w_qkv.shape, BF16), ((3, length, width), F32)],
            [starts, tokens, beside, w_qkv],
            ["s", "v", "v", "a"],
            flops=2 * step_flops,
            nbytes=w_qkv.size * 2,
            scratch=[pltpu.SemaphoreType.DMA((4,))],
        )
        (acc,) = call(
            project_more, "project_more", [(acc.shape, F32)], [starts, across, w_vm, acc],
            ["s", "v", "v", "v"], flops=step_flops,
        )
        qkv, own = call(
            project_last,
            "project_last",
            [qkv_shape, states_shape],
            [starts, across_beside, w_vm, acc, out_grad, cols_h],
            ["s", "v", "v", "v", "v", "v"],
            flops=step_flops,
        )
    else:
        gathered = lax.all_gather(tokens, "tp", axis=1, tiled=True)
        qkv = jnp.einsum("td,mdc->mtc", gathered, w_qkv, preferred_element_type=F32).astype(BF16)
        (own,) = call(own_states, "own_states", [states_shape], [qkv, out_grad, cols_h])

    out, gq, gk, gv = call(
        intra,
        "intra",
        [((length, width), F32)] * 4,
        [qkv, out_grad, cols_h, rows_h, first],
        flops=16 * length * length * width,
    )
    states, ends = states_direct(own, through) if seqs == 8 and heads % 2 == 0 else states_gathered(own, through)

    attn_shape = ((length, width), F32)
    finish_args = [qkv, out_grad, cols_h, out, gq, gk, gv, states, ends]
    if by_hand:
        attn, gstack, chunk = call(
            back_first,
            "back_first",
            [attn_shape, qkv_shape, ((length, part), BF16)],
            [starts] + finish_args + [w_vm],
            ["s"] + ["v"] * 10,
            flops=step_flops,
        )
        beside = lax.ppermute(chunk, "tp", core)
        (chunk,) = call(
            back_second, "back_second", [((length, part), F32)], [starts, gstack, w_vm], ["s", "v", "v"], flops=step_flops
        )
        across = lax.ppermute((chunk + beside.astype(F32)).astype(BF16), "tp", chip)
        chunk_other, chunk_own = call(
            back_rest,
            "back_rest",
            [((length, part), BF16), ((length, part), F32)],
            [starts, gstack, w_vm],
            ["s", "v", "v"],
            flops=2 * step_flops,
        )
        beside = lax.ppermute(chunk_other, "tp", core)
        input_grad = chunk_own + beside.astype(F32) + across.astype(F32)
    else:
        attn, gstack = call(finish, "finish", [attn_shape, qkv_shape], finish_args)
        grad_terms = jnp.einsum("mtc,mdc->td", gstack, w_qkv, preferred_element_type=F32)
        input_grad = lax.psum_scatter(grad_terms, "tp", scatter_dimension=1, tiled=True)
    return (attn, input_grad)


def solution(mesh):
    placed = (P("seq", "tp"), P(None, None, "tp"), P("seq", "tp"), P("seq", "tp"), P())
    return jax.shard_map(
        local,
        mesh=mesh,
        in_specs=placed,
        out_specs=(P("seq", "tp"), P("seq", "tp")),
        check_vma=False,
    )
```

```python
import jax
import jax.numpy as jnp
from jax import lax
from jax.experimental import pallas as pl
from jax.experimental.pallas import tpu as pltpu
from jax.sharding import PartitionSpec as P

DH = 128
F32 = jnp.float32
BF16 = jnp.bfloat16
MIB = 1 << 20


def dot(a, b, ca, cb):
    return lax.dot_general(a, b, (((ca,), (cb,)), ((), ())), preferred_element_type=F32)


def split(a):
    high = a.astype(BF16)
    return high, (a - high.astype(F32)).astype(BF16)


def dot_split(a, b, ca, cb):
    high, low = split(a)
    return dot(high, b, ca, cb) + dot(low, b, ca, cb)


def call(kernel, name, outs, args, spaces=None, flops=0, limit=4, aliases=None, scratch=()):
    spaces = spaces or ["v"] * len(args)
    kinds = {"v": pltpu.VMEM, "s": pltpu.SMEM, "a": pl.ANY}
    placed = [
        pltpu.with_memory_space_constraint(a, pltpu.VMEM) if s == "v" else a
        for a, s in zip(args, spaces)
    ]
    return pl.pallas_call(
        kernel,
        name=name,
        out_shape=[pltpu.VMEM(shape, dtype) for shape, dtype in outs],
        in_specs=[pl.BlockSpec(memory_space=kinds[s]) for s in spaces],
        out_specs=[pl.BlockSpec(memory_space=pltpu.VMEM)] * len(outs),
        input_output_aliases=aliases or {},
        scratch_shapes=scratch,
        compiler_params=pltpu.CompilerParams(vmem_limit_bytes=limit * MIB),
        cost_estimate=pl.CostEstimate(flops=flops, bytes_accessed=0, transcendentals=0),
    )(*placed)


def tiles(width):
    tile = 256 if width % 256 == 0 else 128
    return [slice(i, i + tile) for i in range(0, width, tile)]


def rows_of(starts, which, part):
    return pl.ds(pl.multiple_of(starts[which] * part, part), part)


def prepare(starts, lengths, forget, cols_h, rows_h, through):
    count, heads = forget.shape
    offset = starts[6]
    t = lax.broadcasted_iota(jnp.int32, (count, count), 0)
    s = lax.broadcasted_iota(jnp.int32, (count, count), 1)
    lower = jnp.where(s <= t, 1.0, 0.0).astype(BF16)
    high, rest = split(forget[...])
    rest = forget[...] - high.astype(F32)
    middle, low = split(rest)
    total = dot(lower, high, 1, 0) + (dot(lower, middle, 1, 0) + dot(lower, low, 1, 0))
    rows = dot(high, lower, 0, 1) + (dot(middle, lower, 0, 1) + dot(low, lower, 0, 1))
    position = offset + lax.broadcasted_iota(jnp.int32, (count, 1), 0)
    first, end = jnp.zeros((count, 1), jnp.int32), jnp.int32(0)
    for j in range(lengths.shape[0]):
        end = end + lengths[j]
        first = jnp.where(position >= end, end, first)
    first = first - offset
    last = first[count - 1 :, :]
    final = total[count - 1 :, :]
    rows_h[...] = rows
    cols_h[:, :heads] = total
    cols_h[:, heads : 2 * heads] = jnp.where(first < 0, jnp.exp(total), 0.0)
    cols_h[:, 2 * heads : 3 * heads] = jnp.where(first == last, jnp.exp(jnp.where(first == last, final - total, 0.0)), 0.0)
    cols_h[:, 3 * heads : 3 * heads + 1] = first.astype(F32)
    factor = jnp.where(last < 0, jnp.exp(rows[:, count - 1 :]), 0.0)
    factor = jnp.broadcast_to(factor, (heads, DH))
    through[...] = jnp.concatenate(split(factor), axis=0)


def load_and_project(starts, lengths, forget, own, other, w, w_vm, acc, cols_h, rows_h, through, sems):
    part = own.shape[1]
    copies = []
    for j in range(w.shape[1] // part):
        rows = rows_of(starts, j, part)
        copies.append(pltpu.make_async_copy(w.at[:, rows, :], w_vm.at[:, rows, :], sems.at[j]))
        copies[-1].start()
    prepare(starts, lengths, forget, cols_h, rows_h, through)
    for j, x in enumerate((own, other)):
        copies[j].wait()
        for m in range(3):
            for cols in tiles(w.shape[2]):
                term = dot(x[...], w_vm[m, rows_of(starts, j, part), cols], 1, 0)
                acc[m, :, cols] = acc[m, :, cols] + term if j else term
    for copy in copies[2:]:
        copy.wait()


def project_more(starts, x, w, acc_in, acc):
    part = x.shape[1]
    for m in range(3):
        for cols in tiles(w.shape[2]):
            acc[m, :, cols] = acc_in[m, :, cols] + dot(x[...], w[m, rows_of(starts, 2, part), cols], 1, 0)


def project_last(starts, x, w, acc_in, grads, cols_h, own_through, qkv, mine, message):
    part = x.shape[1]
    for m in range(3):
        for cols in tiles(w.shape[2]):
            term = dot(x[...], w[m, rows_of(starts, 3, part), cols], 1, 0)
            qkv[m, :, cols] = (acc_in[m, :, cols] + term).astype(BF16)
    half = mine.shape[1]
    upper = starts[4]
    for h in range(2 * half):
        state = own_state(qkv, grads, cols_h, h)
        kept = (h >= half) == (upper == 1)

        @pl.when(kept)
        def _():
            mine[0, h % half], mine[1, h % half] = state

        @pl.when(jnp.logical_not(kept))
        def _():
            for i in range(2):
                message[(i * half + h % half) * DH : (i * half + h % half + 1) * DH, :] = state[i].astype(BF16)

    message[2 * half * DH :, :] = own_through[...]


def columns(cols_h, h):
    heads = cols_h.shape[1] // 3
    return [cols_h[:, i * heads + h : i * heads + h + 1] for i in range(3)]


def own_state(qkv, grads, cols_h, h):
    cols = slice(h * DH, (h + 1) * DH)
    lead, tail = columns(cols_h, h)[1:]
    state = dot_split(qkv[1, :, cols].astype(F32) * tail, qkv[2, :, cols], 0, 0)
    grad = dot_split(qkv[0, :, cols].astype(F32) * lead, grads[:, cols], 0, 0) * (1.0 / DH)
    return state, grad


def own_states(qkv, grads, cols_h, states):
    for h in range(states.shape[1]):
        states[0, h], states[1, h] = own_state(qkv, grads, cols_h, h)


def intra(qkv, grads, cols_h, rows_h, out, gq, gk, gv):
    length, heads = qkv.shape[1], rows_h.shape[0]
    t = lax.broadcasted_iota(jnp.int32, (length, length), 0)
    s = lax.broadcasted_iota(jnp.int32, (length, length), 1)
    mask = (s <= t) & (s.astype(F32) >= cols_h[:, 3 * heads : 3 * heads + 1])
    for h in range(heads):
        cols = slice(h * DH, (h + 1) * DH)
        gap = jnp.where(mask, columns(cols_h, h)[0] - rows_h[h : h + 1, :], 0.0)
        weight = jnp.where(mask, jnp.exp(gap), 0.0)
        q, k, v, g = qkv[0, :, cols], qkv[1, :, cols], qkv[2, :, cols], grads[:, cols]
        scores = split(dot(q, k, 1, 1) * weight)
        dots = split(dot(g, v, 1, 1) * weight)
        out[:, cols] = dot(scores[0], v, 1, 0) + dot(scores[1], v, 1, 0)
        gq[:, cols] = dot(dots[0], k, 1, 0) + dot(dots[1], k, 1, 0)
        gk[:, cols] = dot(dots[0], q, 0, 0) + dot(dots[1], q, 0, 0)
        gv[:, cols] = dot(scores[0], g, 0, 0) + dot(scores[1], g, 0, 0)


def finish(qkv, grads, cols_h, out, gq, gk, gv, state_of, attn, gstack):
    for h in range(qkv.shape[2] // DH):
        cols = slice(h * DH, (h + 1) * DH)
        lead, tail = columns(cols_h, h)[1:]
        q, k, v, g = qkv[0, :, cols], qkv[1, :, cols], qkv[2, :, cols], grads[:, cols]
        state, end = state_of(0, h), state_of(1, h)
        attn[:, cols] = (out[:, cols] + dot(q, state, 1, 0) * lead) * (1.0 / DH)
        gstack[0, :, cols] = ((gq[:, cols] + dot(g, state, 1, 1) * lead) * (1.0 / DH)).astype(BF16)
        gstack[1, :, cols] = (gk[:, cols] * (1.0 / DH) + dot(v, end, 1, 1) * tail).astype(BF16)
        gstack[2, :, cols] = (gv[:, cols] * (1.0 / DH) + dot(k, end, 1, 0) * tail).astype(BF16)


def finish_whole(qkv, grads, cols_h, out, gq, gk, gv, both, attn, gstack):
    finish(qkv, grads, cols_h, out, gq, gk, gv, lambda i, h: both[i, h], attn, gstack)


def back(starts, which, gstack, w, out):
    part = out.shape[1]
    for cols in tiles(part):
        rows = pl.ds(pl.multiple_of(starts[which] * part + cols.start, cols.stop - cols.start), cols.stop - cols.start)
        total = dot(gstack[0], w[0, rows, :], 1, 1)
        total += dot(gstack[1], w[1, rows, :], 1, 1)
        total += dot(gstack[2], w[2, rows, :], 1, 1)
        out[:, cols] = total.astype(out.dtype)


def back_first(starts, qkv, grads, cols_h, out, gq, gk, gv, kept, passed, w, attn, gstack, chunk):
    half = kept.shape[1]
    upper = starts[4] == 1

    def state_of(i, h):
        mine = (h >= half) == upper
        return jnp.where(mine, kept[i, h % half], passed[i, h % half])

    finish(qkv, grads, cols_h, out, gq, gk, gv, state_of, attn, gstack)
    back(starts, 3, gstack, w, chunk)


def back_second(starts, gstack, w, chunk):
    back(starts, 2, gstack, w, chunk)


def back_rest(starts, gstack, w, chunk_other, chunk_own):
    back(starts, 1, gstack, w, chunk_other)
    back(starts, 0, gstack, w, chunk_own)


def per_head(scale, matrix):
    return scale[..., None, None] * matrix


def head_factors(rows):
    half = rows.shape[0] // 2
    return rows[:half].astype(F32) + rows[half:].astype(F32)


def pair_kernel(starts, own_through, mine, got, to_near, to_middle, to_far, mate_through):
    half = mine.shape[1]
    upper, z = starts[4] == 1, starts[5]
    own, mate = head_factors(own_through[...]), head_factors(got[2 * half * DH :, :])
    mate_through[...] = mate
    low, high = jnp.where(upper, mate, own), jnp.where(upper, own, mate)
    first = jnp.where(upper, half, 0)
    joint = split(own * mate)
    ends = jnp.concatenate(joint, axis=0)
    for to in (to_near, to_middle, to_far):
        to[half * DH :, :] = ends
    for j in range(half):
        rows = slice(j * DH, (j + 1) * DH)
        got_state = got[j * DH : (j + 1) * DH, :].astype(F32)
        got_grad = got[(half + j) * DH : (half + j + 1) * DH, :].astype(F32)
        low_j = jnp.where(upper, low[half + j : half + j + 1], low[j : j + 1])
        high_j = jnp.where(upper, high[half + j : half + j + 1], high[j : j + 1])
        state = jnp.where(upper, mine[0, j] + high_j * got_state, got_state + high_j * mine[0, j]).astype(BF16)
        grad = jnp.where(upper, got_grad + low_j * mine[1, j], mine[1, j] + low_j * got_grad).astype(BF16)
        to_near[rows, :] = jnp.where(z % 2 == 0, state, grad)
        to_middle[rows, :] = jnp.where(z == 1, state, grad)
        to_far[rows, :] = jnp.where(z < 2, state, grad)


def spread_kernel(starts, own_through, mate_through, mine, got, near, middle, far, kept, passed):
    half = mine.shape[1]
    upper, z = starts[4] == 1, starts[5]
    own, mate = head_factors(own_through[...]), mate_through[...]
    low, high = jnp.where(upper, mate, own), jnp.where(upper, own, mate)
    inner = (z == 1) | (z == 2)
    step = head_factors(jnp.where(inner, middle[half * DH :, :], near[half * DH :, :]))
    for j in range(half):
        rows = slice(j * DH, (j + 1) * DH)

        def factor(a):
            return jnp.where(upper, a[half + j : half + j + 1], a[j : j + 1])

        close = near[rows, :].astype(F32)
        beyond = jnp.where(inner, middle[rows, :], near[rows, :]).astype(F32) + factor(step) * far[rows, :].astype(F32)
        state = jnp.where(z == 0, 0.0, jnp.where(z == 1, close, beyond))
        grad = jnp.where(z == 3, 0.0, jnp.where(z == 2, close, beyond))
        got_state = got[j * DH : (j + 1) * DH, :].astype(F32)
        got_grad = got[(half + j) * DH : (half + j + 1) * DH, :].astype(F32)
        low_state, high_grad = jnp.where(upper, got_state, mine[0, j]), jnp.where(upper, mine[1, j], got_grad)
        high_in = (low_state + factor(low) * state).astype(BF16)
        low_in = (high_grad + factor(high) * grad).astype(BF16)
        state, grad = state.astype(BF16), grad.astype(BF16)
        kept[0, j], passed[0, j] = jnp.where(upper, high_in, state), jnp.where(upper, state, high_in)
        kept[1, j], passed[1, j] = jnp.where(upper, grad, low_in), jnp.where(upper, low_in, grad)


def states_direct(starts, own_through, mine, message, inside):
    half = mine.shape[1]
    mate = [(i, i ^ 1) for i in range(8)]
    near = [(i, i ^ 2) for i in range(8)]
    middle = [(2, 4), (4, 2), (3, 5), (5, 3)]
    far = [(i, i ^ 4) for i in range(8)]
    got = lax.ppermute(message, "seq", mate)
    to = ((half * DH + own_through.shape[0], DH), BF16)
    to_near, to_middle, to_far, mate_through = call(
        pair_kernel,
        "pair",
        [to, to, to, ((2 * half, DH), F32)],
        [starts, own_through, mine, got],
        ["s", "v", "v", "v"],
    )
    from_far = lax.ppermute(to_far, "seq", far)
    from_middle = lax.ppermute(to_middle, "seq", middle)
    from_near = lax.ppermute(to_near, "seq", near)
    inside, mine = lax.optimization_barrier((inside, mine))
    kept, passed = call(
        spread_kernel,
        "spread",
        [(mine.shape, BF16), (mine.shape, BF16)],
        [starts, own_through, mate_through, mine, got, from_near, from_middle, from_far],
        ["s"] + ["v"] * 7,
    )
    return kept, lax.ppermute(passed, "seq", mate), inside


def states_gathered(own, through):
    count = lax.axis_size("seq")
    place = lax.axis_index("seq")
    all_own = lax.all_gather(own, "seq")
    all_through = lax.all_gather(through, "seq")

    def pick(a, i):
        return lax.dynamic_index_in_dim(a, i, 0, False)

    def ahead(step, state):
        return per_head(pick(all_through, step), state) + pick(all_own, step)[0]

    def behind(step, state):
        source = count - 1 - step
        return per_head(pick(all_through, source), state) + pick(all_own, source)[1]

    zero = jnp.zeros_like(own[0])
    state = lax.fori_loop(0, place, ahead, zero)
    grad = lax.fori_loop(0, count - 1 - place, behind, zero)
    return jnp.stack([state, grad]).astype(BF16)


def local(tokens, w_qkv, forget, out_grad, doc_lengths):
    length, part = tokens.shape
    width = w_qkv.shape[2]
    heads = width // DH
    tps = lax.axis_size("tp")
    tp = lax.axis_index("tp")
    seqs = lax.axis_size("seq")
    place = lax.axis_index("seq")
    starts = jnp.stack([tp, tp ^ 1, tp ^ 2, tp ^ 3, place % 2, place // 2, place * length]).astype(jnp.int32)
    decays = [((length, 3 * heads + 1), F32), ((heads, length), F32), ((2 * heads, DH), BF16)]
    qkv_shape = ((3, length, width), BF16)
    sum_shape = ((length, width), F32)
    by_hand = tps == 4 and seqs == 8 and heads % 8 == 0
    if by_hand:
        half = heads // 2
        core = [(i, i ^ 1) for i in range(4)]
        chip = [(i, i ^ 2) for i in range(4)]
        step_flops = 2 * 3 * length * part * width
        across = lax.ppermute(tokens, "tp", chip)
        beside = lax.ppermute(tokens, "tp", core)
        w_vm, acc, cols_h, rows_h, own_through = call(
            load_and_project,
            "load_and_project",
            [(w_qkv.shape, BF16), ((3, length, width), F32)] + decays,
            [starts, doc_lengths, forget, tokens, beside, w_qkv],
            ["s", "s", "v", "v", "v", "a"],
            flops=2 * step_flops,
            scratch=[pltpu.SemaphoreType.DMA((tps,))],
        )
        across, acc = lax.optimization_barrier((across, acc))
        across_beside = lax.ppermute(across, "tp", core)
        (acc,) = call(
            project_more, "project_more", [(acc.shape, F32)], [starts, across, w_vm, acc],
            ["s", "v", "v", "v"], flops=step_flops, aliases={3: 0},
        )
        qkv, mine, message = call(
            project_last,
            "project_last",
            [qkv_shape, ((2, half, DH, DH), F32), ((heads * DH + own_through.shape[0], DH), BF16)],
            [starts, across_beside, w_vm, acc, out_grad, cols_h, own_through],
            ["s"] + ["v"] * 6,
            flops=step_flops,
        )
        inside = call(
            intra,
            "intra",
            [sum_shape] * 4,
            [qkv, out_grad, cols_h, rows_h],
            flops=16 * length * length * width,
        )
        kept, passed, inside = states_direct(starts, own_through, mine, message, inside)
    else:
        gathered = lax.all_gather(tokens, "tp", axis=1, tiled=True)
        qkv = jnp.einsum("td,mdc->mtc", gathered, w_qkv, preferred_element_type=F32).astype(BF16)
        cols_h, rows_h, own_through = call(
            prepare, "prepare", decays, [starts, doc_lengths, forget], ["s", "s", "v"]
        )
        through = jnp.sum(own_through.astype(F32).reshape(2, heads, DH), axis=0)[:, 0]
        (own,) = call(own_states, "own_states", [((2, heads, DH, DH), F32)], [qkv, out_grad, cols_h])
        both = states_gathered(own, through)
        inside = call(
            intra,
            "intra",
            [sum_shape] * 4,
            [qkv, out_grad, cols_h, rows_h],
            flops=16 * length * length * width,
        )

    if by_hand:
        attn, gstack, chunk = call(
            back_first,
            "back_first",
            [sum_shape, qkv_shape, ((length, part), BF16)],
            [starts, qkv, out_grad, cols_h] + list(inside) + [kept, passed, w_vm],
            ["s"] + ["v"] * 10,
            flops=step_flops,
        )
        beside = lax.ppermute(chunk, "tp", core)
        (chunk,) = call(
            back_second, "back_second", [((length, part), F32)], [starts, gstack, w_vm], ["s", "v", "v"], flops=step_flops
        )
        chunk = (chunk + beside.astype(F32)).astype(BF16)
        chunk, gstack = lax.optimization_barrier((chunk, gstack))
        across = lax.ppermute(chunk, "tp", chip)
        chunk_other, chunk_own = call(
            back_rest,
            "back_rest",
            [((length, part), BF16), ((length, part), F32)],
            [starts, gstack, w_vm],
            ["s", "v", "v"],
            flops=2 * step_flops,
        )
        beside = [lax.ppermute(c, "tp", core) for c in jnp.split(chunk_other, 2)]
        input_grad = chunk_own + jnp.concatenate(beside).astype(F32) + across.astype(F32)
    else:
        attn, gstack = call(
            finish_whole, "finish", [sum_shape, qkv_shape], [qkv, out_grad, cols_h] + list(inside) + [both]
        )
        grad_terms = jnp.einsum("mtc,mdc->td", gstack, w_qkv, preferred_element_type=F32)
        input_grad = lax.psum_scatter(grad_terms, "tp", scatter_dimension=1, tiled=True)
    return (attn, input_grad)


def solution(mesh):
    placed = (P("seq", "tp"), P(None, None, "tp"), P("seq", "tp"), P("seq", "tp"), P())
    return jax.shard_map(
        local,
        mesh=mesh,
        in_specs=placed,
        out_specs=(P("seq", "tp"), P("seq", "tp")),
        check_vma=False,
    )
```

```python
import jax
import jax.numpy as jnp
from jax import lax
from jax.experimental import pallas as pl
from jax.experimental.pallas import tpu as pltpu
from jax.sharding import PartitionSpec as P

DH = 128
F32 = jnp.float32
BF16 = jnp.bfloat16
MIB = 1 << 20


def dot(a, b, ca, cb):
    return lax.dot_general(a, b, (((ca,), (cb,)), ((), ())), preferred_element_type=F32)


def split(a):
    high = a.astype(BF16)
    return high, (a - high.astype(F32)).astype(BF16)


def dot_split(a, b, ca, cb):
    high, low = split(a)
    return dot(high, b, ca, cb) + dot(low, b, ca, cb)


def call(kernel, name, outs, args, spaces=None, flops=0, limit=4, aliases=None, scratch=()):
    spaces = spaces or ["v"] * len(args)
    kinds = {"v": pltpu.VMEM, "s": pltpu.SMEM, "h": pltpu.HBM}
    placed = [
        a if s == "s" else pltpu.with_memory_space_constraint(a, kinds[s])
        for a, s in zip(args, spaces)
    ]
    return pl.pallas_call(
        kernel,
        name=name,
        out_shape=[pltpu.VMEM(shape, dtype) for shape, dtype in outs],
        in_specs=[pl.BlockSpec(memory_space=kinds[s]) for s in spaces],
        out_specs=[pl.BlockSpec(memory_space=pltpu.VMEM)] * len(outs),
        input_output_aliases=aliases or {},
        scratch_shapes=scratch,
        compiler_params=pltpu.CompilerParams(vmem_limit_bytes=limit * MIB),
        cost_estimate=pl.CostEstimate(flops=flops, bytes_accessed=0, transcendentals=0),
    )(*placed)


def tiles(width):
    tile = 256 if width % 256 == 0 else 128
    return [slice(i, i + tile) for i in range(0, width, tile)]


def rows_of(starts, which, part):
    return pl.ds(pl.multiple_of(starts[which] * part, part), part)


def prepare(starts, forget, cols_h, rows_h, through):
    heads, count = forget.shape
    offset = starts[6]
    t = lax.broadcasted_iota(jnp.int32, (count, count), 0)
    s = lax.broadcasted_iota(jnp.int32, (count, count), 1)
    lower = jnp.where(s <= t, 1.0, 0.0).astype(BF16)
    high, rest = split(forget[...])
    rest = forget[...] - high.astype(F32)
    middle, low = split(rest)

    def weights(axis):
        if axis:
            total = dot(high, lower, 1, 1) + (dot(middle, lower, 1, 1) + dot(low, lower, 1, 1))
        else:
            total = dot(lower, high, 1, 1) + (dot(lower, middle, 1, 1) + dot(lower, low, 1, 1))
        shape = (1, count) if axis else (count, 1)
        position = offset + lax.broadcasted_iota(jnp.int32, shape, axis)
        first, end = jnp.zeros(shape, jnp.int32), jnp.int32(0)
        for j in range(7, starts.shape[0]):
            end = end + starts[j]
            first = jnp.where(position >= end, end, first)
        first = first - offset
        last = lax.slice_in_dim(first, count - 1, count, axis=axis)
        final = lax.slice_in_dim(total, count - 1, count, axis=axis)
        lead = jnp.where(first < 0, jnp.exp(total), 0.0)
        tail = jnp.where(first == last, jnp.exp(jnp.where(first == last, final - total, 0.0)), 0.0)
        return total, lead, tail, first

    total, lead, tail, first = weights(0)
    cols_h[:, :heads] = total
    cols_h[:, heads : 2 * heads] = lead
    cols_h[:, 2 * heads : 3 * heads] = tail
    cols_h[:, 3 * heads : 3 * heads + 1] = first.astype(F32)
    total, lead, tail, first = weights(1)
    rows_h[:heads, :] = total
    rows_h[heads : 2 * heads, :] = lead
    rows_h[2 * heads :, :] = tail
    factor = jnp.broadcast_to(lead[:, count - 1 :], (heads, DH))
    through[...] = jnp.concatenate(split(factor), axis=0)


def load_and_project(starts, forget, tokens, other, w, own, w_vm, acc, cols_h, rows_h, through, sems):
    part = tokens.shape[1]
    own_copy = pltpu.make_async_copy(tokens, own, sems.at[w.shape[1] // part])
    own_copy.start()
    copies = []
    for j in range(w.shape[1] // part):
        rows = rows_of(starts, j, part)
        copies.append(pltpu.make_async_copy(w.at[:, rows, :], w_vm.at[:, rows, :], sems.at[j]))
        copies[-1].start()
    prepare(starts, forget, cols_h, rows_h, through)
    own_copy.wait()
    for j, x in enumerate((own, other)):
        copies[j].wait()
        for m in range(3):
            for cols in tiles(w.shape[2]):
                term = dot(x[...], w_vm[m, rows_of(starts, j, part), cols], 1, 0)
                acc[m, :, cols] = acc[m, :, cols] + term if j else term
    for copy in copies[2:]:
        copy.wait()


def project_more(starts, x, w, acc_in, acc):
    part = x.shape[1]
    for m in range(3):
        for cols in tiles(w.shape[2]):
            acc[m, :, cols] = acc_in[m, :, cols] + dot(x[...], w[m, rows_of(starts, 2, part), cols], 1, 0)


def project_last(starts, x, w, acc_in, grads, rows_h, own_through, qkv, mine, message):
    part = x.shape[1]
    for m in range(3):
        for cols in tiles(w.shape[2]):
            term = dot(x[...], w[m, rows_of(starts, 3, part), cols], 1, 0)
            qkv[m, :, cols] = (acc_in[m, :, cols] + term).astype(BF16)
    half = mine.shape[1]
    upper = starts[4]
    for h in range(2 * half):
        state = own_state(qkv, grads, rows_h, h)
        kept = (h >= half) == (upper == 1)

        @pl.when(kept)
        def _():
            mine[0, h % half], mine[1, h % half] = state

        @pl.when(jnp.logical_not(kept))
        def _():
            for i in range(2):
                message[(i * half + h % half) * DH : (i * half + h % half + 1) * DH, :] = state[i].astype(BF16)

    message[2 * half * DH :, :] = own_through[...]


def columns(cols_h, h):
    heads = cols_h.shape[1] // 3
    return [cols_h[:, i * heads + h : i * heads + h + 1] for i in range(3)]


def own_state(qkv, grads, rows_h, h):
    cols = slice(h * DH, (h + 1) * DH)
    heads = rows_h.shape[0] // 3
    lead, tail = rows_h[heads + h : heads + h + 1, :], rows_h[2 * heads + h : 2 * heads + h + 1, :]
    state = dot_split(qkv[1, :, cols].T.astype(F32) * tail, qkv[2, :, cols], 1, 0)
    grad = dot_split(qkv[0, :, cols].T.astype(F32) * (lead * (1.0 / DH)), grads[:, cols], 1, 0)
    return state, grad


def own_states(qkv, grads, rows_h, states):
    for h in range(states.shape[1]):
        states[0, h], states[1, h] = own_state(qkv, grads, rows_h, h)


def intra(qkv, grads, cols_h, rows_h, out, gq, gk, gv):
    length, heads = qkv.shape[1], rows_h.shape[0] // 3
    t = lax.broadcasted_iota(jnp.int32, (length, length), 0)
    s = lax.broadcasted_iota(jnp.int32, (length, length), 1)
    mask = (s <= t) & (s.astype(F32) >= cols_h[:, 3 * heads : 3 * heads + 1])
    for h in range(heads):
        cols = slice(h * DH, (h + 1) * DH)
        gap = jnp.where(mask, columns(cols_h, h)[0] - rows_h[h : h + 1, :], 0.0)
        weight = jnp.where(mask, jnp.exp(gap), 0.0)
        q, k, v, g = qkv[0, :, cols], qkv[1, :, cols], qkv[2, :, cols], grads[:, cols]
        scores = split(dot(q, k, 1, 1) * weight)
        dots = split(dot(g, v, 1, 1) * weight)
        out[:, cols] = dot(scores[0], v, 1, 0) + dot(scores[1], v, 1, 0)
        gq[:, cols] = dot(dots[0], k, 1, 0) + dot(dots[1], k, 1, 0)
        gk[:, cols] = dot(dots[0], q, 0, 0) + dot(dots[1], q, 0, 0)
        gv[:, cols] = dot(scores[0], g, 0, 0) + dot(scores[1], g, 0, 0)


def finish_grads(qkv, grads, cols_h, gq, gk, gv, state_of, gstack):
    for h in range(qkv.shape[2] // DH):
        cols = slice(h * DH, (h + 1) * DH)
        lead, tail = columns(cols_h, h)[1:]
        state, end = state_of(0, h), state_of(1, h)
        gstack[0, :, cols] = ((gq[:, cols] + dot(grads[:, cols], state, 1, 1) * lead) * (1.0 / DH)).astype(BF16)
        gstack[1, :, cols] = (gk[:, cols] * (1.0 / DH) + dot(qkv[2, :, cols], end, 1, 1) * tail).astype(BF16)
        gstack[2, :, cols] = (gv[:, cols] * (1.0 / DH) + dot(qkv[1, :, cols], end, 1, 0) * tail).astype(BF16)


def finish_out(qkv, cols_h, out, state_of, attn):
    for h in range(qkv.shape[2] // DH):
        cols = slice(h * DH, (h + 1) * DH)
        lead = columns(cols_h, h)[1]
        attn[:, cols] = (out[:, cols] + dot(qkv[0, :, cols], state_of(0, h), 1, 0) * lead) * (1.0 / DH)


def finish_whole(qkv, grads, cols_h, out, gq, gk, gv, both, attn, gstack):
    finish_grads(qkv, grads, cols_h, gq, gk, gv, lambda i, h: both[i, h], gstack)
    finish_out(qkv, cols_h, out, lambda i, h: both[i, h], attn)


def states_of(starts, kept, passed):
    half = kept.shape[1]
    upper = starts[4] == 1
    return lambda i, h: jnp.where((h >= half) == upper, kept[i, h % half], passed[i, h % half])


def back(starts, which, gstack, w, out, offset=0):
    part = w.shape[1] // 4
    for cols in tiles(out.shape[1]):
        size = cols.stop - cols.start
        rows = pl.ds(pl.multiple_of(starts[which] * part + offset + cols.start, size), size)
        total = dot(gstack[0], w[0, rows, :], 1, 1)
        total += dot(gstack[1], w[1, rows, :], 1, 1)
        total += dot(gstack[2], w[2, rows, :], 1, 1)
        out[:, cols] = total.astype(out.dtype)


def back_first(starts, qkv, grads, cols_h, gq, gk, gv, kept, passed, w, gstack, chunk_a, chunk_b):
    finish_grads(qkv, grads, cols_h, gq, gk, gv, states_of(starts, kept, passed), gstack)
    back(starts, 3, gstack, w, chunk_a)
    back(starts, 3, gstack, w, chunk_b, chunk_a.shape[1])


def back_second_a(starts, gstack, w, chunk):
    back(starts, 2, gstack, w, chunk)


def back_second_b(starts, gstack, w, chunk):
    back(starts, 2, gstack, w, chunk, w.shape[1] // 4 - chunk.shape[1])


def hand_on(a, b, a_out, b_out):
    pass


def back_rest(starts, gstack, w, qkv, cols_h, out, kept, passed, attn, chunk_other, chunk_own):
    back(starts, 1, gstack, w, chunk_other)
    back(starts, 0, gstack, w, chunk_own)
    finish_out(qkv, cols_h, out, states_of(starts, kept, passed), attn)


def per_head(scale, matrix):
    return scale[..., None, None] * matrix


def head_factors(rows):
    half = rows.shape[0] // 2
    return rows[:half].astype(F32) + rows[half:].astype(F32)


def pair_kernel(starts, own_through, mine, got, to_near, to_middle, to_far, mate_through):
    half = mine.shape[1]
    upper, z = starts[4] == 1, starts[5]
    own, mate = head_factors(own_through[...]), head_factors(got[2 * half * DH :, :])
    mate_through[...] = mate
    low, high = jnp.where(upper, mate, own), jnp.where(upper, own, mate)
    first = jnp.where(upper, half, 0)
    joint = split(own * mate)
    ends = jnp.concatenate(joint, axis=0)
    for to in (to_near, to_middle, to_far):
        to[half * DH :, :] = ends
    for j in range(half):
        rows = slice(j * DH, (j + 1) * DH)
        got_state = got[j * DH : (j + 1) * DH, :].astype(F32)
        got_grad = got[(half + j) * DH : (half + j + 1) * DH, :].astype(F32)
        low_j = jnp.where(upper, low[half + j : half + j + 1], low[j : j + 1])
        high_j = jnp.where(upper, high[half + j : half + j + 1], high[j : j + 1])
        state = jnp.where(upper, mine[0, j] + high_j * got_state, got_state + high_j * mine[0, j]).astype(BF16)
        grad = jnp.where(upper, got_grad + low_j * mine[1, j], mine[1, j] + low_j * got_grad).astype(BF16)
        to_near[rows, :] = jnp.where(z % 2 == 0, state, grad)
        to_middle[rows, :] = jnp.where(z == 1, state, grad)
        to_far[rows, :] = jnp.where(z < 2, state, grad)


def spread_kernel(starts, own_through, mate_through, mine, got, far, middle, near, kept, passed):
    half = mine.shape[1]
    upper, z = starts[4] == 1, starts[5]
    own, mate = head_factors(own_through[...]), mate_through[...]
    low, high = jnp.where(upper, mate, own), jnp.where(upper, own, mate)
    inner = (z == 1) | (z == 2)
    step = head_factors(jnp.where(inner, middle[half * DH :, :], near[half * DH :, :]))
    for j in range(half):
        rows = slice(j * DH, (j + 1) * DH)

        def factor(a):
            return jnp.where(upper, a[half + j : half + j + 1], a[j : j + 1])

        close = near[rows, :].astype(F32)
        beyond = jnp.where(inner, middle[rows, :], near[rows, :]).astype(F32) + factor(step) * far[rows, :].astype(F32)
        state = jnp.where(z == 0, 0.0, jnp.where(z == 1, close, beyond))
        grad = jnp.where(z == 3, 0.0, jnp.where(z == 2, close, beyond))
        got_state = got[j * DH : (j + 1) * DH, :].astype(F32)
        got_grad = got[(half + j) * DH : (half + j + 1) * DH, :].astype(F32)
        low_state, high_grad = jnp.where(upper, got_state, mine[0, j]), jnp.where(upper, mine[1, j], got_grad)
        high_in = (low_state + factor(low) * state).astype(BF16)
        low_in = (high_grad + factor(high) * grad).astype(BF16)
        state, grad = state.astype(BF16), grad.astype(BF16)
        kept[0, j], passed[0, j] = jnp.where(upper, high_in, state), jnp.where(upper, state, high_in)
        kept[1, j], passed[1, j] = jnp.where(upper, grad, low_in), jnp.where(upper, low_in, grad)


def states_direct(starts, own_through, mine, message, inside):
    half = mine.shape[1]
    mate = [(i, i ^ 1) for i in range(8)]
    near = [(i, i ^ 2) for i in range(8)]
    middle = [(2, 4), (4, 2), (3, 5), (5, 3)]
    far = [(i, i ^ 4) for i in range(8)]
    got = lax.ppermute(message, "seq", mate)
    to = ((half * DH + own_through.shape[0], DH), BF16)
    to_near, to_middle, to_far, mate_through = call(
        pair_kernel,
        "pair",
        [to, to, to, ((2 * half, DH), F32)],
        [starts, own_through, mine, got],
        ["s", "v", "v", "v"],
    )
    from_far = lax.ppermute(to_far, "seq", far)
    from_middle = lax.ppermute(to_middle, "seq", middle)
    from_near = lax.ppermute(to_near, "seq", near)
    inside, mine = lax.optimization_barrier((inside, mine))
    kept, passed = call(
        spread_kernel,
        "spread",
        [(mine.shape, BF16), (mine.shape, BF16)],
        [starts, own_through, mate_through, mine, got, from_far, from_middle, from_near],
        ["s"] + ["v"] * 7,
    )
    return kept, lax.ppermute(passed, "seq", mate), inside


def states_gathered(own, through):
    count = lax.axis_size("seq")
    place = lax.axis_index("seq")
    all_own = lax.all_gather(own, "seq")
    all_through = lax.all_gather(through, "seq")

    def pick(a, i):
        return lax.dynamic_index_in_dim(a, i, 0, False)

    def ahead(step, state):
        return per_head(pick(all_through, step), state) + pick(all_own, step)[0]

    def behind(step, state):
        source = count - 1 - step
        return per_head(pick(all_through, source), state) + pick(all_own, source)[1]

    zero = jnp.zeros_like(own[0])
    state = lax.fori_loop(0, place, ahead, zero)
    grad = lax.fori_loop(0, count - 1 - place, behind, zero)
    return jnp.stack([state, grad]).astype(BF16)


def local(tokens, w_qkv, forget, out_grad, doc_lengths):
    length, part = tokens.shape
    width = w_qkv.shape[2]
    heads = width // DH
    tps = lax.axis_size("tp")
    tp = lax.axis_index("tp")
    seqs = lax.axis_size("seq")
    place = lax.axis_index("seq")
    starts = jnp.stack([tp, tp ^ 1, tp ^ 2, tp ^ 3, place % 2, place // 2, place * length]).astype(jnp.int32)
    starts = jnp.concatenate([starts, doc_lengths])
    decays = [((length, 3 * heads + 1), F32), ((3 * heads, length), F32), ((2 * heads, DH), BF16)]
    qkv_shape = ((3, length, width), BF16)
    sum_shape = ((length, width), F32)
    by_hand = tps == 4 and seqs == 8 and heads % 8 == 0
    if by_hand:
        half = heads // 2
        core = [(i, i ^ 1) for i in range(4)]
        chip = [(i, i ^ 2) for i in range(4)]
        step_flops = 2 * 3 * length * part * width
        across = lax.ppermute(tokens, "tp", chip)
        beside = lax.ppermute(tokens, "tp", core)
        _, w_vm, acc, cols_h, rows_h, own_through = call(
            load_and_project,
            "load_and_project",
            [(tokens.shape, BF16), (w_qkv.shape, BF16), ((3, length, width), F32)] + decays,
            [starts, forget.T, tokens, beside, w_qkv],
            ["s", "v", "h", "v", "h"],
            flops=2 * step_flops,
            scratch=[pltpu.SemaphoreType.DMA((tps + 1,))],
        )
        across, acc = lax.optimization_barrier((across, acc))
        across_beside = lax.ppermute(across, "tp", core)
        (acc,) = call(
            project_more, "project_more", [(acc.shape, F32)], [starts, across, w_vm, acc],
            ["s", "v", "v", "v"], flops=step_flops, aliases={3: 0},
        )
        qkv, mine, message = call(
            project_last,
            "project_last",
            [qkv_shape, ((2, half, DH, DH), F32), ((heads * DH + own_through.shape[0], DH), BF16)],
            [starts, across_beside, w_vm, acc, out_grad, rows_h, own_through],
            ["s"] + ["v"] * 6,
            flops=step_flops,
        )
        inside = call(
            intra,
            "intra",
            [sum_shape] * 4,
            [qkv, out_grad, cols_h, rows_h],
            flops=16 * length * length * width,
        )
        kept, passed, inside = states_direct(starts, own_through, mine, message, inside)
    else:
        gathered = lax.all_gather(tokens, "tp", axis=1, tiled=True)
        qkv = jnp.einsum("td,mdc->mtc", gathered, w_qkv, preferred_element_type=F32).astype(BF16)
        cols_h, rows_h, own_through = call(
            prepare, "prepare", decays, [starts, forget.T], ["s", "v"]
        )
        through = jnp.sum(own_through.astype(F32).reshape(2, heads, DH), axis=0)[:, 0]
        (own,) = call(own_states, "own_states", [((2, heads, DH, DH), F32)], [qkv, out_grad, rows_h])
        both = states_gathered(own, through)
        inside = call(
            intra,
            "intra",
            [sum_shape] * 4,
            [qkv, out_grad, cols_h, rows_h],
            flops=16 * length * length * width,
        )

    if by_hand:
        part_a = part // 2
        part_b = part - part_a
        gstack, chunk_a, chunk_b = call(
            back_first,
            "back_first",
            [qkv_shape, ((length, part_a), BF16), ((length, part_b), BF16)],
            [starts, qkv, out_grad, cols_h] + list(inside[1:]) + [kept, passed, w_vm],
            ["s"] + ["v"] * 9,
        )
        beside_a = lax.ppermute(chunk_a, "tp", core)
        beside_b = lax.ppermute(chunk_b, "tp", core)
        (chunk_a,) = call(
            back_second_a, "back_second_a", [((length, part_a), F32)], [starts, gstack, w_vm], ["s", "v", "v"]
        )
        chunk_a = (chunk_a + beside_a.astype(F32)).astype(BF16)
        chunk_a, gstack = lax.optimization_barrier((chunk_a, gstack))
        across_a = lax.ppermute(chunk_a, "tp", chip)
        (chunk_b,) = call(
            back_second_b, "back_second_b", [((length, part_b), F32)], [starts, gstack, w_vm], ["s", "v", "v"]
        )
        chunk_b = (chunk_b + beside_b.astype(F32)).astype(BF16)
        chunk_b, gstack = lax.optimization_barrier((chunk_b, gstack))
        across_b = lax.ppermute(chunk_b, "tp", chip)
        attn, chunk_other, chunk_own = call(
            back_rest,
            "back_rest",
            [sum_shape, ((length, part), BF16), ((length, part), F32)],
            [starts, gstack, w_vm, qkv, cols_h, inside[0], kept, passed],
            ["s"] + ["v"] * 7,
        )
        beside = [lax.ppermute(c, "tp", core) for c in jnp.split(chunk_other, 4)]
        across = call(
            hand_on,
            "hand_on",
            [(across_a.shape, BF16), (across_b.shape, BF16)],
            [across_a, across_b],
            flops=8 * step_flops,
            aliases={0: 0, 1: 1},
        )
        across = jnp.concatenate(across, axis=1)
        input_grad = (across.astype(F32) + chunk_own) + jnp.concatenate(beside).astype(F32)
    else:
        attn, gstack = call(
            finish_whole, "finish", [sum_shape, qkv_shape], [qkv, out_grad, cols_h] + list(inside) + [both]
        )
        grad_terms = jnp.einsum("mtc,mdc->td", gstack, w_qkv, preferred_element_type=F32)
        input_grad = lax.psum_scatter(grad_terms, "tp", scatter_dimension=1, tiled=True)
    return (attn, input_grad)


def solution(mesh):
    placed = (P("seq", "tp"), P(None, None, "tp"), P("seq", "tp"), P("seq", "tp"), P())
    return jax.shard_map(
        local,
        mesh=mesh,
        in_specs=placed,
        out_specs=(P("seq", "tp"), P("seq", "tp")),
        check_vma=False,
    )
```

```python
import functools

import jax
import jax.numpy as jnp
from jax import lax
from jax.experimental import pallas as pl
from jax.experimental.pallas import tpu as pltpu
from jax.sharding import PartitionSpec as P

DH = 128
F32 = jnp.float32
BF16 = jnp.bfloat16
MIB = 1 << 20


def dot(a, b, ca, cb):
    return lax.dot_general(a, b, (((ca,), (cb,)), ((), ())), preferred_element_type=F32)


def split(a):
    high = a.astype(BF16)
    return high, (a - high.astype(F32)).astype(BF16)


def dot_split(a, b, ca, cb):
    high, low = split(a)
    return dot(high, b, ca, cb) + dot(low, b, ca, cb)


def call(kernel, name, outs, args, spaces=None, flops=0, limit=4, aliases=None, scratch=()):
    spaces = spaces or "v" * len(args)
    kinds = {"v": pltpu.VMEM, "s": pltpu.SMEM, "h": pltpu.HBM}
    placed = [
        a if s == "s" else pltpu.with_memory_space_constraint(a, kinds[s])
        for a, s in zip(args, spaces)
    ]
    return pl.pallas_call(
        kernel,
        name=name,
        out_shape=[pltpu.VMEM(shape, dtype) for shape, dtype in outs],
        in_specs=[pl.BlockSpec(memory_space=kinds[s]) for s in spaces],
        out_specs=[pl.BlockSpec(memory_space=pltpu.VMEM)] * len(outs),
        input_output_aliases=aliases or {},
        scratch_shapes=scratch,
        compiler_params=pltpu.CompilerParams(vmem_limit_bytes=limit * MIB),
        cost_estimate=pl.CostEstimate(flops=flops, bytes_accessed=0, transcendentals=0),
    )(*placed)


def tiles(width):
    tile = 256 if width % 256 == 0 else 128
    return [slice(i, i + tile) for i in range(0, width, tile)]


def rows_of(which, part, offset=0, size=None):
    size = size or part
    return pl.ds(pl.multiple_of((lax.axis_index("tp") ^ which) * part + offset, size), size)


def pair_place():
    place = lax.axis_index("seq")
    return place % 2 == 1, place // 2


def prepare(lengths, forget, cols_h, rows_h, through):
    heads, count = forget.shape
    offset = lax.axis_index("seq") * count
    t = lax.broadcasted_iota(jnp.int32, (count, count), 0)
    s = lax.broadcasted_iota(jnp.int32, (count, count), 1)
    lower = jnp.where(s <= t, 1.0, 0.0).astype(BF16)
    high, rest = split(forget[...])
    rest = forget[...] - high.astype(F32)
    middle, low = split(rest)

    def weights(axis):
        if axis:
            total = dot(high, lower, 1, 1) + (dot(middle, lower, 1, 1) + dot(low, lower, 1, 1))
        else:
            total = dot(lower, high, 1, 1) + (dot(lower, middle, 1, 1) + dot(lower, low, 1, 1))
        shape = (1, count) if axis else (count, 1)
        position = offset + lax.broadcasted_iota(jnp.int32, shape, axis)
        first, end = jnp.zeros(shape, jnp.int32), jnp.int32(0)
        for j in range(lengths.shape[0]):
            end = end + lengths[j]
            first = jnp.where(position >= end, end, first)
        first = first - offset
        last = lax.slice_in_dim(first, count - 1, count, axis=axis)
        final = lax.slice_in_dim(total, count - 1, count, axis=axis)
        lead = jnp.where(first < 0, jnp.exp(total), 0.0)
        tail = jnp.where(first == last, jnp.exp(jnp.where(first == last, final - total, 0.0)), 0.0)
        return total, lead, tail, first

    total, lead, tail, first = weights(0)
    cols_h[:, :heads] = total
    cols_h[:, heads : 2 * heads] = lead
    cols_h[:, 2 * heads : 3 * heads] = tail
    cols_h[:, 3 * heads : 3 * heads + 1] = first.astype(F32)
    total, lead, tail, first = weights(1)
    rows_h[:heads, :] = total
    rows_h[heads : 2 * heads, :] = lead
    rows_h[2 * heads :, :] = tail
    factor = jnp.broadcast_to(lead[:, count - 1 :], (heads, DH))
    through[...] = jnp.concatenate(split(factor), axis=0)


def load_and_project(lengths, forget, tokens, w, w_vm, acc, cols_h, rows_h, through, lengths_sm, forget_vm, own, sems):
    part = tokens.shape[1]
    count = w.shape[1] // part
    small = [
        pltpu.make_async_copy(lengths, lengths_sm, sems.at[count]),
        pltpu.make_async_copy(forget, forget_vm, sems.at[count + 1]),
        pltpu.make_async_copy(tokens, own, sems.at[count + 2]),
    ]
    copies = []
    for j in range(count):
        rows = rows_of(j, part)
        copies.append(pltpu.make_async_copy(w.at[:, rows, :], w_vm.at[:, rows, :], sems.at[j]))
    for copy in small + copies:
        copy.start()
    for copy in small:
        copy.wait()
    prepare(lengths_sm, forget_vm, cols_h, rows_h, through)
    copies[0].wait()
    for m in range(3):
        for cols in tiles(w.shape[2]):
            acc[m, :, cols] = dot(own[...], w_vm[m, rows_of(0, part), cols], 1, 0)
    for copy in copies[1:]:
        copy.wait()


def project_more(which, x, w, acc_in, acc):
    part = x.shape[1]
    for m in range(3):
        for cols in tiles(w.shape[2]):
            acc[m, :, cols] = acc_in[m, :, cols] + dot(x[...], w[m, rows_of(which, part), cols], 1, 0)


def project_last(m, x, w, acc_in, out):
    part = x.shape[1]
    for cols in tiles(w.shape[2]):
        out[:, cols] = (acc_in[m, :, cols] + dot(x[...], w[m, rows_of(3, part), cols], 1, 0)).astype(BF16)


def project_key_value(x, w, acc_in, rows_h, through, key, value, mine, message, states):
    project_last(1, x, w, acc_in, key)
    project_last(2, x, w, acc_in, value)
    hand_out(lambda h: state_end(key, value, rows_h, h), states, mine, message)
    message[mine.shape[0] * DH :, :] = through[...]


def project_query(x, w, acc_in, rows_h, grads, query, mine, message, states):
    project_last(0, x, w, acc_in, query)
    hand_out(lambda h: grad_start(query, grads, rows_h, h), states, mine, message)


def hand_out(state_of, states, mine, message):
    half = mine.shape[0]
    for h in range(2 * half):
        states[h] = state_of(h)
    upper = jnp.where(pair_place()[0], half, 0)
    for j in range(half):
        mine[j] = states[upper + j]
        message[j * DH : (j + 1) * DH, :] = states[half - upper + j].astype(BF16)


def columns(cols_h, h):
    heads = cols_h.shape[1] // 3
    return [cols_h[:, i * heads + h : i * heads + h + 1] for i in range(3)]


def state_end(key, value, rows_h, h):
    cols = slice(h * DH, (h + 1) * DH)
    heads = rows_h.shape[0] // 3
    return dot_split(key[:, cols].T.astype(F32) * rows_h[2 * heads + h : 2 * heads + h + 1, :], value[:, cols], 1, 0)


def grad_start(query, grads, rows_h, h):
    cols = slice(h * DH, (h + 1) * DH)
    heads = rows_h.shape[0] // 3
    weight = rows_h[heads + h : heads + h + 1, :] * (1.0 / DH)
    return dot_split(query[:, cols].T.astype(F32) * weight, grads[:, cols], 1, 0)


def own_states(query, key, value, grads, rows_h, states):
    for h in range(states.shape[1]):
        states[0, h] = state_end(key, value, rows_h, h)
        states[1, h] = grad_start(query, grads, rows_h, h)


def intra(query, key, value, grads, cols_h, rows_h, out, gq, gk, gv):
    length, heads = query.shape[0], rows_h.shape[0] // 3
    t = lax.broadcasted_iota(jnp.int32, (length, length), 0)
    s = lax.broadcasted_iota(jnp.int32, (length, length), 1)
    mask = (s <= t) & (s.astype(F32) >= cols_h[:, 3 * heads : 3 * heads + 1])
    for h in range(heads):
        cols = slice(h * DH, (h + 1) * DH)
        gap = jnp.where(mask, columns(cols_h, h)[0] - rows_h[h : h + 1, :], 0.0)
        weight = jnp.where(mask, jnp.exp(gap), 0.0)
        q, k, v, g = query[:, cols], key[:, cols], value[:, cols], grads[:, cols]
        scores = split(dot(q, k, 1, 1) * weight)
        dots = split(dot(g, v, 1, 1) * weight)
        out[:, cols] = dot(scores[0], v, 1, 0) + dot(scores[1], v, 1, 0)
        gq[:, cols] = dot(dots[0], k, 1, 0) + dot(dots[1], k, 1, 0)
        gk[:, cols] = dot(dots[0], q, 0, 0) + dot(dots[1], q, 0, 0)
        gv[:, cols] = dot(scores[0], g, 0, 0) + dot(scores[1], g, 0, 0)


def finish_grads(key, value, grads, gq, gk, gv, cols, lead, tail, state, end, gstack, at):
    gstack[0, :, at] = ((gq[:, cols] + dot(grads[:, cols], state, 1, 1) * lead) * (1.0 / DH)).astype(BF16)
    gstack[1, :, at] = (gk[:, cols] * (1.0 / DH) + dot(value[:, cols], end, 1, 1) * tail).astype(BF16)
    gstack[2, :, at] = (gv[:, cols] * (1.0 / DH) + dot(key[:, cols], end, 1, 0) * tail).astype(BF16)


def finish_out(query, cols_h, out, state_of, attn):
    for h in range(query.shape[1] // DH):
        cols = slice(h * DH, (h + 1) * DH)
        lead = columns(cols_h, h)[1]
        attn[:, cols] = (out[:, cols] + dot(query[:, cols], state_of(h), 1, 0) * lead) * (1.0 / DH)


def finish_whole(query, key, value, grads, cols_h, out, gq, gk, gv, both, attn, gstack):
    for h in range(query.shape[1] // DH):
        cols = slice(h * DH, (h + 1) * DH)
        lead, tail = columns(cols_h, h)[1:]
        finish_grads(key, value, grads, gq, gk, gv, cols, lead, tail, both[0, h], both[1, h], gstack, cols)
    finish_out(query, cols_h, out, lambda h: both[0, h], attn)


def finish_half(kept, key, value, grads, cols_h, gq, gk, gv, states, gstack):
    half = states.shape[1]
    second = pair_place()[0] == kept
    base = jnp.where(second, half * DH, 0)
    for j in range(half):
        cols = pl.ds(pl.multiple_of(base + j * DH, DH), DH)
        lead, tail = [
            jnp.where(second, b, a) for a, b in zip(columns(cols_h, j)[1:], columns(cols_h, half + j)[1:])
        ]
        at = slice(j * DH, (j + 1) * DH)
        finish_grads(key, value, grads, gq, gk, gv, cols, lead, tail, states[0, j], states[1, j], gstack, at)
    return pl.ds(pl.multiple_of(base, half * DH), half * DH)


def back(which, stacks, w, out, offset=0, start=None):
    part = w.shape[1] // 4
    for cols in tiles(out.shape[1]):
        rows = rows_of(which, part, offset + cols.start, cols.stop - cols.start)
        total = None if start is None else start[:, slice(offset + cols.start, offset + cols.stop)]
        for gstack, heads in stacks:
            for m in range(3):
                term = dot(gstack[m], w[m, rows, heads], 1, 1)
                total = term if total is None else total + term
        out[:, cols] = total.astype(out.dtype)


def half_columns(kept, w):
    width = w.shape[2] // 2
    return pl.ds(pl.multiple_of(jnp.where(pair_place()[0] == kept, width, 0), width), width)


def back_kept(key, value, grads, cols_h, gq, gk, gv, kept, w, stack, start3, start2):
    heads = finish_half(True, key, value, grads, cols_h, gq, gk, gv, kept, stack)
    back(3, [(stack, heads)], w, start3)
    back(2, [(stack, heads)], w, start2)


def back_first(key, value, grads, cols_h, gq, gk, gv, passed, w, start3, stack, chunk_a, chunk_b):
    heads = finish_half(False, key, value, grads, cols_h, gq, gk, gv, passed, stack)
    back(3, [(stack, heads)], w, chunk_a, 0, start3)
    back(3, [(stack, heads)], w, chunk_b, chunk_a.shape[1], start3)


def back_second_a(stack, w, start2, chunk):
    back(2, [(stack, half_columns(False, w))], w, chunk, 0, start2)


def back_second_b(stack, w, start2, chunk):
    back(2, [(stack, half_columns(False, w))], w, chunk, w.shape[1] // 4 - chunk.shape[1], start2)


def hand_on(*refs):
    pass


def back_rest(kept_stack, stack, w, query, cols_h, out, kept, passed, attn, chunk_other, chunk_own):
    stacks = [(kept_stack, half_columns(True, w)), (stack, half_columns(False, w))]
    back(1, stacks, w, chunk_other)
    back(0, stacks, w, chunk_own)
    half = kept.shape[1]
    upper = pair_place()[0]

    def state_of(h):
        return jnp.where((h >= half) == upper, kept[0, h % half], passed[0, h % half])

    finish_out(query, cols_h, out, state_of, attn)


def per_head(scale, matrix):
    return scale[..., None, None] * matrix


def head_factors(rows):
    half = rows.shape[0] // 2
    return rows[:half].astype(F32) + rows[half:].astype(F32)


def pair_kernel(own_through, my_state, my_grad, got_state, got_grad, to_far, to_middle, to_near, mate_through):
    half = my_state.shape[0]
    upper, z = pair_place()
    own, mate = head_factors(own_through[...]), head_factors(got_state[half * DH :, :])
    mate_through[...] = mate
    low, high = jnp.where(upper, mate, own), jnp.where(upper, own, mate)
    ends = jnp.concatenate(split(own * mate), axis=0)
    for to in (to_near, to_middle, to_far):
        to[half * DH :, :] = ends
    for j in range(half):
        rows = slice(j * DH, (j + 1) * DH)
        theirs, theirs_grad = got_state[rows, :].astype(F32), got_grad[rows, :].astype(F32)
        low_j, high_j = half_factor(upper, low, j), half_factor(upper, high, j)
        mine, mine_grad = my_state[j], my_grad[j]
        state = jnp.where(upper, mine + high_j * theirs, theirs + high_j * mine).astype(BF16)
        grad = jnp.where(upper, theirs_grad + low_j * mine_grad, mine_grad + low_j * theirs_grad).astype(BF16)
        to_near[rows, :] = jnp.where(z % 2 == 0, state, grad)
        to_middle[rows, :] = jnp.where(z == 1, state, grad)
        to_far[rows, :] = jnp.where(z < 2, state, grad)


def half_factor(upper, factors, j):
    half = factors.shape[0] // 2
    return jnp.where(upper, factors[half + j : half + j + 1], factors[j : j + 1])


def spread_kernel(own_through, mate_through, my_state, my_grad, got_state, got_grad, far, middle, near, kept, passed):
    half = my_state.shape[0]
    upper, z = pair_place()
    own, mate = head_factors(own_through[...]), mate_through[...]
    low, high = jnp.where(upper, mate, own), jnp.where(upper, own, mate)
    inner = (z == 1) | (z == 2)
    step = head_factors(jnp.where(inner, middle[half * DH :, :], near[half * DH :, :]))
    for j in range(half):
        rows = slice(j * DH, (j + 1) * DH)
        close = near[rows, :].astype(F32)
        beyond = jnp.where(inner, middle[rows, :], near[rows, :]).astype(F32)
        beyond = beyond + half_factor(upper, step, j) * far[rows, :].astype(F32)
        state = jnp.where(z == 0, 0.0, jnp.where(z == 1, close, beyond))
        grad = jnp.where(z == 3, 0.0, jnp.where(z == 2, close, beyond))
        low_state = jnp.where(upper, got_state[rows, :].astype(F32), my_state[j])
        high_grad = jnp.where(upper, my_grad[j], got_grad[rows, :].astype(F32))
        high_in = (low_state + half_factor(upper, low, j) * state).astype(BF16)
        low_in = (high_grad + half_factor(upper, high, j) * grad).astype(BF16)
        state, grad = state.astype(BF16), grad.astype(BF16)
        kept[0, j], passed[0, j] = jnp.where(upper, high_in, state), jnp.where(upper, state, high_in)
        kept[1, j], passed[1, j] = jnp.where(upper, grad, low_in), jnp.where(upper, low_in, grad)


MATE = [(i, i ^ 1) for i in range(8)]
NEAR = [(i, i ^ 2) for i in range(8)]
MIDDLE = [(2, 4), (4, 2), (3, 5), (5, 3)]
FAR = [(i, i ^ 4) for i in range(8)]


def states_direct(own_through, my_state, my_grad, got_state, got_grad, inside):
    half = my_state.shape[0]
    to = ((half * DH + own_through.shape[0], DH), BF16)
    known = [my_state, my_grad, got_state, got_grad]
    to_far, to_middle, to_near, mate_through = call(
        pair_kernel, "pair", [to, to, to, ((2 * half, DH), F32)], [own_through] + known
    )
    from_far = lax.ppermute(to_far, "seq", FAR)
    from_middle = lax.ppermute(to_middle, "seq", MIDDLE)
    from_near = lax.ppermute(to_near, "seq", NEAR)
    inside, mate_through = lax.optimization_barrier((inside, mate_through))
    both = ((2, half, DH, DH), BF16)
    kept, passed = call(
        spread_kernel, "spread", [both, both], [own_through, mate_through] + known + [from_far, from_middle, from_near]
    )
    return kept, lax.ppermute(passed, "seq", MATE), inside


def states_gathered(own, through):
    count = lax.axis_size("seq")
    place = lax.axis_index("seq")
    all_own = lax.all_gather(own, "seq")
    all_through = lax.all_gather(through, "seq")

    def pick(a, i):
        return lax.dynamic_index_in_dim(a, i, 0, False)

    def ahead(step, state):
        return per_head(pick(all_through, step), state) + pick(all_own, step)[0]

    def behind(step, state):
        source = count - 1 - step
        return per_head(pick(all_through, source), state) + pick(all_own, source)[1]

    zero = jnp.zeros_like(own[0])
    state = lax.fori_loop(0, place, ahead, zero)
    grad = lax.fori_loop(0, count - 1 - place, behind, zero)
    return jnp.stack([state, grad]).astype(BF16)


def local(tokens, w_qkv, forget, out_grad, doc_lengths):
    length, part = tokens.shape
    width = w_qkv.shape[2]
    heads = width // DH
    tps = lax.axis_size("tp")
    seqs = lax.axis_size("seq")
    by_hand = tps == 4 and seqs == 8 and heads % 8 == 0
    decays = [((length, 3 * heads + 1), F32), ((3 * heads, length), F32), ((2 * heads, DH), BF16)]
    rows_shape = ((length, width), BF16)
    sum_shape = ((length, width), F32)
    intra_flops = 16 * length * length * width
    forget = forget.T
    if not by_hand:
        gathered = lax.all_gather(tokens, "tp", axis=1, tiled=True)
        projected = jnp.einsum("td,mdc->mtc", gathered, w_qkv, preferred_element_type=F32).astype(BF16)
        qkv = [projected[m] for m in range(3)]
        cols_h, rows_h, through = call(prepare, "prepare", decays, [doc_lengths, forget], "sv")
        through = jnp.sum(through.astype(F32).reshape(2, heads, DH), axis=0)[:, 0]
        (own,) = call(own_states, "own_states", [((2, heads, DH, DH), F32)], qkv + [out_grad, rows_h])
        both = states_gathered(own, through)
        inside = call(intra, "intra", [sum_shape] * 4, qkv + [out_grad, cols_h, rows_h], flops=intra_flops)
        attn, gstack = call(
            finish_whole,
            "finish",
            [sum_shape, ((3, length, width), BF16)],
            qkv + [out_grad, cols_h] + list(inside) + [both],
        )
        grad_terms = jnp.einsum("mtc,mdc->td", gstack, w_qkv, preferred_element_type=F32)
        return attn, lax.psum_scatter(grad_terms, "tp", scatter_dimension=1, tiled=True)

    half = heads // 2
    core = [(i, i ^ 1) for i in range(4)]
    chip = [(i, i ^ 2) for i in range(4)]
    step_flops = 2 * 3 * length * part * width
    across = lax.ppermute(tokens, "tp", chip)
    beside = lax.ppermute(tokens, "tp", core)
    w_vm, acc, cols_h, rows_h, through = call(
        load_and_project,
        "load_and_project",
        [(w_qkv.shape, BF16), ((3, length, width), F32)] + decays,
        [doc_lengths, forget, tokens, w_qkv],
        "hhhh",
        scratch=[
            pltpu.SMEM(doc_lengths.shape, jnp.int32),
            pltpu.VMEM(forget.shape, F32),
            pltpu.VMEM(tokens.shape, BF16),
            pltpu.SemaphoreType.DMA((tps + 3,)),
        ],
    )
    (acc,) = call(
        functools.partial(project_more, 1),
        "project_beside",
        [(acc.shape, F32)],
        [beside, w_vm, acc],
        aliases={2: 0},
    )
    across, acc = lax.optimization_barrier((across, acc))
    across_beside = lax.ppermute(across, "tp", core)
    (acc,) = call(
        functools.partial(project_more, 2),
        "project_across",
        [(acc.shape, F32)],
        [across, w_vm, acc],
        aliases={2: 0},
    )
    states_scratch = [pltpu.VMEM((heads, DH, DH), F32)]
    mine_shape = ((half, DH, DH), F32)
    key, value, my_state, message = call(
        project_key_value,
        "project_key_value",
        [rows_shape, rows_shape, mine_shape, ((half * DH + through.shape[0], DH), BF16)],
        [across_beside, w_vm, acc, rows_h, through],
        scratch=states_scratch,
    )
    got_state = lax.ppermute(message, "seq", MATE)
    acc, my_state = lax.optimization_barrier((acc, my_state))
    query, my_grad, message = call(
        project_query,
        "project_query",
        [rows_shape, mine_shape, ((half * DH, DH), BF16)],
        [across_beside, w_vm, acc, rows_h, out_grad],
        scratch=states_scratch,
    )
    got_grad = lax.ppermute(message, "seq", MATE)
    inside = call(
        intra, "intra", [sum_shape] * 4, [query, key, value, out_grad, cols_h, rows_h], flops=intra_flops
    )
    kept, passed, inside = states_direct(through, my_state, my_grad, got_state, got_grad, inside)

    part_a = part // 2
    part_b = part - part_a
    stack_shape = ((3, length, width // 2), BF16)
    chunk_shape = ((length, part), F32)
    common = [key, value, out_grad, cols_h] + list(inside[1:])
    kept_stack, start3, start2 = call(
        back_kept, "back_kept", [stack_shape, chunk_shape, chunk_shape], common + [kept, w_vm]
    )
    stack, chunk_a, chunk_b = call(
        back_first,
        "back_first",
        [stack_shape, ((length, part_a), BF16), ((length, part_b), BF16)],
        common + [passed, w_vm, start3],
    )
    beside_a = lax.ppermute(chunk_a, "tp", core)
    beside_b = lax.ppermute(chunk_b, "tp", core)
    (chunk_a,) = call(back_second_a, "back_second_a", [((length, part_a), F32)], [stack, w_vm, start2])
    chunk_a = (chunk_a + beside_a.astype(F32)).astype(BF16)
    chunk_a, stack = lax.optimization_barrier((chunk_a, stack))
    across_a = lax.ppermute(chunk_a, "tp", chip)
    (chunk_b,) = call(back_second_b, "back_second_b", [((length, part_b), F32)], [stack, w_vm, start2])
    chunk_b = (chunk_b + beside_b.astype(F32)).astype(BF16)
    chunk_b, stack = lax.optimization_barrier((chunk_b, stack))
    across_b = lax.ppermute(chunk_b, "tp", chip)
    attn, chunk_other, chunk_own = call(
        back_rest,
        "back_rest",
        [sum_shape, ((length, part), BF16), chunk_shape],
        [kept_stack, stack, w_vm, query, cols_h, inside[0], kept, passed],
    )
    beside = [lax.ppermute(c, "tp", core) for c in jnp.split(chunk_other, 4)]
    across = [across_a]
    for more in ([], [across_b]):
        across = list(across) + more
        across = call(
            hand_on,
            "hand_on",
            [(a.shape, BF16) for a in across],
            across,
            flops=8 * step_flops if more else 0,
            aliases={i: i for i in range(len(across))},
        )
    across = jnp.concatenate(across, axis=1)
    input_grad = (across.astype(F32) + chunk_own) + jnp.concatenate(beside).astype(F32)
    return attn, input_grad


def solution(mesh):
    placed = (P("seq", "tp"), P(None, None, "tp"), P("seq", "tp"), P("seq", "tp"), P())
    return jax.shard_map(
        local,
        mesh=mesh,
        in_specs=placed,
        out_specs=(P("seq", "tp"), P("seq", "tp")),
        check_vma=False,
    )
```

```python
import functools

import jax
import jax.numpy as jnp
from jax import lax
from jax.experimental import pallas as pl
from jax.experimental.pallas import tpu as pltpu
from jax.sharding import PartitionSpec as P

DH = 128
F32 = jnp.float32
BF16 = jnp.bfloat16
MIB = 1 << 20


def dot(a, b, ca, cb):
    return lax.dot_general(a, b, (((ca,), (cb,)), ((), ())), preferred_element_type=F32)


def split(a):
    high = a.astype(BF16)
    return high, (a - high.astype(F32)).astype(BF16)


def dot_split(a, b, ca, cb):
    high, low = split(a)
    return dot(high, b, ca, cb) + dot(low, b, ca, cb)


def call(kernel, name, outs, args, spaces=None, flops=0, limit=4, aliases=None, scratch=(), out_space=pltpu.VMEM):
    spaces = spaces or "v" * len(args)
    kinds = {"v": pltpu.VMEM, "s": pltpu.SMEM, "h": pltpu.HBM}
    placed = [
        a if s == "s" else pltpu.with_memory_space_constraint(a, kinds[s])
        for a, s in zip(args, spaces)
    ]
    return pl.pallas_call(
        kernel,
        name=name,
        out_shape=[out_space(shape, dtype) for shape, dtype in outs],
        in_specs=[pl.BlockSpec(memory_space=kinds[s]) for s in spaces],
        out_specs=[pl.BlockSpec(memory_space=out_space)] * len(outs),
        input_output_aliases=aliases or {},
        scratch_shapes=scratch,
        compiler_params=pltpu.CompilerParams(vmem_limit_bytes=limit * MIB),
        cost_estimate=pl.CostEstimate(flops=flops, bytes_accessed=0, transcendentals=0),
    )(*placed)


def tiles(width):
    tile = 256 if width % 256 == 0 else 128
    return [slice(i, i + tile) for i in range(0, width, tile)]


def rows_of(which, part, offset=0, size=None):
    size = size or part
    return pl.ds(pl.multiple_of((lax.axis_index("tp") ^ which) * part + offset, size), size)


def pair_place():
    place = lax.axis_index("seq")
    return place % 2 == 1, place // 2


def prepare(lengths, forget, cols_h, rows_h, through):
    heads, count = forget.shape
    offset = lax.axis_index("seq") * count
    t = lax.broadcasted_iota(jnp.int32, (count, count), 0)
    s = lax.broadcasted_iota(jnp.int32, (count, count), 1)
    lower = jnp.where(s <= t, 1.0, 0.0).astype(BF16)
    high, rest = split(forget[...])
    rest = forget[...] - high.astype(F32)
    middle, low = split(rest)

    def weights(axis):
        if axis:
            total = dot(high, lower, 1, 1) + (dot(middle, lower, 1, 1) + dot(low, lower, 1, 1))
        else:
            total = dot(lower, high, 1, 1) + (dot(lower, middle, 1, 1) + dot(lower, low, 1, 1))
        shape = (1, count) if axis else (count, 1)
        position = offset + lax.broadcasted_iota(jnp.int32, shape, axis)
        first, end = jnp.zeros(shape, jnp.int32), jnp.int32(0)
        for j in range(lengths.shape[0]):
            end = end + lengths[j]
            first = jnp.where(position >= end, end, first)
        first = first - offset
        last = lax.slice_in_dim(first, count - 1, count, axis=axis)
        final = lax.slice_in_dim(total, count - 1, count, axis=axis)
        lead = jnp.where(first < 0, jnp.exp(total), 0.0)
        tail = jnp.where(first == last, jnp.exp(jnp.where(first == last, final - total, 0.0)), 0.0)
        return total, lead, tail, first

    total, lead, tail, first = weights(0)
    cols_h[:, :heads] = total
    cols_h[:, heads : 2 * heads] = lead
    cols_h[:, 2 * heads : 3 * heads] = tail
    cols_h[:, 3 * heads : 3 * heads + 1] = first.astype(F32)
    total, lead, tail, first = weights(1)
    rows_h[:heads, :] = total
    rows_h[heads : 2 * heads, :] = lead
    rows_h[2 * heads :, :] = tail
    factor = jnp.broadcast_to(lead[:, count - 1 :], (heads, DH))
    through[...] = jnp.concatenate(split(factor), axis=0)


def load_and_project(lengths, forget, tokens, w, w_vm, acc, cols_h, rows_h, through, lengths_sm, forget_vm, own, sems):
    part = tokens.shape[1]
    count = w.shape[1] // part
    small = [
        pltpu.make_async_copy(lengths, lengths_sm, sems.at[count]),
        pltpu.make_async_copy(forget, forget_vm, sems.at[count + 1]),
        pltpu.make_async_copy(tokens, own, sems.at[count + 2]),
    ]
    copies = []
    for j in range(count):
        rows = rows_of(j, part)
        copies.append(pltpu.make_async_copy(w.at[:, rows, :], w_vm.at[:, rows, :], sems.at[j]))
    for copy in small + copies:
        copy.start()
    for copy in small:
        copy.wait()
    prepare(lengths_sm, forget_vm, cols_h, rows_h, through)
    copies[0].wait()
    for m in range(3):
        for cols in tiles(w.shape[2]):
            acc[m, :, cols] = dot(own[...], w_vm[m, rows_of(0, part), cols], 1, 0)
    for copy in copies[1:]:
        copy.wait()


def project_chunks(pieces, *refs):
    xs, (w, acc_in, acc) = refs[: len(pieces)], refs[len(pieces) :]
    for m in range(3):
        for cols in tiles(w.shape[2]):
            acc[m, :, cols] = acc_in[m, :, cols] + products(pieces, xs, w, m, cols)


def products(pieces, xs, w, m, cols):
    part = w.shape[1] // 4
    total = None
    for (which, offset), x in zip(pieces, xs):
        term = dot(x[...], w[m, rows_of(which, part, offset, x.shape[1]), cols], 1, 0)
        total = term if total is None else total + term
    return total


def project_last(piece, m, x, w, acc_in, out):
    for cols in tiles(w.shape[2]):
        out[:, cols] = (acc_in[m, :, cols] + products([piece], [x], w, m, cols)).astype(BF16)


def project_key_value(piece, x, w, acc_in, rows_h, through, key, value, mine, message, states):
    project_last(piece, 1, x, w, acc_in, key)
    project_last(piece, 2, x, w, acc_in, value)
    hand_out(lambda h: state_end(key, value, rows_h, h), states, mine, message)
    message[mine.shape[0] * DH :, :] = through[...]


def project_query(piece, x, w, acc_in, rows_h, grads, query, mine, message, states):
    project_last(piece, 0, x, w, acc_in, query)
    hand_out(lambda h: grad_start(query, grads, rows_h, h), states, mine, message)


def hand_out(state_of, states, mine, message):
    half = mine.shape[0]
    for h in range(2 * half):
        states[h] = state_of(h)
    upper = jnp.where(pair_place()[0], half, 0)
    for j in range(half):
        mine[j] = states[upper + j]
        message[j * DH : (j + 1) * DH, :] = states[half - upper + j].astype(BF16)


def columns(cols_h, h):
    heads = cols_h.shape[1] // 3
    return [cols_h[:, i * heads + h : i * heads + h + 1] for i in range(3)]


def state_end(key, value, rows_h, h):
    cols = slice(h * DH, (h + 1) * DH)
    heads = rows_h.shape[0] // 3
    return dot_split(key[:, cols].T.astype(F32) * rows_h[2 * heads + h : 2 * heads + h + 1, :], value[:, cols], 1, 0)


def grad_start(query, grads, rows_h, h):
    cols = slice(h * DH, (h + 1) * DH)
    heads = rows_h.shape[0] // 3
    weight = rows_h[heads + h : heads + h + 1, :] * (1.0 / DH)
    return dot_split(query[:, cols].T.astype(F32) * weight, grads[:, cols], 1, 0)


def own_states(query, key, value, grads, rows_h, states):
    for h in range(states.shape[1]):
        states[0, h] = state_end(key, value, rows_h, h)
        states[1, h] = grad_start(query, grads, rows_h, h)


def intra(query, key, value, grads, cols_h, rows_h, out, gq, gk, gv):
    length, heads = query.shape[0], rows_h.shape[0] // 3
    t = lax.broadcasted_iota(jnp.int32, (length, length), 0)
    s = lax.broadcasted_iota(jnp.int32, (length, length), 1)
    mask = (s <= t) & (s.astype(F32) >= cols_h[:, 3 * heads : 3 * heads + 1])
    for h in range(heads):
        cols = slice(h * DH, (h + 1) * DH)
        gap = jnp.where(mask, columns(cols_h, h)[0] - rows_h[h : h + 1, :], 0.0)
        weight = jnp.where(mask, jnp.exp(gap), 0.0)
        q, k, v, g = query[:, cols], key[:, cols], value[:, cols], grads[:, cols]
        scores = split(dot(q, k, 1, 1) * weight)
        dots = split(dot(g, v, 1, 1) * weight)
        out[:, cols] = dot(scores[0], v, 1, 0) + dot(scores[1], v, 1, 0)
        gq[:, cols] = dot(dots[0], k, 1, 0) + dot(dots[1], k, 1, 0)
        gk[:, cols] = dot(dots[0], q, 0, 0) + dot(dots[1], q, 0, 0)
        gv[:, cols] = dot(scores[0], g, 0, 0) + dot(scores[1], g, 0, 0)


def finish_grads(key, value, grads, gq, gk, gv, cols, lead, tail, state, end, gstack, at):
    gstack[0, :, at] = ((gq[:, cols] + dot(grads[:, cols], state, 1, 1) * lead) * (1.0 / DH)).astype(BF16)
    gstack[1, :, at] = (gk[:, cols] * (1.0 / DH) + dot(value[:, cols], end, 1, 1) * tail).astype(BF16)
    gstack[2, :, at] = (gv[:, cols] * (1.0 / DH) + dot(key[:, cols], end, 1, 0) * tail).astype(BF16)


def finish_out(query, cols_h, out, state_of, attn):
    for h in range(query.shape[1] // DH):
        cols = slice(h * DH, (h + 1) * DH)
        lead = columns(cols_h, h)[1]
        attn[:, cols] = (out[:, cols] + dot(query[:, cols], state_of(h), 1, 0) * lead) * (1.0 / DH)


def finish_whole(query, key, value, grads, cols_h, out, gq, gk, gv, both, attn, gstack):
    for h in range(query.shape[1] // DH):
        cols = slice(h * DH, (h + 1) * DH)
        lead, tail = columns(cols_h, h)[1:]
        finish_grads(key, value, grads, gq, gk, gv, cols, lead, tail, both[0, h], both[1, h], gstack, cols)
    finish_out(query, cols_h, out, lambda h: both[0, h], attn)


def finish_half(kept, key, value, grads, cols_h, gq, gk, gv, states, gstack):
    half = states.shape[1]
    second = pair_place()[0] == kept
    base = jnp.where(second, half * DH, 0)
    for j in range(half):
        cols = pl.ds(pl.multiple_of(base + j * DH, DH), DH)
        lead, tail = [
            jnp.where(second, b, a) for a, b in zip(columns(cols_h, j)[1:], columns(cols_h, half + j)[1:])
        ]
        at = slice(j * DH, (j + 1) * DH)
        finish_grads(key, value, grads, gq, gk, gv, cols, lead, tail, states[0, j], states[1, j], gstack, at)
    return pl.ds(pl.multiple_of(base, half * DH), half * DH)


def back(which, stacks, w, out, offset=0, start=None):
    part = w.shape[1] // 4
    for cols in tiles(out.shape[1]):
        rows = rows_of(which, part, offset + cols.start, cols.stop - cols.start)
        total = None if start is None else start[:, slice(offset + cols.start, offset + cols.stop)]
        for gstack, heads in stacks:
            for m in range(3):
                term = dot(gstack[m], w[m, rows, heads], 1, 1)
                total = term if total is None else total + term
        out[:, cols] = total.astype(out.dtype)


def half_columns(kept, w):
    width = w.shape[2] // 2
    return pl.ds(pl.multiple_of(jnp.where(pair_place()[0] == kept, width, 0), width), width)


def back_kept(key, value, grads, cols_h, gq, gk, gv, kept, w, stack, start3, start2):
    heads = finish_half(True, key, value, grads, cols_h, gq, gk, gv, kept, stack)
    back(3, [(stack, heads)], w, start3)
    back(2, [(stack, heads)], w, start2)


def back_first(key, value, grads, cols_h, gq, gk, gv, passed, w, start3, stack, chunk3_a):
    heads = finish_half(False, key, value, grads, cols_h, gq, gk, gv, passed, stack)
    back(3, [(stack, heads)], w, chunk3_a, 0, start3)


def back_second(stack, w, start3, start2, chunk3_b, chunk2_a, chunk2_b):
    stacks = [(stack, half_columns(False, w))]
    back(3, stacks, w, chunk3_b, start3.shape[1] - chunk3_b.shape[1], start3)
    back(2, stacks, w, chunk2_a, 0, start2)
    back(2, stacks, w, chunk2_b, chunk2_a.shape[1], start2)


def hand_on(*refs):
    pass


def last_sum(own, across_a, across_b, *refs):
    besides, (out, total, sems) = refs[:-3], refs[-3:]
    size, middle = besides[0].shape[0], across_a.shape[1]
    copies = []
    for i, beside in enumerate(besides):
        rows = slice(i * size, (i + 1) * size)
        for cols, across in ((slice(0, middle), across_a), (slice(middle, own.shape[1]), across_b)):
            total[rows, cols] = (own[rows, cols] + beside[:, cols].astype(F32)) + across[rows, :].astype(F32)
        copies.append(pltpu.make_async_copy(total.at[rows, :], out.at[rows, :], sems.at[i]))
        copies[-1].start()
    for copy in copies:
        copy.wait()


def back_rest(kept_stack, stack, w, query, cols_h, out, kept, passed, attn, chunk_other, chunk_own):
    stacks = [(kept_stack, half_columns(True, w)), (stack, half_columns(False, w))]
    back(1, stacks, w, chunk_other)
    back(0, stacks, w, chunk_own)
    half = kept.shape[1]
    upper = pair_place()[0]

    def state_of(h):
        return jnp.where((h >= half) == upper, kept[0, h % half], passed[0, h % half])

    finish_out(query, cols_h, out, state_of, attn)


def per_head(scale, matrix):
    return scale[..., None, None] * matrix


def head_factors(rows):
    half = rows.shape[0] // 2
    return rows[:half].astype(F32) + rows[half:].astype(F32)


def pair_kernel(own_through, my_state, my_grad, got_state, got_grad, to_far, to_middle, to_near, mate_through):
    half = my_state.shape[0]
    upper, z = pair_place()
    own, mate = head_factors(own_through[...]), head_factors(got_state[half * DH :, :])
    mate_through[...] = mate
    low, high = jnp.where(upper, mate, own), jnp.where(upper, own, mate)
    ends = jnp.concatenate(split(own * mate), axis=0)
    for to in (to_near, to_middle, to_far):
        to[half * DH :, :] = ends
    for j in range(half):
        rows = slice(j * DH, (j + 1) * DH)
        theirs, theirs_grad = got_state[rows, :].astype(F32), got_grad[rows, :].astype(F32)
        low_j, high_j = half_factor(upper, low, j), half_factor(upper, high, j)
        mine, mine_grad = my_state[j], my_grad[j]
        state = jnp.where(upper, mine + high_j * theirs, theirs + high_j * mine).astype(BF16)
        grad = jnp.where(upper, theirs_grad + low_j * mine_grad, mine_grad + low_j * theirs_grad).astype(BF16)
        to_near[rows, :] = jnp.where(z % 2 == 0, state, grad)
        to_middle[rows, :] = jnp.where(z == 1, state, grad)
        to_far[rows, :] = jnp.where(z < 2, state, grad)


def half_factor(upper, factors, j):
    half = factors.shape[0] // 2
    return jnp.where(upper, factors[half + j : half + j + 1], factors[j : j + 1])


def spread_kernel(own_through, mate_through, my_state, my_grad, got_state, got_grad, far, middle, near, kept, passed):
    half = my_state.shape[0]
    upper, z = pair_place()
    own, mate = head_factors(own_through[...]), mate_through[...]
    low, high = jnp.where(upper, mate, own), jnp.where(upper, own, mate)
    inner = (z == 1) | (z == 2)
    step = head_factors(jnp.where(inner, middle[half * DH :, :], near[half * DH :, :]))
    for j in range(half):
        rows = slice(j * DH, (j + 1) * DH)
        close = near[rows, :].astype(F32)
        beyond = jnp.where(inner, middle[rows, :], near[rows, :]).astype(F32)
        beyond = beyond + half_factor(upper, step, j) * far[rows, :].astype(F32)
        state = jnp.where(z == 0, 0.0, jnp.where(z == 1, close, beyond))
        grad = jnp.where(z == 3, 0.0, jnp.where(z == 2, close, beyond))
        low_state = jnp.where(upper, got_state[rows, :].astype(F32), my_state[j])
        high_grad = jnp.where(upper, my_grad[j], got_grad[rows, :].astype(F32))
        high_in = (low_state + half_factor(upper, low, j) * state).astype(BF16)
        low_in = (high_grad + half_factor(upper, high, j) * grad).astype(BF16)
        state, grad = state.astype(BF16), grad.astype(BF16)
        kept[0, j], passed[0, j] = jnp.where(upper, high_in, state), jnp.where(upper, state, high_in)
        kept[1, j], passed[1, j] = jnp.where(upper, grad, low_in), jnp.where(upper, low_in, grad)


MATE = [(i, i ^ 1) for i in range(8)]
NEAR = [(i, i ^ 2) for i in range(8)]
MIDDLE = [(2, 4), (4, 2), (3, 5), (5, 3)]
FAR = [(i, i ^ 4) for i in range(8)]


def states_direct(own_through, my_state, my_grad, got_state, got_grad, inside):
    half = my_state.shape[0]
    to = ((half * DH + own_through.shape[0], DH), BF16)
    known = [my_state, my_grad, got_state, got_grad]
    to_far, to_middle, to_near, mate_through = call(
        pair_kernel, "pair", [to, to, to, ((2 * half, DH), F32)], [own_through] + known
    )
    from_far = lax.ppermute(to_far, "seq", FAR)
    from_middle = lax.ppermute(to_middle, "seq", MIDDLE)
    from_near = lax.ppermute(to_near, "seq", NEAR)
    inside, mate_through = lax.optimization_barrier((inside, mate_through))
    both = ((2, half, DH, DH), BF16)
    kept, passed = call(
        spread_kernel, "spread", [both, both], [own_through, mate_through] + known + [from_far, from_middle, from_near]
    )
    return kept, lax.ppermute(passed, "seq", MATE), inside


def states_gathered(own, through):
    count = lax.axis_size("seq")
    place = lax.axis_index("seq")
    all_own = lax.all_gather(own, "seq")
    all_through = lax.all_gather(through, "seq")

    def pick(a, i):
        return lax.dynamic_index_in_dim(a, i, 0, False)

    def ahead(step, state):
        return per_head(pick(all_through, step), state) + pick(all_own, step)[0]

    def behind(step, state):
        source = count - 1 - step
        return per_head(pick(all_through, source), state) + pick(all_own, source)[1]

    zero = jnp.zeros_like(own[0])
    state = lax.fori_loop(0, place, ahead, zero)
    grad = lax.fori_loop(0, count - 1 - place, behind, zero)
    return jnp.stack([state, grad]).astype(BF16)


def local(tokens, w_qkv, forget, out_grad, doc_lengths):
    length, part = tokens.shape
    width = w_qkv.shape[2]
    heads = width // DH
    tps = lax.axis_size("tp")
    seqs = lax.axis_size("seq")
    by_hand = tps == 4 and seqs == 8 and heads % 8 == 0
    decays = [((length, 3 * heads + 1), F32), ((3 * heads, length), F32), ((2 * heads, DH), BF16)]
    rows_shape = ((length, width), BF16)
    sum_shape = ((length, width), F32)
    intra_flops = 16 * length * length * width
    forget = forget.T
    if not by_hand:
        gathered = lax.all_gather(tokens, "tp", axis=1, tiled=True)
        projected = jnp.einsum("td,mdc->mtc", gathered, w_qkv, preferred_element_type=F32).astype(BF16)
        qkv = [projected[m] for m in range(3)]
        cols_h, rows_h, through = call(prepare, "prepare", decays, [doc_lengths, forget], "sv")
        through = jnp.sum(through.astype(F32).reshape(2, heads, DH), axis=0)[:, 0]
        (own,) = call(own_states, "own_states", [((2, heads, DH, DH), F32)], qkv + [out_grad, rows_h])
        both = states_gathered(own, through)
        inside = call(intra, "intra", [sum_shape] * 4, qkv + [out_grad, cols_h, rows_h], flops=intra_flops)
        attn, gstack = call(
            finish_whole,
            "finish",
            [sum_shape, ((3, length, width), BF16)],
            qkv + [out_grad, cols_h] + list(inside) + [both],
        )
        grad_terms = jnp.einsum("mtc,mdc->td", gstack, w_qkv, preferred_element_type=F32)
        return attn, lax.psum_scatter(grad_terms, "tp", scatter_dimension=1, tiled=True)

    half = heads // 2
    core = [(i, i ^ 1) for i in range(4)]
    chip = [(i, i ^ 2) for i in range(4)]
    step_flops = 2 * 3 * length * part * width
    across = lax.ppermute(tokens, "tp", chip)
    beside = lax.ppermute(tokens, "tp", core)
    w_vm, acc, cols_h, rows_h, through = call(
        load_and_project,
        "load_and_project",
        [(w_qkv.shape, BF16), ((3, length, width), F32)] + decays,
        [doc_lengths, forget, tokens, w_qkv],
        "hhhh",
        flops=8 * step_flops,
        scratch=[
            pltpu.SMEM(doc_lengths.shape, jnp.int32),
            pltpu.VMEM(forget.shape, F32),
            pltpu.VMEM(tokens.shape, BF16),
            pltpu.SemaphoreType.DMA((tps + 3,)),
        ],
    )

    def project(name, acc, *pieces):
        kernel = functools.partial(project_chunks, [place for place, _ in pieces])
        return call(kernel, name, [(acc.shape, F32)], [x for _, x in pieces] + [w_vm, acc])[0]

    acc = project("project_beside", acc, ((1, 0), beside))
    across, acc = lax.optimization_barrier((across, acc))
    across_beside = lax.ppermute(across, "tp", core)
    acc = project("project_across", acc, ((2, 0), across))
    last = (3, 0)
    states_scratch = [pltpu.VMEM((heads, DH, DH), F32)]
    mine_shape = ((half, DH, DH), F32)
    key, value, my_state, message = call(
        functools.partial(project_key_value, last),
        "project_key_value",
        [rows_shape, rows_shape, mine_shape, ((half * DH + through.shape[0], DH), BF16)],
        [across_beside, w_vm, acc, rows_h, through],
        scratch=states_scratch,
    )
    got_state = lax.ppermute(message, "seq", MATE)
    acc, my_state = lax.optimization_barrier((acc, my_state))
    query, my_grad, message = call(
        functools.partial(project_query, last),
        "project_query",
        [rows_shape, mine_shape, ((half * DH, DH), BF16)],
        [across_beside, w_vm, acc, rows_h, out_grad],
        scratch=states_scratch,
    )
    got_grad = lax.ppermute(message, "seq", MATE)
    inside = call(
        intra, "intra", [sum_shape] * 4, [query, key, value, out_grad, cols_h, rows_h], flops=intra_flops
    )
    kept, passed, inside = states_direct(through, my_state, my_grad, got_state, got_grad, inside)

    part_a = part // 2
    part_b = part - part_a
    stack_shape = ((3, length, width // 2), BF16)
    chunk_shape = ((length, part), F32)
    common = [key, value, out_grad, cols_h] + list(inside[1:])
    kept_stack, start3, start2 = call(
        back_kept, "back_kept", [stack_shape, chunk_shape, chunk_shape], common + [kept, w_vm]
    )
    stack, chunk3_a = call(
        back_first, "back_first", [stack_shape, ((length, part_a), BF16)], common + [passed, w_vm, start3]
    )
    beside_a = lax.ppermute(chunk3_a, "tp", core)
    chunk3_b, chunk_a, chunk_b = call(
        back_second,
        "back_second",
        [((length, part_b), BF16), ((length, part_a), F32), ((length, part_b), F32)],
        [stack, w_vm, start3, start2],
    )
    beside_b = lax.ppermute(chunk3_b, "tp", core)
    chunk_a = (chunk_a + beside_a.astype(F32)).astype(BF16)
    chunk_a, chunk_b = lax.optimization_barrier((chunk_a, chunk_b))
    across_a = lax.ppermute(chunk_a, "tp", chip)
    chunk_b = (chunk_b + beside_b.astype(F32)).astype(BF16)
    chunk_b, stack = lax.optimization_barrier((chunk_b, stack))
    across_b = lax.ppermute(chunk_b, "tp", chip)
    attn, chunk_other, chunk_own = call(
        back_rest,
        "back_rest",
        [sum_shape, ((length, part), BF16), chunk_shape],
        [kept_stack, stack, w_vm, query, cols_h, inside[0], kept, passed],
    )
    beside = [lax.ppermute(c, "tp", core) for c in jnp.split(chunk_other, 4)]
    across = [across_a]
    for more in ([], [across_b]):
        across = list(across) + more
        across = call(
            hand_on,
            "hand_on",
            [(a.shape, BF16) for a in across],
            across,
            flops=8 * step_flops if more else 0,
            aliases={i: i for i in range(len(across))},
        )
    (input_grad,) = call(
        last_sum,
        "last_sum",
        [chunk_shape],
        [chunk_own] + list(across) + beside,
        out_space=pltpu.HBM,
        scratch=[pltpu.VMEM(chunk_shape[0], F32), pltpu.SemaphoreType.DMA((len(beside),))],
    )
    return attn, input_grad


def solution(mesh):
    placed = (P("seq", "tp"), P(None, None, "tp"), P("seq", "tp"), P("seq", "tp"), P())
    return jax.shard_map(
        local,
        mesh=mesh,
        in_specs=placed,
        out_specs=(P("seq", "tp"), P("seq", "tp")),
        check_vma=False,
    )
```

```python
import functools

import jax
import jax.numpy as jnp
from jax import lax
from jax.experimental import pallas as pl
from jax.experimental.pallas import tpu as pltpu
from jax.sharding import PartitionSpec as P

DH = 128
F32 = jnp.float32
BF16 = jnp.bfloat16
MIB = 1 << 20


def dot(a, b, ca, cb):
    return lax.dot_general(a, b, (((ca,), (cb,)), ((), ())), preferred_element_type=F32)


def split(a):
    high = a.astype(BF16)
    return high, (a - high.astype(F32)).astype(BF16)


def dot_split(a, b, ca, cb):
    high, low = split(a)
    return dot(high, b, ca, cb) + dot(low, b, ca, cb)


def call(kernel, name, outs, args, spaces=None, flops=0, limit=4, aliases=None, scratch=(), out_space=pltpu.VMEM):
    spaces = spaces or "v" * len(args)
    kinds = {"v": pltpu.VMEM, "s": pltpu.SMEM, "h": pltpu.HBM}
    placed = [
        a if s == "s" else pltpu.with_memory_space_constraint(a, kinds[s])
        for a, s in zip(args, spaces)
    ]
    return pl.pallas_call(
        kernel,
        name=name,
        out_shape=[out_space(shape, dtype) for shape, dtype in outs],
        in_specs=[pl.BlockSpec(memory_space=kinds[s]) for s in spaces],
        out_specs=[pl.BlockSpec(memory_space=out_space)] * len(outs),
        input_output_aliases=aliases or {},
        scratch_shapes=scratch,
        compiler_params=pltpu.CompilerParams(vmem_limit_bytes=limit * MIB),
        cost_estimate=pl.CostEstimate(flops=flops, bytes_accessed=0, transcendentals=0),
    )(*placed)


def tiles(width):
    tile = 256 if width % 256 == 0 else 128
    return [slice(i, i + tile) for i in range(0, width, tile)]


def rows_of(which, part, offset=0, size=None):
    size = size or part
    return pl.ds(pl.multiple_of((lax.axis_index("tp") ^ which) * part + offset, size), size)


def group_place():
    place = lax.axis_index("seq")
    return place % 4, place // 4


def pick(index, values):
    out = values[-1]
    for i in reversed(range(len(values) - 1)):
        out = jnp.where(index == i, values[i], out)
    return out


def prepare(lengths, forget, cols_h, rows_h, through):
    heads, count = forget.shape
    offset = lax.axis_index("seq") * count
    t = lax.broadcasted_iota(jnp.int32, (count, count), 0)
    s = lax.broadcasted_iota(jnp.int32, (count, count), 1)
    lower = jnp.where(s <= t, 1.0, 0.0).astype(BF16)
    high, rest = split(forget[...])
    rest = forget[...] - high.astype(F32)
    middle, low = split(rest)

    def weights(axis):
        if axis:
            total = dot(high, lower, 1, 1) + (dot(middle, lower, 1, 1) + dot(low, lower, 1, 1))
        else:
            total = dot(lower, high, 1, 1) + (dot(lower, middle, 1, 1) + dot(lower, low, 1, 1))
        shape = (1, count) if axis else (count, 1)
        position = offset + lax.broadcasted_iota(jnp.int32, shape, axis)
        first, end = jnp.zeros(shape, jnp.int32), jnp.int32(0)
        for j in range(lengths.shape[0]):
            end = end + lengths[j]
            first = jnp.where(position >= end, end, first)
        first = first - offset
        last = lax.slice_in_dim(first, count - 1, count, axis=axis)
        final = lax.slice_in_dim(total, count - 1, count, axis=axis)
        lead = jnp.where(first < 0, jnp.exp(total), 0.0)
        tail = jnp.where(first == last, jnp.exp(jnp.where(first == last, final - total, 0.0)), 0.0)
        return total, lead, tail, first

    total, lead, tail, first = weights(0)
    cols_h[:, :heads] = total
    cols_h[:, heads : 2 * heads] = lead
    cols_h[:, 2 * heads : 3 * heads] = tail
    cols_h[:, 3 * heads : 3 * heads + 1] = first.astype(F32)
    total, lead, tail, first = weights(1)
    rows_h[:heads, :] = total
    rows_h[heads : 2 * heads, :] = lead
    rows_h[2 * heads :, :] = tail
    factor = jnp.broadcast_to(lead[:, count - 1 :], (heads, DH))
    through[...] = jnp.concatenate(split(factor), axis=0)


def load_and_project(lengths, forget, tokens, w, w_vm, acc, cols_h, rows_h, through, lengths_sm, forget_vm, own, sems):
    part = tokens.shape[1]
    count = w.shape[1] // part
    small = [
        pltpu.make_async_copy(lengths, lengths_sm, sems.at[count]),
        pltpu.make_async_copy(forget, forget_vm, sems.at[count + 1]),
        pltpu.make_async_copy(tokens, own, sems.at[count + 2]),
    ]
    copies = []
    for j in range(count):
        rows = rows_of(j, part)
        copies.append(pltpu.make_async_copy(w.at[:, rows, :], w_vm.at[:, rows, :], sems.at[j]))
    for copy in small + copies:
        copy.start()
    for copy in small:
        copy.wait()
    prepare(lengths_sm, forget_vm, cols_h, rows_h, through)
    copies[0].wait()
    for m in range(3):
        for cols in tiles(w.shape[2]):
            acc[m, :, cols] = dot(own[...], w_vm[m, rows_of(0, part), cols], 1, 0)
    for copy in copies[1:]:
        copy.wait()


def project_chunks(pieces, *refs):
    xs, (w, acc_in, acc) = refs[: len(pieces)], refs[len(pieces) :]
    for m in range(3):
        for cols in tiles(w.shape[2]):
            acc[m, :, cols] = acc_in[m, :, cols] + products(pieces, xs, w, m, cols)


def products(pieces, xs, w, m, cols):
    part = w.shape[1] // 4
    total = None
    for (which, offset), x in zip(pieces, xs):
        term = dot(x[...], w[m, rows_of(which, part, offset, x.shape[1]), cols], 1, 0)
        total = term if total is None else total + term
    return total


def project_last(piece, x, w, acc_in, rows_h, own_through, grads, query, key, value, mine, to1, to2, to3, states):
    for m, out in ((1, key), (2, value), (0, query)):
        for cols in tiles(w.shape[2]):
            out[:, cols] = (acc_in[m, :, cols] + products([piece], [x], w, m, cols)).astype(BF16)
    own_states(query, key, value, grads, rows_h, states)
    quarter = mine.shape[1]
    place = group_place()[0]
    for d, to in enumerate((mine, to1, to2, to3)):
        for i in range(2):
            for j in range(quarter):
                state = states[i, (place ^ d) * quarter + j]
                if d:
                    first = (i * quarter + j) * DH
                    to[first : first + DH, :] = state.astype(BF16)
                else:
                    to[i, j] = state
        if d:
            to[2 * quarter * DH :, :] = own_through[...]


def columns(cols_h, h):
    heads = cols_h.shape[1] // 3
    return [cols_h[:, i * heads + h : i * heads + h + 1] for i in range(3)]


def state_end(key, value, rows_h, h):
    cols = slice(h * DH, (h + 1) * DH)
    heads = rows_h.shape[0] // 3
    return dot_split(key[:, cols].T.astype(F32) * rows_h[2 * heads + h : 2 * heads + h + 1, :], value[:, cols], 1, 0)


def grad_start(query, grads, rows_h, h):
    cols = slice(h * DH, (h + 1) * DH)
    heads = rows_h.shape[0] // 3
    weight = rows_h[heads + h : heads + h + 1, :] * (1.0 / DH)
    return dot_split(query[:, cols].T.astype(F32) * weight, grads[:, cols], 1, 0)


def own_states(query, key, value, grads, rows_h, states):
    for h in range(states.shape[1]):
        states[0, h] = state_end(key, value, rows_h, h)
        states[1, h] = grad_start(query, grads, rows_h, h)


def intra(query, key, value, grads, cols_h, rows_h, out, gq, gk, gv):
    length, heads = query.shape[0], rows_h.shape[0] // 3
    t = lax.broadcasted_iota(jnp.int32, (length, length), 0)
    s = lax.broadcasted_iota(jnp.int32, (length, length), 1)
    mask = (s <= t) & (s.astype(F32) >= cols_h[:, 3 * heads : 3 * heads + 1])
    for h in range(heads):
        cols = slice(h * DH, (h + 1) * DH)
        gap = jnp.where(mask, columns(cols_h, h)[0] - rows_h[h : h + 1, :], 0.0)
        weight = jnp.where(mask, jnp.exp(gap), 0.0)
        q, k, v, g = query[:, cols], key[:, cols], value[:, cols], grads[:, cols]
        scores = split(dot(q, k, 1, 1) * weight)
        dots = split(dot(g, v, 1, 1) * weight)
        out[:, cols] = dot(scores[0], v, 1, 0) + dot(scores[1], v, 1, 0)
        gq[:, cols] = dot(dots[0], k, 1, 0) + dot(dots[1], k, 1, 0)
        gk[:, cols] = dot(dots[0], q, 0, 0) + dot(dots[1], q, 0, 0)
        gv[:, cols] = dot(scores[0], g, 0, 0) + dot(scores[1], g, 0, 0)


def finish_grads(key, value, grads, gq, gk, gv, cols, lead, tail, state, end, gstack, at):
    gstack[0, :, at] = ((gq[:, cols] + dot(grads[:, cols], state, 1, 1) * lead) * (1.0 / DH)).astype(BF16)
    gstack[1, :, at] = (gk[:, cols] * (1.0 / DH) + dot(value[:, cols], end, 1, 1) * tail).astype(BF16)
    gstack[2, :, at] = (gv[:, cols] * (1.0 / DH) + dot(key[:, cols], end, 1, 0) * tail).astype(BF16)


def finish_whole(query, key, value, grads, cols_h, out, gq, gk, gv, both, attn, gstack):
    for h in range(query.shape[1] // DH):
        cols = slice(h * DH, (h + 1) * DH)
        lead, tail = columns(cols_h, h)[1:]
        finish_grads(key, value, grads, gq, gk, gv, cols, lead, tail, both[0, h], both[1, h], gstack, cols)
        attn[:, cols] = (out[:, cols] + dot(query[:, cols], both[0, h], 1, 0) * lead) * (1.0 / DH)


def quarter_heads(d, quarter, cols_h):
    member = group_place()[0] ^ d
    for j in range(quarter):
        lead, tail = [pick(member, [columns(cols_h, c * quarter + j)[i] for c in range(4)]) for i in (1, 2)]
        yield j, pl.ds(pl.multiple_of((member * quarter + j) * DH, DH), DH), lead, tail


def quarter_columns(d, w):
    width = w.shape[2] // 4
    return pl.ds(pl.multiple_of((group_place()[0] ^ d) * width, width), width)


def finish_quarter(d, key, value, grads, cols_h, gq, gk, gv, states, stack):
    for j, cols, lead, tail in quarter_heads(d, states.shape[1], cols_h):
        at = slice(j * DH, (j + 1) * DH)
        finish_grads(key, value, grads, gq, gk, gv, cols, lead, tail, states[0, j], states[1, j], stack, at)


def back(which, stacks, w, out, offset=0, start=None):
    part = w.shape[1] // 4
    for cols in tiles(out.shape[1]):
        rows = rows_of(which, part, offset + cols.start, cols.stop - cols.start)
        total = None if start is None else start[:, slice(offset + cols.start, offset + cols.stop)]
        for d, stack in stacks:
            for m in range(3):
                term = dot(stack[m], w[m, rows, quarter_columns(d, w)], 1, 1)
                total = term if total is None else total + term
        out[:, cols] = total.astype(out.dtype)


def back_own(key, value, grads, cols_h, gq, gk, gv, states, w, stack, out3, out2):
    finish_quarter(0, key, value, grads, cols_h, gq, gk, gv, states, stack)
    back(3, [(0, stack)], w, out3)
    back(2, [(0, stack)], w, out2)


def back_more(d, key, value, grads, cols_h, gq, gk, gv, states, w, start3, start2, stack, out3, out2):
    finish_quarter(d, key, value, grads, cols_h, gq, gk, gv, states, stack)
    back(3, [(d, stack)], w, out3, 0, start3)
    back(2, [(d, stack)], w, out2, 0, start2)


def back_first(key, value, grads, cols_h, gq, gk, gv, states, w, start3, stack, chunk3_a):
    finish_quarter(3, key, value, grads, cols_h, gq, gk, gv, states, stack)
    back(3, [(3, stack)], w, chunk3_a, 0, start3)


def back_second(stack, w, start3, start2, chunk3_b, chunk2_a, chunk2_b):
    back(3, [(3, stack)], w, chunk3_b, start3.shape[1] - chunk3_b.shape[1], start3)
    back(2, [(3, stack)], w, chunk2_a, 0, start2)
    back(2, [(3, stack)], w, chunk2_b, chunk2_a.shape[1], start2)


def hand_on(*refs):
    pass


def last_sum(own, across_a, across_b, *refs):
    besides, (out, total, sems) = refs[:-3], refs[-3:]
    size, middle = besides[0].shape[0], across_a.shape[1]
    copies = []
    for i, beside in enumerate(besides):
        rows = slice(i * size, (i + 1) * size)
        for cols, across in ((slice(0, middle), across_a), (slice(middle, own.shape[1]), across_b)):
            total[rows, cols] = (own[rows, cols] + beside[:, cols].astype(F32)) + across[rows, :].astype(F32)
        copies.append(pltpu.make_async_copy(total.at[rows, :], out.at[rows, :], sems.at[i]))
        copies[-1].start()
    for copy in copies:
        copy.wait()


def back_rest(stack0, stack1, stack2, stack3, w, query, cols_h, out, states0, states1, states2, states3, *outs):
    attn, chunk_other, chunk_own = outs
    stacks = list(enumerate((stack0, stack1, stack2, stack3)))
    back(1, stacks, w, chunk_other)
    back(0, stacks, w, chunk_own)
    for d, states in enumerate((states0, states1, states2, states3)):
        for j, cols, lead, _ in quarter_heads(d, states.shape[1], cols_h):
            attn[:, cols] = (out[:, cols] + dot(query[:, cols], states[0, j], 1, 0) * lead) * (1.0 / DH)


def per_head(scale, matrix):
    return scale[..., None, None] * matrix


def head_factors(rows):
    half = rows.shape[0] // 2
    return rows[:half].astype(F32) + rows[half:].astype(F32)


def join_kernel(own_through, mine, got1, got2, got3, to_group, inner, factors):
    quarter = mine.shape[1]
    place, group = group_place()
    gots = (got1, got2, got3)
    through = [own_through] + [got.at[2 * quarter * DH :, :] for got in gots]
    through = [head_factors(rows[...]) for rows in through]
    ones = jnp.ones((1, DH), F32)
    for j in range(quarter):
        step = [pick(place, [t[c * quarter + j : c * quarter + j + 1] for c in range(4)]) for t in through]
        step = [pick(place, [step[k ^ p] for p in range(4)]) for k in range(4)]
        totals = []
        for i in range(2):
            first = (i * quarter + j) * DH
            own = [mine[i, j]] + [got[first : first + DH, :].astype(F32) for got in gots]
            own = [pick(place, [own[k ^ p] for p in range(4)]) for k in range(4)]
            order = (0, 1, 2, 3) if i == 0 else (3, 2, 1, 0)
            state, factor = jnp.zeros((DH, DH), F32), ones
            for k in order:
                inner[i, k, j], factors[i, k, j] = state, factor
                state, factor = own[k] + step[k] * state, step[k] * factor
            totals.append(state)
        to_group[j * DH : (j + 1) * DH, :] = jnp.where(group == 0, totals[0], totals[1]).astype(BF16)


def spread_kernel(inner, factors, other, *outs):
    quarter = inner.shape[2]
    place, group = group_place()
    for j in range(quarter):
        arrived = other[j * DH : (j + 1) * DH, :].astype(F32)
        for d, out in enumerate(outs):
            for i in range(2):
                factor = jnp.where(group == 1 - i, factors[i, place ^ d, j], 0.0)
                out[i, j] = (inner[i, place ^ d, j] + factor * arrived).astype(BF16)


def member(d):
    return [(i, i ^ d) for i in range(8)]


def states_direct(own_through, mine, messages, inside):
    quarter = mine.shape[1]
    got = [lax.ppermute(message, "seq", member(d)) for d, message in zip((1, 2, 3), messages)]
    inside, mine = lax.optimization_barrier((inside, mine))
    to_group, inner, factors = call(
        join_kernel,
        "join",
        [((quarter * DH, DH), BF16), ((2, 4, quarter, DH, DH), F32), ((2, 4, quarter, 1, DH), F32)],
        [own_through, mine] + got,
    )
    other = lax.ppermute(to_group, "seq", member(4))
    states = call(spread_kernel, "spread", [(mine.shape, BF16)] * 4, [inner, factors, other])
    return [states[0]] + [lax.ppermute(states[d], "seq", member(d)) for d in (1, 2, 3)], inside


def states_gathered(own, through):
    count = lax.axis_size("seq")
    place = lax.axis_index("seq")
    all_own = lax.all_gather(own, "seq")
    all_through = lax.all_gather(through, "seq")

    def pick(a, i):
        return lax.dynamic_index_in_dim(a, i, 0, False)

    def ahead(step, state):
        return per_head(pick(all_through, step), state) + pick(all_own, step)[0]

    def behind(step, state):
        source = count - 1 - step
        return per_head(pick(all_through, source), state) + pick(all_own, source)[1]

    zero = jnp.zeros_like(own[0])
    state = lax.fori_loop(0, place, ahead, zero)
    grad = lax.fori_loop(0, count - 1 - place, behind, zero)
    return jnp.stack([state, grad]).astype(BF16)


def local(tokens, w_qkv, forget, out_grad, doc_lengths):
    length, part = tokens.shape
    width = w_qkv.shape[2]
    heads = width // DH
    tps = lax.axis_size("tp")
    seqs = lax.axis_size("seq")
    by_hand = tps == 4 and seqs == 8 and heads % 4 == 0
    decays = [((length, 3 * heads + 1), F32), ((3 * heads, length), F32), ((2 * heads, DH), BF16)]
    rows_shape = ((length, width), BF16)
    sum_shape = ((length, width), F32)
    intra_flops = 16 * length * length * width
    forget = forget.T
    if not by_hand:
        gathered = lax.all_gather(tokens, "tp", axis=1, tiled=True)
        projected = jnp.einsum("td,mdc->mtc", gathered, w_qkv, preferred_element_type=F32).astype(BF16)
        qkv = [projected[m] for m in range(3)]
        cols_h, rows_h, through = call(prepare, "prepare", decays, [doc_lengths, forget], "sv")
        through = jnp.sum(through.astype(F32).reshape(2, heads, DH), axis=0)[:, 0]
        (own,) = call(own_states, "own_states", [((2, heads, DH, DH), F32)], qkv + [out_grad, rows_h])
        both = states_gathered(own, through)
        inside = call(intra, "intra", [sum_shape] * 4, qkv + [out_grad, cols_h, rows_h], flops=intra_flops)
        attn, gstack = call(
            finish_whole,
            "finish",
            [sum_shape, ((3, length, width), BF16)],
            qkv + [out_grad, cols_h] + list(inside) + [both],
        )
        grad_terms = jnp.einsum("mtc,mdc->td", gstack, w_qkv, preferred_element_type=F32)
        return attn, lax.psum_scatter(grad_terms, "tp", scatter_dimension=1, tiled=True)

    quarter = heads // 4
    core = [(i, i ^ 1) for i in range(4)]
    chip = [(i, i ^ 2) for i in range(4)]
    step_flops = 2 * 3 * length * part * width
    across = lax.ppermute(tokens, "tp", chip)
    beside = lax.ppermute(tokens, "tp", core)
    w_vm, acc, cols_h, rows_h, through = call(
        load_and_project,
        "load_and_project",
        [(w_qkv.shape, BF16), ((3, length, width), F32)] + decays,
        [doc_lengths, forget, tokens, w_qkv],
        "hhhh",
        flops=8 * step_flops,
        scratch=[
            pltpu.SMEM(doc_lengths.shape, jnp.int32),
            pltpu.VMEM(forget.shape, F32),
            pltpu.VMEM(tokens.shape, BF16),
            pltpu.SemaphoreType.DMA((tps + 3,)),
        ],
    )

    def project(name, acc, *pieces):
        kernel = functools.partial(project_chunks, [place for place, _ in pieces])
        return call(kernel, name, [(acc.shape, F32)], [x for _, x in pieces] + [w_vm, acc])[0]

    acc = project("project_beside", acc, ((1, 0), beside))
    across, acc = lax.optimization_barrier((across, acc))
    across_beside = lax.ppermute(across, "tp", core)
    acc = project("project_across", acc, ((2, 0), across))
    last = (3, 0)
    message_shape = ((2 * quarter * DH + through.shape[0], DH), BF16)
    query, key, value, mine, *messages = call(
        functools.partial(project_last, last),
        "project_last",
        [rows_shape] * 3 + [((2, quarter, DH, DH), F32)] + [message_shape] * 3,
        [across_beside, w_vm, acc, rows_h, through, out_grad],
        scratch=[pltpu.VMEM((2, heads, DH, DH), F32)],
    )
    inside = call(
        intra, "intra", [sum_shape] * 4, [query, key, value, out_grad, cols_h, rows_h], flops=intra_flops
    )
    states, inside = states_direct(through, mine, messages, inside)

    part_a = part // 2
    part_b = part - part_a
    stack_shape = ((3, length, width // 4), BF16)
    chunk_shape = ((length, part), F32)
    common = [key, value, out_grad, cols_h] + list(inside[1:])
    stack0, start3, start2 = call(
        back_own, "back_own", [stack_shape, chunk_shape, chunk_shape], common + [states[0], w_vm]
    )
    stacks = [stack0]
    for d in (1, 2):
        stack, start3, start2 = call(
            functools.partial(back_more, d),
            f"back_{d}",
            [stack_shape, chunk_shape, chunk_shape],
            common + [states[d], w_vm, start3, start2],
            aliases={9: 1, 10: 2},
        )
        stacks.append(stack)
    stack3, chunk3_a = call(
        back_first, "back_first", [stack_shape, ((length, part_a), BF16)], common + [states[3], w_vm, start3]
    )
    beside_a = lax.ppermute(chunk3_a, "tp", core)
    chunk3_b, chunk_a, chunk_b = call(
        back_second,
        "back_second",
        [((length, part_b), BF16), ((length, part_a), F32), ((length, part_b), F32)],
        [stack3, w_vm, start3, start2],
    )
    beside_b = lax.ppermute(chunk3_b, "tp", core)
    chunk_a = (chunk_a + beside_a.astype(F32)).astype(BF16)
    chunk_a, chunk_b = lax.optimization_barrier((chunk_a, chunk_b))
    across_a = lax.ppermute(chunk_a, "tp", chip)
    chunk_b = (chunk_b + beside_b.astype(F32)).astype(BF16)
    chunk_b, stack3 = lax.optimization_barrier((chunk_b, stack3))
    across_b = lax.ppermute(chunk_b, "tp", chip)
    attn, chunk_other, chunk_own = call(
        back_rest,
        "back_rest",
        [sum_shape, ((length, part), BF16), chunk_shape],
        stacks + [stack3, w_vm, query, cols_h, inside[0]] + states,
    )
    beside = [lax.ppermute(c, "tp", core) for c in jnp.split(chunk_other, 4)]
    across = [across_a]
    for more in ([], [across_b]):
        across = list(across) + more
        across = call(
            hand_on,
            "hand_on",
            [(a.shape, BF16) for a in across],
            across,
            flops=8 * step_flops if more else 0,
            aliases={i: i for i in range(len(across))},
        )
    (input_grad,) = call(
        last_sum,
        "last_sum",
        [chunk_shape],
        [chunk_own] + list(across) + beside,
        out_space=pltpu.HBM,
        scratch=[pltpu.VMEM(chunk_shape[0], F32), pltpu.SemaphoreType.DMA((len(beside),))],
    )
    return attn, input_grad


def solution(mesh):
    placed = (P("seq", "tp"), P(None, None, "tp"), P("seq", "tp"), P("seq", "tp"), P())
    return jax.shard_map(
        local,
        mesh=mesh,
        in_specs=placed,
        out_specs=(P("seq", "tp"), P("seq", "tp")),
        check_vma=False,
    )
```

```python
import functools

import jax
import jax.numpy as jnp
from jax import lax
from jax.experimental import pallas as pl
from jax.experimental.pallas import tpu as pltpu
from jax.sharding import PartitionSpec as P

DH = 128
F32 = jnp.float32
BF16 = jnp.bfloat16
MIB = 1 << 20


def dot(a, b, ca, cb):
    return lax.dot_general(a, b, (((ca,), (cb,)), ((), ())), preferred_element_type=F32)


def split(a):
    high = a.astype(BF16)
    return high, (a - high.astype(F32)).astype(BF16)


def dot_split(a, b, ca, cb):
    high, low = split(a)
    return dot(high, b, ca, cb) + dot(low, b, ca, cb)


def call(kernel, name, outs, args, spaces=None, flops=0, limit=4, aliases=None, scratch=(), out_spaces=None):
    spaces = spaces or "v" * len(args)
    out_spaces = out_spaces or "v" * len(outs)
    kinds = {"v": pltpu.VMEM, "s": pltpu.SMEM, "h": pltpu.HBM}
    placed = [
        a if s == "s" else pltpu.with_memory_space_constraint(a, kinds[s])
        for a, s in zip(args, spaces)
    ]
    return pl.pallas_call(
        kernel,
        name=name,
        out_shape=[kinds[s](shape, dtype) for s, (shape, dtype) in zip(out_spaces, outs)],
        in_specs=[pl.BlockSpec(memory_space=kinds[s]) for s in spaces],
        out_specs=[pl.BlockSpec(memory_space=kinds[s]) for s in out_spaces],
        input_output_aliases=aliases or {},
        scratch_shapes=scratch,
        compiler_params=pltpu.CompilerParams(vmem_limit_bytes=limit * MIB),
        cost_estimate=pl.CostEstimate(flops=flops, bytes_accessed=0, transcendentals=0),
    )(*placed)


def tiles(width):
    tile = 256 if width % 256 == 0 else 128
    return [slice(i, i + tile) for i in range(0, width, tile)]


def rows_of(which, part, offset=0, size=None):
    size = size or part
    return pl.ds(pl.multiple_of((lax.axis_index("tp") ^ which) * part + offset, size), size)


def group_place():
    place = lax.axis_index("seq")
    return place % 4, place // 4


def pick(index, values):
    out = values[-1]
    for i in reversed(range(len(values) - 1)):
        out = jnp.where(index == i, values[i], out)
    return out


def prepare(lengths, forget, cols_h, rows_h, through):
    heads, count = forget.shape
    offset = lax.axis_index("seq") * count
    t = lax.broadcasted_iota(jnp.int32, (count, count), 0)
    s = lax.broadcasted_iota(jnp.int32, (count, count), 1)
    lower = jnp.where(s <= t, 1.0, 0.0).astype(BF16)
    high, rest = split(forget[...])
    rest = forget[...] - high.astype(F32)
    middle, low = split(rest)

    def weights(axis):
        if axis:
            total = dot(high, lower, 1, 1) + (dot(middle, lower, 1, 1) + dot(low, lower, 1, 1))
        else:
            total = dot(lower, high, 1, 1) + (dot(lower, middle, 1, 1) + dot(lower, low, 1, 1))
        shape = (1, count) if axis else (count, 1)
        position = offset + lax.broadcasted_iota(jnp.int32, shape, axis)
        first, end = jnp.zeros(shape, jnp.int32), jnp.int32(0)
        for j in range(lengths.shape[0]):
            end = end + lengths[j]
            first = jnp.where(position >= end, end, first)
        first = first - offset
        last = lax.slice_in_dim(first, count - 1, count, axis=axis)
        final = lax.slice_in_dim(total, count - 1, count, axis=axis)
        lead = jnp.where(first < 0, jnp.exp(total), 0.0)
        tail = jnp.where(first == last, jnp.exp(jnp.where(first == last, final - total, 0.0)), 0.0)
        return total, lead, tail, first

    total, lead, tail, first = weights(0)
    cols_h[:, :heads] = total
    cols_h[:, heads : 2 * heads] = lead
    cols_h[:, 2 * heads : 3 * heads] = tail
    cols_h[:, 3 * heads : 3 * heads + 1] = first.astype(F32)
    total, lead, tail, first = weights(1)
    rows_h[:heads, :] = total
    rows_h[heads : 2 * heads, :] = lead
    rows_h[2 * heads :, :] = tail
    factor = jnp.broadcast_to(lead[:, count - 1 :], (heads, DH))
    through[...] = jnp.concatenate(split(factor), axis=0)


def load_and_project(lengths, forget, tokens, w, w_vm, acc, cols_h, rows_h, through, lengths_sm, forget_vm, own, sems):
    part = tokens.shape[1]
    count = w.shape[1] // part
    small = [
        pltpu.make_async_copy(lengths, lengths_sm, sems.at[count]),
        pltpu.make_async_copy(forget, forget_vm, sems.at[count + 1]),
        pltpu.make_async_copy(tokens, own, sems.at[count + 2]),
    ]
    copies = []
    for j in range(count):
        rows = rows_of(j, part)
        copies.append(pltpu.make_async_copy(w.at[:, rows, :], w_vm.at[:, rows, :], sems.at[j]))
    for copy in small + copies:
        copy.start()
    for copy in small:
        copy.wait()
    prepare(lengths_sm, forget_vm, cols_h, rows_h, through)
    copies[0].wait()
    for m in range(3):
        for cols in tiles(w.shape[2]):
            acc[m, :, cols] = dot(own[...], w_vm[m, rows_of(0, part), cols], 1, 0)
    for copy in copies[1:]:
        copy.wait()


def project_chunks(pieces, *refs):
    xs, (w, acc_in, acc) = refs[: len(pieces)], refs[len(pieces) :]
    for m in range(3):
        for cols in tiles(w.shape[2]):
            acc[m, :, cols] = acc_in[m, :, cols] + products(pieces, xs, w, m, cols)


def products(pieces, xs, w, m, cols):
    part = w.shape[1] // 4
    total = None
    for (which, offset), x in zip(pieces, xs):
        term = dot(x[...], w[m, rows_of(which, part, offset, x.shape[1]), cols], 1, 0)
        total = term if total is None else total + term
    return total


def project_last(piece, x, w, acc_in, rows_h, own_through, grads, query, key, value, mine, to1, to2, to3, states):
    for m, out in ((1, key), (2, value), (0, query)):
        for cols in tiles(w.shape[2]):
            out[:, cols] = (acc_in[m, :, cols] + products([piece], [x], w, m, cols)).astype(BF16)
    own_states(query, key, value, grads, rows_h, states)
    quarter = mine.shape[1]
    place = group_place()[0]
    for d, to in enumerate((mine, to1, to2, to3)):
        for i in range(2):
            for j in range(quarter):
                state = states[i, (place ^ d) * quarter + j]
                if d:
                    first = (i * quarter + j) * DH
                    to[first : first + DH, :] = state.astype(BF16)
                else:
                    to[i, j] = state
        if d:
            to[2 * quarter * DH :, :] = own_through[...]


def columns(cols_h, h):
    heads = cols_h.shape[1] // 3
    return [cols_h[:, i * heads + h : i * heads + h + 1] for i in range(3)]


def state_end(key, value, rows_h, h):
    cols = slice(h * DH, (h + 1) * DH)
    heads = rows_h.shape[0] // 3
    return dot_split(key[:, cols].T.astype(F32) * rows_h[2 * heads + h : 2 * heads + h + 1, :], value[:, cols], 1, 0)


def grad_start(query, grads, rows_h, h):
    cols = slice(h * DH, (h + 1) * DH)
    heads = rows_h.shape[0] // 3
    weight = rows_h[heads + h : heads + h + 1, :] * (1.0 / DH)
    return dot_split(query[:, cols].T.astype(F32) * weight, grads[:, cols], 1, 0)


def own_states(query, key, value, grads, rows_h, states):
    for h in range(states.shape[1]):
        states[0, h] = state_end(key, value, rows_h, h)
        states[1, h] = grad_start(query, grads, rows_h, h)


def intra(query, key, value, grads, cols_h, rows_h, out, gq, gk, gv):
    length, heads = query.shape[0], rows_h.shape[0] // 3
    t = lax.broadcasted_iota(jnp.int32, (length, length), 0)
    s = lax.broadcasted_iota(jnp.int32, (length, length), 1)
    mask = (s <= t) & (s.astype(F32) >= cols_h[:, 3 * heads : 3 * heads + 1])
    for h in range(heads):
        cols = slice(h * DH, (h + 1) * DH)
        gap = jnp.where(mask, columns(cols_h, h)[0] - rows_h[h : h + 1, :], 0.0)
        weight = jnp.where(mask, jnp.exp(gap), 0.0)
        q, k, v, g = query[:, cols], key[:, cols], value[:, cols], grads[:, cols]
        scores = split(dot(q, k, 1, 1) * weight)
        dots = split(dot(g, v, 1, 1) * weight)
        out[:, cols] = dot(scores[0], v, 1, 0) + dot(scores[1], v, 1, 0)
        gq[:, cols] = dot(dots[0], k, 1, 0) + dot(dots[1], k, 1, 0)
        gk[:, cols] = dot(dots[0], q, 0, 0) + dot(dots[1], q, 0, 0)
        gv[:, cols] = dot(scores[0], g, 0, 0) + dot(scores[1], g, 0, 0)


def finish_grads(key, value, grads, gq, gk, gv, cols, lead, tail, state, end, gstack, at):
    gstack[0, :, at] = ((gq[:, cols] + dot(grads[:, cols], state, 1, 1) * lead) * (1.0 / DH)).astype(BF16)
    gstack[1, :, at] = (gk[:, cols] * (1.0 / DH) + dot(value[:, cols], end, 1, 1) * tail).astype(BF16)
    gstack[2, :, at] = (gv[:, cols] * (1.0 / DH) + dot(key[:, cols], end, 1, 0) * tail).astype(BF16)


def finish_whole(query, key, value, grads, cols_h, out, gq, gk, gv, both, attn, gstack):
    for h in range(query.shape[1] // DH):
        cols = slice(h * DH, (h + 1) * DH)
        lead, tail = columns(cols_h, h)[1:]
        finish_grads(key, value, grads, gq, gk, gv, cols, lead, tail, both[0, h], both[1, h], gstack, cols)
        attn[:, cols] = (out[:, cols] + dot(query[:, cols], both[0, h], 1, 0) * lead) * (1.0 / DH)


def quarter_heads(d, quarter, cols_h):
    member = group_place()[0] ^ d
    for j in range(quarter):
        lead, tail = [pick(member, [columns(cols_h, c * quarter + j)[i] for c in range(4)]) for i in (1, 2)]
        yield j, pl.ds(pl.multiple_of((member * quarter + j) * DH, DH), DH), lead, tail


def quarter_columns(d, w):
    width = w.shape[2] // 4
    return pl.ds(pl.multiple_of((group_place()[0] ^ d) * width, width), width)


def finish_quarter(d, key, value, grads, cols_h, gq, gk, gv, states, stack):
    for j, cols, lead, tail in quarter_heads(d, states.shape[1], cols_h):
        at = slice(j * DH, (j + 1) * DH)
        finish_grads(key, value, grads, gq, gk, gv, cols, lead, tail, states[0, j], states[1, j], stack, at)


def back(which, stacks, w, out, offset=0, start=None):
    part = w.shape[1] // 4
    for cols in tiles(out.shape[1]):
        rows = rows_of(which, part, offset + cols.start, cols.stop - cols.start)
        total = None if start is None else start[:, slice(offset + cols.start, offset + cols.stop)]
        for d, stack in stacks:
            for m in range(3):
                term = dot(stack[m], w[m, rows, quarter_columns(d, w)], 1, 1)
                total = term if total is None else total + term
        out[:, cols] = total.astype(out.dtype)


def back_own(key, value, grads, cols_h, gq, gk, gv, states, w, stack, out3, out2):
    finish_quarter(0, key, value, grads, cols_h, gq, gk, gv, states, stack)
    back(3, [(0, stack)], w, out3)
    back(2, [(0, stack)], w, out2)


def back_sides(key, value, grads, cols_h, gq, gk, gv, states1, states2, w, start3, stack1, stack2, out3):
    finish_quarter(1, key, value, grads, cols_h, gq, gk, gv, states1, stack1)
    finish_quarter(2, key, value, grads, cols_h, gq, gk, gv, states2, stack2)
    back(3, [(1, stack1), (2, stack2)], w, out3, 0, start3)


def back_first(key, value, grads, cols_h, gq, gk, gv, states, w, start3, stack, chunk3_a):
    finish_quarter(3, key, value, grads, cols_h, gq, gk, gv, states, stack)
    back(3, [(3, stack)], w, chunk3_a, 0, start3)


def back_second(stack1, stack2, stack3, w, start3, start2, chunk3_b, chunk2_a):
    back(3, [(3, stack3)], w, chunk3_b, start3.shape[1] - chunk3_b.shape[1], start3)
    back(2, [(1, stack1), (2, stack2), (3, stack3)], w, chunk2_a, 0, start2)


def back_third(stack1, stack2, stack3, w, start2, chunk2_b):
    back(2, [(1, stack1), (2, stack2), (3, stack3)], w, chunk2_b, start2.shape[1] - chunk2_b.shape[1], start2)


def hand_on(*refs):
    pass


def last_sum(own, across_b, *refs):
    besides, (out, total, sems) = refs[:-3], refs[-3:]
    size, middle = besides[0].shape[0], own.shape[1] - across_b.shape[1]
    copies = []
    for i, beside in enumerate(besides):
        rows = slice(i * size, (i + 1) * size)
        total[rows, :middle] = own[rows, :middle] + beside[:, :middle].astype(F32)
        right = own[rows, middle:] + beside[:, middle:].astype(F32)
        total[rows, middle:] = right + across_b[rows, :].astype(F32)
        copies.append(pltpu.make_async_copy(total.at[rows, :], out.at[rows, :], sems.at[i]))
        copies[-1].start()
    for copy in copies:
        copy.wait()


def back_mine(stack0, stack1, stack2, stack3, w, query, cols_h, out, states0, states1, states2, states3, *refs):
    attn, chunk_own, attn_vm, sem = refs
    for d, states in enumerate((states0, states1, states2, states3)):
        for j, cols, lead, _ in quarter_heads(d, states.shape[1], cols_h):
            attn_vm[:, cols] = (out[:, cols] + dot(query[:, cols], states[0, j], 1, 0) * lead) * (1.0 / DH)
    copy = pltpu.make_async_copy(attn_vm, attn, sem)
    copy.start()
    back(0, list(enumerate((stack0, stack1, stack2, stack3))), w, chunk_own)
    copy.wait()


def back_other(stack0, stack1, stack2, stack3, w, across_a, own_in, chunk_other, own):
    back(1, list(enumerate((stack0, stack1, stack2, stack3))), w, chunk_other)
    middle = across_a.shape[1]
    own[:, :middle] = own_in[:, :middle] + across_a[...].astype(F32)
    own[:, middle:] = own_in[:, middle:]


def per_head(scale, matrix):
    return scale[..., None, None] * matrix


def head_factors(rows):
    half = rows.shape[0] // 2
    return rows[:half].astype(F32) + rows[half:].astype(F32)


def join_kernel(own_through, mine, got1, got2, got3, to_group, inner, factors):
    quarter = mine.shape[1]
    place, group = group_place()
    gots = (got1, got2, got3)
    through = [own_through] + [got.at[2 * quarter * DH :, :] for got in gots]
    through = [head_factors(rows[...]) for rows in through]
    ones = jnp.ones((1, DH), F32)
    for j in range(quarter):
        step = [pick(place, [t[c * quarter + j : c * quarter + j + 1] for c in range(4)]) for t in through]
        step = [pick(place, [step[k ^ p] for p in range(4)]) for k in range(4)]
        totals = []
        for i in range(2):
            first = (i * quarter + j) * DH
            own = [mine[i, j]] + [got[first : first + DH, :].astype(F32) for got in gots]
            own = [pick(place, [own[k ^ p] for p in range(4)]) for k in range(4)]
            order = (0, 1, 2, 3) if i == 0 else (3, 2, 1, 0)
            state, factor = jnp.zeros((DH, DH), F32), ones
            for k in order:
                inner[i, k, j], factors[i, k, j] = state, factor
                state, factor = own[k] + step[k] * state, step[k] * factor
            totals.append(state)
        to_group[j * DH : (j + 1) * DH, :] = jnp.where(group == 0, totals[0], totals[1]).astype(BF16)


def spread_kernel(inner, factors, other, *outs):
    quarter = inner.shape[2]
    place, group = group_place()
    for j in range(quarter):
        arrived = other[j * DH : (j + 1) * DH, :].astype(F32)
        for d, out in enumerate(outs):
            for i in range(2):
                factor = jnp.where(group == 1 - i, factors[i, place ^ d, j], 0.0)
                out[i, j] = (inner[i, place ^ d, j] + factor * arrived).astype(BF16)


def member(d):
    return [(i, i ^ d) for i in range(8)]


def states_direct(own_through, mine, messages, inside):
    quarter = mine.shape[1]
    got = [lax.ppermute(message, "seq", member(d)) for d, message in zip((1, 2, 3), messages)]
    inside, mine = lax.optimization_barrier((inside, mine))
    to_group, inner, factors = call(
        join_kernel,
        "join",
        [((quarter * DH, DH), BF16), ((2, 4, quarter, DH, DH), F32), ((2, 4, quarter, 1, DH), F32)],
        [own_through, mine] + got,
    )
    other = lax.ppermute(to_group, "seq", member(4))
    states = call(spread_kernel, "spread", [(mine.shape, BF16)] * 4, [inner, factors, other])
    return [states[0]] + [lax.ppermute(states[d], "seq", member(d)) for d in (1, 2, 3)], inside


def states_gathered(own, through):
    count = lax.axis_size("seq")
    place = lax.axis_index("seq")
    all_own = lax.all_gather(own, "seq")
    all_through = lax.all_gather(through, "seq")

    def pick(a, i):
        return lax.dynamic_index_in_dim(a, i, 0, False)

    def ahead(step, state):
        return per_head(pick(all_through, step), state) + pick(all_own, step)[0]

    def behind(step, state):
        source = count - 1 - step
        return per_head(pick(all_through, source), state) + pick(all_own, source)[1]

    zero = jnp.zeros_like(own[0])
    state = lax.fori_loop(0, place, ahead, zero)
    grad = lax.fori_loop(0, count - 1 - place, behind, zero)
    return jnp.stack([state, grad]).astype(BF16)


def local(tokens, w_qkv, forget, out_grad, doc_lengths):
    length, part = tokens.shape
    width = w_qkv.shape[2]
    heads = width // DH
    tps = lax.axis_size("tp")
    seqs = lax.axis_size("seq")
    by_hand = tps == 4 and seqs == 8 and heads % 4 == 0
    decays = [((length, 3 * heads + 1), F32), ((3 * heads, length), F32), ((2 * heads, DH), BF16)]
    rows_shape = ((length, width), BF16)
    sum_shape = ((length, width), F32)
    intra_flops = 16 * length * length * width
    forget = forget.T
    if not by_hand:
        gathered = lax.all_gather(tokens, "tp", axis=1, tiled=True)
        projected = jnp.einsum("td,mdc->mtc", gathered, w_qkv, preferred_element_type=F32).astype(BF16)
        qkv = [projected[m] for m in range(3)]
        cols_h, rows_h, through = call(prepare, "prepare", decays, [doc_lengths, forget], "sv")
        through = jnp.sum(through.astype(F32).reshape(2, heads, DH), axis=0)[:, 0]
        (own,) = call(own_states, "own_states", [((2, heads, DH, DH), F32)], qkv + [out_grad, rows_h])
        both = states_gathered(own, through)
        inside = call(intra, "intra", [sum_shape] * 4, qkv + [out_grad, cols_h, rows_h], flops=intra_flops)
        attn, gstack = call(
            finish_whole,
            "finish",
            [sum_shape, ((3, length, width), BF16)],
            qkv + [out_grad, cols_h] + list(inside) + [both],
        )
        grad_terms = jnp.einsum("mtc,mdc->td", gstack, w_qkv, preferred_element_type=F32)
        return attn, lax.psum_scatter(grad_terms, "tp", scatter_dimension=1, tiled=True)

    quarter = heads // 4
    core = [(i, i ^ 1) for i in range(4)]
    chip = [(i, i ^ 2) for i in range(4)]
    step_flops = 2 * 3 * length * part * width
    across = lax.ppermute(tokens, "tp", chip)
    beside = lax.ppermute(tokens, "tp", core)
    w_vm, acc, cols_h, rows_h, through = call(
        load_and_project,
        "load_and_project",
        [(w_qkv.shape, BF16), ((3, length, width), F32)] + decays,
        [doc_lengths, forget, tokens, w_qkv],
        "hhhh",
        flops=8 * step_flops,
        scratch=[
            pltpu.SMEM(doc_lengths.shape, jnp.int32),
            pltpu.VMEM(forget.shape, F32),
            pltpu.VMEM(tokens.shape, BF16),
            pltpu.SemaphoreType.DMA((tps + 3,)),
        ],
    )

    def project(name, acc, *pieces):
        kernel = functools.partial(project_chunks, [place for place, _ in pieces])
        return call(kernel, name, [(acc.shape, F32)], [x for _, x in pieces] + [w_vm, acc])[0]

    acc = project("project_beside", acc, ((1, 0), beside))
    across, acc = lax.optimization_barrier((across, acc))
    across_beside = lax.ppermute(across, "tp", core)
    acc = project("project_across", acc, ((2, 0), across))
    last = (3, 0)
    message_shape = ((2 * quarter * DH + through.shape[0], DH), BF16)
    query, key, value, mine, *messages = call(
        functools.partial(project_last, last),
        "project_last",
        [rows_shape] * 3 + [((2, quarter, DH, DH), F32)] + [message_shape] * 3,
        [across_beside, w_vm, acc, rows_h, through, out_grad],
        scratch=[pltpu.VMEM((2, heads, DH, DH), F32)],
    )
    inside = call(
        intra, "intra", [sum_shape] * 4, [query, key, value, out_grad, cols_h, rows_h], flops=intra_flops
    )
    states, inside = states_direct(through, mine, messages, inside)

    part_a = part // 2
    part_b = part - part_a
    stack_shape = ((3, length, width // 4), BF16)
    chunk_shape = ((length, part), F32)
    common = [key, value, out_grad, cols_h] + list(inside[1:])
    stack0, start3, start2 = call(
        back_own, "back_own", [stack_shape, chunk_shape, chunk_shape], common + [states[0], w_vm]
    )
    stack1, stack2, start3 = call(
        back_sides,
        "back_sides",
        [stack_shape, stack_shape, chunk_shape],
        common + [states[1], states[2], w_vm, start3],
        aliases={10: 2},
    )
    stack3, chunk3_a = call(
        back_first, "back_first", [stack_shape, ((length, part_a), BF16)], common + [states[3], w_vm, start3]
    )
    beside_a = lax.ppermute(chunk3_a, "tp", core)
    late = [stack1, stack2, stack3, w_vm]
    chunk3_b, chunk_a = call(
        back_second, "back_second", [((length, part_b), BF16), ((length, part_a), F32)], late + [start3, start2]
    )
    beside_b = lax.ppermute(chunk3_b, "tp", core)
    chunk_a = (chunk_a + beside_a.astype(F32)).astype(BF16)
    chunk_a, start2 = lax.optimization_barrier((chunk_a, start2))
    across_a = lax.ppermute(chunk_a, "tp", chip)
    (chunk_b,) = call(back_third, "back_third", [((length, part_b), F32)], late + [start2])
    chunk_b = (chunk_b + beside_b.astype(F32)).astype(BF16)
    chunk_b, stack0 = lax.optimization_barrier((chunk_b, stack0))
    across_b = lax.ppermute(chunk_b, "tp", chip)
    attn, chunk_own = call(
        back_mine,
        "back_mine",
        [sum_shape, chunk_shape],
        [stack0] + late + [query, cols_h, inside[0]] + states,
        out_spaces="hv",
        scratch=[pltpu.VMEM(sum_shape[0], F32), pltpu.SemaphoreType.DMA],
    )
    chunk_other, chunk_own = call(
        back_other,
        "back_other",
        [((length, part), BF16), chunk_shape],
        [stack0] + late + [across_a, chunk_own],
        flops=step_flops,
        aliases={6: 1},
    )
    beside = [lax.ppermute(c, "tp", core) for c in jnp.split(chunk_other, 4)]
    (across_b,) = call(
        hand_on, "hand_on", [(across_b.shape, BF16)], [across_b], flops=8 * step_flops, aliases={0: 0}
    )
    (input_grad,) = call(
        last_sum,
        "last_sum",
        [chunk_shape],
        [chunk_own, across_b] + beside,
        out_spaces="h",
        scratch=[pltpu.VMEM(chunk_shape[0], F32), pltpu.SemaphoreType.DMA((len(beside),))],
    )
    return attn, input_grad


def solution(mesh):
    placed = (P("seq", "tp"), P(None, None, "tp"), P("seq", "tp"), P("seq", "tp"), P())
    return jax.shard_map(
        local,
        mesh=mesh,
        in_specs=placed,
        out_specs=(P("seq", "tp"), P("seq", "tp")),
        check_vma=False,
    )
```

```python
import functools

import jax
import jax.numpy as jnp
from jax import lax
from jax.experimental import pallas as pl
from jax.experimental.pallas import tpu as pltpu
from jax.sharding import PartitionSpec as P

DH = 128
F32 = jnp.float32
BF16 = jnp.bfloat16
MIB = 1 << 20


def dot(a, b, ca, cb):
    return lax.dot_general(a, b, (((ca,), (cb,)), ((), ())), preferred_element_type=F32)


def split(a):
    high = a.astype(BF16)
    return high, (a - high.astype(F32)).astype(BF16)


def dot_split(a, b, ca, cb):
    high, low = split(a)
    return dot(high, b, ca, cb) + dot(low, b, ca, cb)


def call(kernel, name, outs, args, spaces=None, flops=0, limit=4, aliases=None, scratch=(), out_spaces=None):
    spaces = spaces or "v" * len(args)
    out_spaces = out_spaces or "v" * len(outs)
    kinds = {"v": pltpu.VMEM, "s": pltpu.SMEM, "h": pltpu.HBM}
    placed = [
        a if s == "s" else pltpu.with_memory_space_constraint(a, kinds[s])
        for a, s in zip(args, spaces)
    ]
    return pl.pallas_call(
        kernel,
        name=name,
        out_shape=[kinds[s](shape, dtype) for s, (shape, dtype) in zip(out_spaces, outs)],
        in_specs=[pl.BlockSpec(memory_space=kinds[s]) for s in spaces],
        out_specs=[pl.BlockSpec(memory_space=kinds[s]) for s in out_spaces],
        input_output_aliases=aliases or {},
        scratch_shapes=scratch,
        compiler_params=pltpu.CompilerParams(vmem_limit_bytes=limit * MIB),
        cost_estimate=pl.CostEstimate(flops=flops, bytes_accessed=0, transcendentals=0),
    )(*placed)


def tiles(width):
    tile = 256 if width % 256 == 0 else 128
    return [slice(i, i + tile) for i in range(0, width, tile)]


def rows_of(which, part, offset=0, size=None):
    size = size or part
    return pl.ds(pl.multiple_of((lax.axis_index("tp") ^ which) * part + offset, size), size)


def group_place():
    place = lax.axis_index("seq")
    return place % 4, place // 4


def order_of(turn):
    odd = lax.axis_index("tp") % 2
    return (0, 1 + odd, 2 - odd, 3)[turn]


def pick(index, values):
    out = values[-1]
    for i in reversed(range(len(values) - 1)):
        out = jnp.where(index == i, values[i], out)
    return out


def prepare(lengths, forget, cols_h, rows_h, through):
    heads, count = forget.shape
    offset = lax.axis_index("seq") * count
    t = lax.broadcasted_iota(jnp.int32, (count, count), 0)
    s = lax.broadcasted_iota(jnp.int32, (count, count), 1)
    lower = jnp.where(s <= t, 1.0, 0.0).astype(BF16)
    high, rest = split(forget[...])
    rest = forget[...] - high.astype(F32)
    middle, low = split(rest)

    def weights(axis):
        if axis:
            total = dot(high, lower, 1, 1) + (dot(middle, lower, 1, 1) + dot(low, lower, 1, 1))
        else:
            total = dot(lower, high, 1, 1) + (dot(lower, middle, 1, 1) + dot(lower, low, 1, 1))
        shape = (1, count) if axis else (count, 1)
        position = offset + lax.broadcasted_iota(jnp.int32, shape, axis)
        first, end = jnp.zeros(shape, jnp.int32), jnp.int32(0)
        for j in range(lengths.shape[0]):
            end = end + lengths[j]
            first = jnp.where(position >= end, end, first)
        first = first - offset
        last = lax.slice_in_dim(first, count - 1, count, axis=axis)
        final = lax.slice_in_dim(total, count - 1, count, axis=axis)
        lead = jnp.where(first < 0, jnp.exp(total), 0.0)
        tail = jnp.where(first == last, jnp.exp(jnp.where(first == last, final - total, 0.0)), 0.0)
        return total, lead, tail, first

    total, lead, tail, first = weights(0)
    cols_h[:, :heads] = total
    cols_h[:, heads : 2 * heads] = lead
    cols_h[:, 2 * heads : 3 * heads] = tail
    cols_h[:, 3 * heads : 3 * heads + 1] = first.astype(F32)
    total, lead, tail, first = weights(1)
    rows_h[:heads, :] = total
    rows_h[heads : 2 * heads, :] = lead
    rows_h[2 * heads :, :] = tail
    factor = jnp.broadcast_to(lead[:, count - 1 :], (heads, DH))
    through[...] = jnp.concatenate(split(factor), axis=0)


def load_and_project(lengths, forget, tokens, w, w_vm, acc, cols_h, rows_h, through, lengths_sm, forget_vm, own, sems):
    part = tokens.shape[1]
    count = w.shape[1] // part
    small = [
        pltpu.make_async_copy(lengths, lengths_sm, sems.at[count]),
        pltpu.make_async_copy(forget, forget_vm, sems.at[count + 1]),
        pltpu.make_async_copy(tokens, own, sems.at[count + 2]),
    ]
    copies = []
    for j in range(count):
        rows = rows_of(j, part)
        copies.append(pltpu.make_async_copy(w.at[:, rows, :], w_vm.at[:, rows, :], sems.at[j]))
    for copy in small + copies:
        copy.start()
    for copy in small:
        copy.wait()
    prepare(lengths_sm, forget_vm, cols_h, rows_h, through)
    copies[0].wait()
    for m in range(3):
        for cols in tiles(w.shape[2]):
            acc[m, :, cols] = dot(own[...], w_vm[m, rows_of(0, part), cols], 1, 0)
    for copy in copies[1:]:
        copy.wait()


def project_chunks(pieces, *refs):
    xs, (w, acc_in, acc) = refs[: len(pieces)], refs[len(pieces) :]
    for m in range(3):
        for cols in tiles(w.shape[2]):
            acc[m, :, cols] = acc_in[m, :, cols] + products(pieces, xs, w, m, cols)


def products(pieces, xs, w, m, cols):
    part = w.shape[1] // 4
    total = None
    for (which, offset), x in zip(pieces, xs):
        term = dot(x[...], w[m, rows_of(which, part, offset, x.shape[1]), cols], 1, 0)
        total = term if total is None else total + term
    return total


def project_last(piece, x, w, acc_in, rows_h, own_through, grads, query, key, value, mine, to1, to2, to3, states):
    for m, out in ((1, key), (2, value), (0, query)):
        for cols in tiles(w.shape[2]):
            out[:, cols] = (acc_in[m, :, cols] + products([piece], [x], w, m, cols)).astype(BF16)
    own_states(query, key, value, grads, rows_h, states)
    quarter = mine.shape[1]
    place = group_place()[0]
    for d, to in enumerate((mine, to1, to2, to3)):
        for i in range(2):
            for j in range(quarter):
                state = states[i, (place ^ order_of(d)) * quarter + j]
                if d:
                    first = (i * quarter + j) * DH
                    to[first : first + DH, :] = state.astype(BF16)
                else:
                    to[i, j] = state
        if d:
            to[2 * quarter * DH :, :] = own_through[...]


def columns(cols_h, h):
    heads = cols_h.shape[1] // 3
    return [cols_h[:, i * heads + h : i * heads + h + 1] for i in range(3)]


def state_end(key, value, rows_h, h):
    cols = slice(h * DH, (h + 1) * DH)
    heads = rows_h.shape[0] // 3
    return dot_split(key[:, cols].T.astype(F32) * rows_h[2 * heads + h : 2 * heads + h + 1, :], value[:, cols], 1, 0)


def grad_start(query, grads, rows_h, h):
    cols = slice(h * DH, (h + 1) * DH)
    heads = rows_h.shape[0] // 3
    weight = rows_h[heads + h : heads + h + 1, :] * (1.0 / DH)
    return dot_split(query[:, cols].T.astype(F32) * weight, grads[:, cols], 1, 0)


def own_states(query, key, value, grads, rows_h, states):
    for h in range(states.shape[1]):
        states[0, h] = state_end(key, value, rows_h, h)
        states[1, h] = grad_start(query, grads, rows_h, h)


def intra(query, key, value, grads, cols_h, rows_h, out, gq, gk, gv):
    length, heads = query.shape[0], rows_h.shape[0] // 3
    t = lax.broadcasted_iota(jnp.int32, (length, length), 0)
    s = lax.broadcasted_iota(jnp.int32, (length, length), 1)
    mask = (s <= t) & (s.astype(F32) >= cols_h[:, 3 * heads : 3 * heads + 1])
    for h in range(heads):
        cols = slice(h * DH, (h + 1) * DH)
        gap = jnp.where(mask, columns(cols_h, h)[0] - rows_h[h : h + 1, :], 0.0)
        weight = jnp.where(mask, jnp.exp(gap), 0.0)
        q, k, v, g = query[:, cols], key[:, cols], value[:, cols], grads[:, cols]
        scores = split(dot(q, k, 1, 1) * weight)
        dots = split(dot(g, v, 1, 1) * weight)
        out[:, cols] = dot(scores[0], v, 1, 0) + dot(scores[1], v, 1, 0)
        gq[:, cols] = dot(dots[0], k, 1, 0) + dot(dots[1], k, 1, 0)
        gk[:, cols] = dot(dots[0], q, 0, 0) + dot(dots[1], q, 0, 0)
        gv[:, cols] = dot(scores[0], g, 0, 0) + dot(scores[1], g, 0, 0)


def finish_grads(key, value, grads, gq, gk, gv, cols, lead, tail, state, end, gstack, at):
    gstack[0, :, at] = ((gq[:, cols] + dot(grads[:, cols], state, 1, 1) * lead) * (1.0 / DH)).astype(BF16)
    gstack[1, :, at] = (gk[:, cols] * (1.0 / DH) + dot(value[:, cols], end, 1, 1) * tail).astype(BF16)
    gstack[2, :, at] = (gv[:, cols] * (1.0 / DH) + dot(key[:, cols], end, 1, 0) * tail).astype(BF16)


def finish_whole(query, key, value, grads, cols_h, out, gq, gk, gv, both, attn, gstack):
    for h in range(query.shape[1] // DH):
        cols = slice(h * DH, (h + 1) * DH)
        lead, tail = columns(cols_h, h)[1:]
        finish_grads(key, value, grads, gq, gk, gv, cols, lead, tail, both[0, h], both[1, h], gstack, cols)
        attn[:, cols] = (out[:, cols] + dot(query[:, cols], both[0, h], 1, 0) * lead) * (1.0 / DH)


def quarter_heads(d, quarter, cols_h):
    member = group_place()[0] ^ order_of(d)
    for j in range(quarter):
        lead, tail = [pick(member, [columns(cols_h, c * quarter + j)[i] for c in range(4)]) for i in (1, 2)]
        yield j, pl.ds(pl.multiple_of((member * quarter + j) * DH, DH), DH), lead, tail


def quarter_columns(d, w):
    width = w.shape[2] // 4
    return pl.ds(pl.multiple_of((group_place()[0] ^ order_of(d)) * width, width), width)


def finish_quarter(d, key, value, grads, cols_h, gq, gk, gv, states, stack):
    for j, cols, lead, tail in quarter_heads(d, states.shape[1], cols_h):
        at = slice(j * DH, (j + 1) * DH)
        finish_grads(key, value, grads, gq, gk, gv, cols, lead, tail, states[0, j], states[1, j], stack, at)


def back(which, stacks, w, out, offset=0, start=None):
    part = w.shape[1] // 4
    for cols in tiles(out.shape[1]):
        rows = rows_of(which, part, offset + cols.start, cols.stop - cols.start)
        total = None if start is None else start[:, slice(offset + cols.start, offset + cols.stop)]
        for d, stack in stacks:
            for m in range(3):
                term = dot(stack[m], w[m, rows, quarter_columns(d, w)], 1, 1)
                total = term if total is None else total + term
        out[:, cols] = total.astype(out.dtype)


def back_own(key, value, grads, cols_h, gq, gk, gv, states, w, stack, out3, out2):
    finish_quarter(0, key, value, grads, cols_h, gq, gk, gv, states, stack)
    back(3, [(0, stack)], w, out3)
    back(2, [(0, stack)], w, out2)


def back_sides(key, value, grads, cols_h, gq, gk, gv, states1, states2, w, start3, stack1, stack2, out3):
    finish_quarter(1, key, value, grads, cols_h, gq, gk, gv, states1, stack1)
    finish_quarter(2, key, value, grads, cols_h, gq, gk, gv, states2, stack2)
    back(3, [(1, stack1), (2, stack2)], w, out3, 0, start3)


def back_first(key, value, grads, cols_h, gq, gk, gv, states, w, start3, stack, chunk3_a):
    finish_quarter(3, key, value, grads, cols_h, gq, gk, gv, states, stack)
    back(3, [(3, stack)], w, chunk3_a, 0, start3)


def back_second(stack1, stack2, stack3, w, start3, start2, chunk3_b, chunk2_a):
    back(3, [(3, stack3)], w, chunk3_b, start3.shape[1] - chunk3_b.shape[1], start3)
    back(2, [(1, stack1), (2, stack2), (3, stack3)], w, chunk2_a, 0, start2)


def back_third(stack1, stack2, stack3, w, start2, chunk2_b):
    back(2, [(1, stack1), (2, stack2), (3, stack3)], w, chunk2_b, start2.shape[1] - chunk2_b.shape[1], start2)


def hand_on(*refs):
    pass


def last_sum(own, across_b, *refs):
    besides, (out, total, sems) = refs[:-3], refs[-3:]
    size, middle = besides[0].shape[0], own.shape[1] - across_b.shape[1]
    copies = []
    for i, beside in enumerate(besides):
        rows = slice(i * size, (i + 1) * size)
        total[rows, :middle] = own[rows, :middle] + beside[:, :middle].astype(F32)
        right = own[rows, middle:] + beside[:, middle:].astype(F32)
        total[rows, middle:] = right + across_b[rows, :].astype(F32)
        copies.append(pltpu.make_async_copy(total.at[rows, :], out.at[rows, :], sems.at[i]))
        copies[-1].start()
    for copy in copies:
        copy.wait()


def back_mine(stack0, stack1, stack2, stack3, w, query, cols_h, out, states0, states1, states2, states3, *refs):
    attn, chunk_own, attn_vm, sem = refs
    for d, states in enumerate((states0, states1, states2, states3)):
        for j, cols, lead, _ in quarter_heads(d, states.shape[1], cols_h):
            attn_vm[:, cols] = (out[:, cols] + dot(query[:, cols], states[0, j], 1, 0) * lead) * (1.0 / DH)
    copy = pltpu.make_async_copy(attn_vm, attn, sem)
    copy.start()
    back(0, list(enumerate((stack0, stack1, stack2, stack3))), w, chunk_own)
    copy.wait()


def back_other(stack0, stack1, stack2, stack3, w, across_a, own_in, chunk_other, own):
    back(1, list(enumerate((stack0, stack1, stack2, stack3))), w, chunk_other)
    middle = across_a.shape[1]
    own[:, :middle] = own_in[:, :middle] + across_a[...].astype(F32)
    own[:, middle:] = own_in[:, middle:]


def per_head(scale, matrix):
    return scale[..., None, None] * matrix


def head_factors(rows):
    half = rows.shape[0] // 2
    return rows[:half].astype(F32) + rows[half:].astype(F32)


def join_kernel(own_through, mine, got1, got2, got3, to_group, inner, factors):
    quarter = mine.shape[1]
    place, group = group_place()
    odd = order_of(1) == 2

    def by_member(first, rows):
        one, two, three = [got[rows, :] for got in (got1, got2, got3)]
        return [first, jnp.where(odd, two, one), jnp.where(odd, one, two), three]

    through = [head_factors(rows) for rows in by_member(own_through[...], slice(2 * quarter * DH, got1.shape[0]))]
    ones = jnp.ones((1, DH), F32)
    for j in range(quarter):
        step = [pick(place, [t[c * quarter + j : c * quarter + j + 1] for c in range(4)]) for t in through]
        step = [pick(place, [step[k ^ p] for p in range(4)]) for k in range(4)]
        totals = []
        for i in range(2):
            first = (i * quarter + j) * DH
            own = [a.astype(F32) for a in by_member(mine[i, j], slice(first, first + DH))]
            own = [pick(place, [own[k ^ p] for p in range(4)]) for k in range(4)]
            order = (0, 1, 2, 3) if i == 0 else (3, 2, 1, 0)
            state, factor = jnp.zeros((DH, DH), F32), ones
            for k in order:
                inner[i, k, j], factors[i, k, j] = state, factor
                state, factor = own[k] + step[k] * state, step[k] * factor
            totals.append(state)
        to_group[j * DH : (j + 1) * DH, :] = jnp.where(group == 0, totals[0], totals[1]).astype(BF16)


def spread_kernel(inner, factors, other, *outs):
    quarter = inner.shape[2]
    place, group = group_place()
    for j in range(quarter):
        arrived = other[j * DH : (j + 1) * DH, :].astype(F32)
        for turn, out in enumerate(outs):
            k = place ^ order_of(turn)
            for i in range(2):
                factor = jnp.where(group == 1 - i, factors[i, k, j], 0.0)
                out[i, j] = (inner[i, k, j] + factor * arrived).astype(BF16)


def to_other_group(a):
    return lax.ppermute(a, "seq", [(i, i ^ 4) for i in range(8)])


def to_member(a, turn):
    seqs, tps = lax.axis_size("seq"), lax.axis_size("tp")
    pairs = []
    for i in range(seqs):
        for t in range(tps):
            partner = i ^ (0, 1 + t % 2, 2 - t % 2, 3)[turn]
            pairs.append((i * tps + t, partner * tps + t))
    return lax.ppermute(a, ("seq", "tp"), pairs)


def states_direct(own_through, mine, messages, inside):
    quarter = mine.shape[1]
    got = [to_member(message, turn) for turn, message in zip((1, 2, 3), messages)]
    inside, mine = lax.optimization_barrier((inside, mine))
    to_group, inner, factors = call(
        join_kernel,
        "join",
        [((quarter * DH, DH), BF16), ((2, 4, quarter, DH, DH), F32), ((2, 4, quarter, 1, DH), F32)],
        [own_through, mine] + got,
    )
    other = to_other_group(to_group)
    states = call(spread_kernel, "spread", [(mine.shape, BF16)] * 4, [inner, factors, other])
    return [states[0]] + [to_member(states[turn], turn) for turn in (1, 2, 3)], inside


def states_gathered(own, through):
    count = lax.axis_size("seq")
    place = lax.axis_index("seq")
    all_own = lax.all_gather(own, "seq")
    all_through = lax.all_gather(through, "seq")

    def pick(a, i):
        return lax.dynamic_index_in_dim(a, i, 0, False)

    def ahead(step, state):
        return per_head(pick(all_through, step), state) + pick(all_own, step)[0]

    def behind(step, state):
        source = count - 1 - step
        return per_head(pick(all_through, source), state) + pick(all_own, source)[1]

    zero = jnp.zeros_like(own[0])
    state = lax.fori_loop(0, place, ahead, zero)
    grad = lax.fori_loop(0, count - 1 - place, behind, zero)
    return jnp.stack([state, grad]).astype(BF16)


def local(tokens, w_qkv, forget, out_grad, doc_lengths):
    length, part = tokens.shape
    width = w_qkv.shape[2]
    heads = width // DH
    tps = lax.axis_size("tp")
    seqs = lax.axis_size("seq")
    by_hand = tps == 4 and seqs == 8 and heads % 4 == 0
    decays = [((length, 3 * heads + 1), F32), ((3 * heads, length), F32), ((2 * heads, DH), BF16)]
    rows_shape = ((length, width), BF16)
    sum_shape = ((length, width), F32)
    intra_flops = 16 * length * length * width
    forget = forget.T
    if not by_hand:
        gathered = lax.all_gather(tokens, "tp", axis=1, tiled=True)
        projected = jnp.einsum("td,mdc->mtc", gathered, w_qkv, preferred_element_type=F32).astype(BF16)
        qkv = [projected[m] for m in range(3)]
        cols_h, rows_h, through = call(prepare, "prepare", decays, [doc_lengths, forget], "sv")
        through = jnp.sum(through.astype(F32).reshape(2, heads, DH), axis=0)[:, 0]
        (own,) = call(own_states, "own_states", [((2, heads, DH, DH), F32)], qkv + [out_grad, rows_h])
        both = states_gathered(own, through)
        inside = call(intra, "intra", [sum_shape] * 4, qkv + [out_grad, cols_h, rows_h], flops=intra_flops)
        attn, gstack = call(
            finish_whole,
            "finish",
            [sum_shape, ((3, length, width), BF16)],
            qkv + [out_grad, cols_h] + list(inside) + [both],
        )
        grad_terms = jnp.einsum("mtc,mdc->td", gstack, w_qkv, preferred_element_type=F32)
        return attn, lax.psum_scatter(grad_terms, "tp", scatter_dimension=1, tiled=True)

    quarter = heads // 4
    core = [(i, i ^ 1) for i in range(4)]
    chip = [(i, i ^ 2) for i in range(4)]
    step_flops = 2 * 3 * length * part * width
    across = lax.ppermute(tokens, "tp", chip)
    beside = lax.ppermute(tokens, "tp", core)
    w_vm, acc, cols_h, rows_h, through = call(
        load_and_project,
        "load_and_project",
        [(w_qkv.shape, BF16), ((3, length, width), F32)] + decays,
        [doc_lengths, forget, tokens, w_qkv],
        "hhhh",
        flops=8 * step_flops,
        scratch=[
            pltpu.SMEM(doc_lengths.shape, jnp.int32),
            pltpu.VMEM(forget.shape, F32),
            pltpu.VMEM(tokens.shape, BF16),
            pltpu.SemaphoreType.DMA((tps + 3,)),
        ],
    )

    def project(name, acc, *pieces):
        kernel = functools.partial(project_chunks, [place for place, _ in pieces])
        return call(kernel, name, [(acc.shape, F32)], [x for _, x in pieces] + [w_vm, acc])[0]

    acc = project("project_beside", acc, ((1, 0), beside))
    across, acc = lax.optimization_barrier((across, acc))
    across_beside = lax.ppermute(across, "tp", core)
    acc = project("project_across", acc, ((2, 0), across))
    last = (3, 0)
    message_shape = ((2 * quarter * DH + through.shape[0], DH), BF16)
    query, key, value, mine, *messages = call(
        functools.partial(project_last, last),
        "project_last",
        [rows_shape] * 3 + [((2, quarter, DH, DH), F32)] + [message_shape] * 3,
        [across_beside, w_vm, acc, rows_h, through, out_grad],
        scratch=[pltpu.VMEM((2, heads, DH, DH), F32)],
    )
    inside = call(
        intra, "intra", [sum_shape] * 4, [query, key, value, out_grad, cols_h, rows_h], flops=intra_flops
    )
    states, inside = states_direct(through, mine, messages, inside)

    part_a = part // 2
    part_b = part - part_a
    stack_shape = ((3, length, width // 4), BF16)
    chunk_shape = ((length, part), F32)
    common = [key, value, out_grad, cols_h] + list(inside[1:])
    stack0, start3, start2 = call(
        back_own, "back_own", [stack_shape, chunk_shape, chunk_shape], common + [states[0], w_vm]
    )
    stack1, stack2, start3 = call(
        back_sides,
        "back_sides",
        [stack_shape, stack_shape, chunk_shape],
        common + [states[1], states[2], w_vm, start3],
        aliases={10: 2},
    )
    stack3, chunk3_a = call(
        back_first, "back_first", [stack_shape, ((length, part_a), BF16)], common + [states[3], w_vm, start3]
    )
    beside_a = lax.ppermute(chunk3_a, "tp", core)
    late = [stack1, stack2, stack3, w_vm]
    chunk3_b, chunk_a = call(
        back_second, "back_second", [((length, part_b), BF16), ((length, part_a), F32)], late + [start3, start2]
    )
    beside_b = lax.ppermute(chunk3_b, "tp", core)
    chunk_a = (chunk_a + beside_a.astype(F32)).astype(BF16)
    chunk_a, start2 = lax.optimization_barrier((chunk_a, start2))
    across_a = lax.ppermute(chunk_a, "tp", chip)
    (chunk_b,) = call(back_third, "back_third", [((length, part_b), F32)], late + [start2])
    chunk_b = (chunk_b + beside_b.astype(F32)).astype(BF16)
    chunk_b, stack0 = lax.optimization_barrier((chunk_b, stack0))
    across_b = lax.ppermute(chunk_b, "tp", chip)
    attn, chunk_own = call(
        back_mine,
        "back_mine",
        [sum_shape, chunk_shape],
        [stack0] + late + [query, cols_h, inside[0]] + states,
        out_spaces="hv",
        scratch=[pltpu.VMEM(sum_shape[0], F32), pltpu.SemaphoreType.DMA],
    )
    chunk_other, chunk_own = call(
        back_other,
        "back_other",
        [((length, part), BF16), chunk_shape],
        [stack0] + late + [across_a, chunk_own],
        flops=step_flops,
        aliases={6: 1},
    )
    beside = [lax.ppermute(c, "tp", core) for c in jnp.split(chunk_other, 4)]
    (across_b,) = call(
        hand_on, "hand_on", [(across_b.shape, BF16)], [across_b], flops=8 * step_flops, aliases={0: 0}
    )
    (input_grad,) = call(
        last_sum,
        "last_sum",
        [chunk_shape],
        [chunk_own, across_b] + beside,
        out_spaces="h",
        scratch=[pltpu.VMEM(chunk_shape[0], F32), pltpu.SemaphoreType.DMA((len(beside),))],
    )
    return attn, input_grad


def solution(mesh):
    placed = (P("seq", "tp"), P(None, None, "tp"), P("seq", "tp"), P("seq", "tp"), P())
    return jax.shard_map(
        local,
        mesh=mesh,
        in_specs=placed,
        out_specs=(P("seq", "tp"), P("seq", "tp")),
        check_vma=False,
    )
```

```python
import functools

import jax
import jax.numpy as jnp
from jax import lax
from jax.experimental import pallas as pl
from jax.experimental.pallas import tpu as pltpu
from jax.sharding import PartitionSpec as P

DH = 128
F32 = jnp.float32
BF16 = jnp.bfloat16
MIB = 1 << 20


def dot(a, b, ca, cb):
    return lax.dot_general(a, b, (((ca,), (cb,)), ((), ())), preferred_element_type=F32)


def split(a):
    high = a.astype(BF16)
    return high, (a - high.astype(F32)).astype(BF16)


def call(kernel, name, outs, args, spaces=None, flops=0, limit=4, aliases=None, scratch=(), out_spaces=None):
    spaces = spaces or "v" * len(args)
    out_spaces = out_spaces or "v" * len(outs)
    kinds = {"v": pltpu.VMEM, "s": pltpu.SMEM, "h": pltpu.HBM}
    placed = [
        a if s == "s" else pltpu.with_memory_space_constraint(a, kinds[s])
        for a, s in zip(args, spaces)
    ]
    return pl.pallas_call(
        kernel,
        name=name,
        out_shape=[kinds[s](shape, dtype) for s, (shape, dtype) in zip(out_spaces, outs)],
        in_specs=[pl.BlockSpec(memory_space=kinds[s]) for s in spaces],
        out_specs=[pl.BlockSpec(memory_space=kinds[s]) for s in out_spaces],
        input_output_aliases=aliases or {},
        scratch_shapes=scratch,
        compiler_params=pltpu.CompilerParams(vmem_limit_bytes=limit * MIB),
        cost_estimate=pl.CostEstimate(flops=flops, bytes_accessed=0, transcendentals=0),
    )(*placed)


def tiles(width):
    tile = 256 if width % 256 == 0 else 128
    return [slice(i, i + tile) for i in range(0, width, tile)]


def rows_of(which, part, offset=0, size=None):
    size = size or part
    return pl.ds(pl.multiple_of((lax.axis_index("tp") ^ which) * part + offset, size), size)


def group_place():
    place = lax.axis_index("seq")
    return place % 4, place // 4


def order_of(turn):
    odd = lax.axis_index("tp") % 2
    return (0, 1 + odd, 2 - odd, 3)[turn]


def pick(index, values):
    out = values[-1]
    for i in reversed(range(len(values) - 1)):
        out = jnp.where(index == i, values[i], out)
    return out


def prepare(lengths, forget, cols_h, rows_h, through):
    heads, count = forget.shape
    offset = lax.axis_index("seq") * count
    t = lax.broadcasted_iota(jnp.int32, (count, count), 0)
    s = lax.broadcasted_iota(jnp.int32, (count, count), 1)
    lower = jnp.where(s <= t, 1.0, 0.0).astype(BF16)
    high, rest = split(forget[...])
    rest = forget[...] - high.astype(F32)
    middle, low = split(rest)

    def weights(axis):
        if axis:
            total = dot(high, lower, 1, 1) + (dot(middle, lower, 1, 1) + dot(low, lower, 1, 1))
        else:
            total = dot(lower, high, 1, 1) + (dot(lower, middle, 1, 1) + dot(lower, low, 1, 1))
        shape = (1, count) if axis else (count, 1)
        position = offset + lax.broadcasted_iota(jnp.int32, shape, axis)
        first, end = jnp.zeros(shape, jnp.int32), jnp.int32(0)
        for j in range(lengths.shape[0]):
            end = end + lengths[j]
            first = jnp.where(position >= end, end, first)
        first = first - offset
        last = lax.slice_in_dim(first, count - 1, count, axis=axis)
        final = lax.slice_in_dim(total, count - 1, count, axis=axis)
        lead = jnp.where(first < 0, jnp.exp(total), 0.0)
        tail = jnp.where(first == last, jnp.exp(jnp.where(first == last, final - total, 0.0)), 0.0)
        return total, lead, tail, first

    total, lead, tail, first = weights(0)
    cols_h[:, :heads] = total
    cols_h[:, heads : 2 * heads] = lead
    cols_h[:, 2 * heads : 3 * heads] = tail
    cols_h[:, 3 * heads : 3 * heads + 1] = first.astype(F32)
    total, lead, tail, first = weights(1)
    rows_h[:heads, :] = total
    rows_h[heads : 2 * heads, :] = lead
    rows_h[2 * heads :, :] = tail
    factor = jnp.broadcast_to(lead[:, count - 1 :], (heads, DH))
    through[...] = jnp.concatenate(split(factor), axis=0)


def load_and_project(lengths, forget, tokens, w, w_vm, acc, cols_h, rows_h, through, lengths_sm, forget_vm, own, sems):
    part = tokens.shape[1]
    count = w.shape[1] // part
    small = [
        pltpu.make_async_copy(lengths, lengths_sm, sems.at[count]),
        pltpu.make_async_copy(forget, forget_vm, sems.at[count + 1]),
        pltpu.make_async_copy(tokens, own, sems.at[count + 2]),
    ]
    copies = []
    for j in range(count):
        rows = rows_of(j, part)
        copies.append(pltpu.make_async_copy(w.at[:, rows, :], w_vm.at[:, rows, :], sems.at[j]))
    for copy in small + copies:
        copy.start()
    for copy in small:
        copy.wait()
    prepare(lengths_sm, forget_vm, cols_h, rows_h, through)
    copies[0].wait()
    for m in range(3):
        for cols in tiles(w.shape[2]):
            acc[m, :, cols] = dot(own[...], w_vm[m, rows_of(0, part), cols], 1, 0)
    for copy in copies[1:]:
        copy.wait()


def project_chunks(pieces, *refs):
    xs, (w, acc_in, acc) = refs[: len(pieces)], refs[len(pieces) :]
    for m in range(3):
        for cols in tiles(w.shape[2]):
            acc[m, :, cols] = acc_in[m, :, cols] + products(pieces, xs, w, m, cols)


def products(pieces, xs, w, m, cols):
    part = w.shape[1] // 4
    total = None
    for (which, offset), x in zip(pieces, xs):
        term = dot(x[...], w[m, rows_of(which, part, offset, x.shape[1]), cols], 1, 0)
        total = term if total is None else total + term
    return total


def project_last(piece, x, w, acc_in, rows_h, own_through, grads, query, key, value, mine, to1, to2, to3, states):
    for m, out in ((1, key), (2, value), (0, query)):
        for cols in tiles(w.shape[2]):
            out[:, cols] = (acc_in[m, :, cols] + products([piece], [x], w, m, cols)).astype(BF16)
    own_states(query, key, value, grads, rows_h, states)
    quarter = mine.shape[1]
    place = group_place()[0]
    for d, to in enumerate((mine, to1, to2, to3)):
        for i in range(2):
            for j in range(quarter):
                state = states[i, (place ^ order_of(d)) * quarter + j]
                if d:
                    first = (i * quarter + j) * DH
                    to[first : first + DH, :] = state.astype(BF16)
                else:
                    to[i, j] = state
        if d:
            to[2 * quarter * DH :, :] = own_through[...]


def columns(cols_h, h):
    heads = cols_h.shape[1] // 3
    return [cols_h[:, i * heads + h : i * heads + h + 1] for i in range(3)]


def state_end(key, value, rows_h, h):
    cols = slice(h * DH, (h + 1) * DH)
    heads = rows_h.shape[0] // 3
    return dot((key[:, cols].T.astype(F32) * rows_h[2 * heads + h : 2 * heads + h + 1, :]).astype(BF16), value[:, cols], 1, 0)


def grad_start(query, grads, rows_h, h):
    cols = slice(h * DH, (h + 1) * DH)
    heads = rows_h.shape[0] // 3
    weight = rows_h[heads + h : heads + h + 1, :] * (1.0 / DH)
    return dot((query[:, cols].T.astype(F32) * weight).astype(BF16), grads[:, cols], 1, 0)


def own_states(query, key, value, grads, rows_h, states):
    for h in range(states.shape[1]):
        states[0, h] = state_end(key, value, rows_h, h)
        states[1, h] = grad_start(query, grads, rows_h, h)


def intra(query, key, value, grads, cols_h, rows_h, out, gq, gk, gv):
    length, heads = query.shape[0], rows_h.shape[0] // 3
    t = lax.broadcasted_iota(jnp.int32, (length, length), 0)
    s = lax.broadcasted_iota(jnp.int32, (length, length), 1)
    mask = (s <= t) & (s.astype(F32) >= cols_h[:, 3 * heads : 3 * heads + 1])
    for h in range(heads):
        cols = slice(h * DH, (h + 1) * DH)
        gap = jnp.where(mask, columns(cols_h, h)[0] - rows_h[h : h + 1, :], 0.0)
        weight = jnp.where(mask, jnp.exp(gap), 0.0)
        q, k, v, g = query[:, cols], key[:, cols], value[:, cols], grads[:, cols]
        scores = split(dot(q, k, 1, 1) * weight)
        dots = split(dot(g, v, 1, 1) * weight)
        out[:, cols] = dot(scores[0], v, 1, 0) + dot(scores[1], v, 1, 0)
        gq[:, cols] = dot(dots[0], k, 1, 0) + dot(dots[1], k, 1, 0)
        gk[:, cols] = dot(dots[0], q, 0, 0) + dot(dots[1], q, 0, 0)
        gv[:, cols] = dot(scores[0], g, 0, 0) + dot(scores[1], g, 0, 0)


def finish_grads(key, value, grads, gq, gk, gv, cols, lead, tail, state, end, gstack, at):
    gstack[0, :, at] = ((gq[:, cols] + dot(grads[:, cols], state, 1, 1) * lead) * (1.0 / DH)).astype(BF16)
    gstack[1, :, at] = (gk[:, cols] * (1.0 / DH) + dot(value[:, cols], end, 1, 1) * tail).astype(BF16)
    gstack[2, :, at] = (gv[:, cols] * (1.0 / DH) + dot(key[:, cols], end, 1, 0) * tail).astype(BF16)


def finish_whole(query, key, value, grads, cols_h, out, gq, gk, gv, both, attn, gstack):
    for h in range(query.shape[1] // DH):
        cols = slice(h * DH, (h + 1) * DH)
        lead, tail = columns(cols_h, h)[1:]
        finish_grads(key, value, grads, gq, gk, gv, cols, lead, tail, both[0, h], both[1, h], gstack, cols)
        attn[:, cols] = (out[:, cols] + dot(query[:, cols], both[0, h], 1, 0) * lead) * (1.0 / DH)


def quarter_heads(d, quarter, cols_h):
    member = group_place()[0] ^ order_of(d)
    for j in range(quarter):
        lead, tail = [pick(member, [columns(cols_h, c * quarter + j)[i] for c in range(4)]) for i in (1, 2)]
        yield j, pl.ds(pl.multiple_of((member * quarter + j) * DH, DH), DH), lead, tail


def quarter_columns(d, w):
    width = w.shape[2] // 4
    return pl.ds(pl.multiple_of((group_place()[0] ^ order_of(d)) * width, width), width)


def finish_quarter(d, key, value, grads, cols_h, gq, gk, gv, states, stack):
    for j, cols, lead, tail in quarter_heads(d, states.shape[1], cols_h):
        at = slice(j * DH, (j + 1) * DH)
        finish_grads(key, value, grads, gq, gk, gv, cols, lead, tail, states[0, j], states[1, j], stack, at)


def back(which, stacks, w, out, offset=0, start=None):
    part = w.shape[1] // 4
    size = out.shape[1]
    rows = rows_of(which, part, offset, size)
    total = None if start is None else start[:, offset : offset + size]
    for d, stack in stacks:
        for m in range(3):
            term = dot(stack[m], w[m, rows, quarter_columns(d, w)], 1, 1)
            total = term if total is None else total + term
    out[...] = total.astype(out.dtype)


def back_own(key, value, grads, cols_h, gq, gk, gv, states, w, stack, out3, out2):
    finish_quarter(0, key, value, grads, cols_h, gq, gk, gv, states, stack)
    back(3, [(0, stack)], w, out3)
    back(2, [(0, stack)], w, out2)


def back_sides(key, value, grads, cols_h, gq, gk, gv, states1, states2, w, start3, stack1, stack2, out3):
    finish_quarter(1, key, value, grads, cols_h, gq, gk, gv, states1, stack1)
    finish_quarter(2, key, value, grads, cols_h, gq, gk, gv, states2, stack2)
    back(3, [(1, stack1), (2, stack2)], w, out3, 0, start3)


def back_first(key, value, grads, cols_h, gq, gk, gv, states, w, start3, stack, chunk3_a):
    finish_quarter(3, key, value, grads, cols_h, gq, gk, gv, states, stack)
    back(3, [(3, stack)], w, chunk3_a, 0, start3)


def back_second(stack1, stack2, stack3, w, start3, start2, chunk3_b, chunk2_a):
    back(3, [(3, stack3)], w, chunk3_b, start3.shape[1] - chunk3_b.shape[1], start3)
    back(2, [(1, stack1), (2, stack2), (3, stack3)], w, chunk2_a, 0, start2)


def back_third(stack1, stack2, stack3, w, start2, chunk2_b):
    back(2, [(1, stack1), (2, stack2), (3, stack3)], w, chunk2_b, start2.shape[1] - chunk2_b.shape[1], start2)


def hand_on(*refs):
    pass


def last_sum(own, across_b, *refs):
    besides, (out, total, sems) = refs[:-3], refs[-3:]
    size, middle = besides[0].shape[0], own.shape[1] - across_b.shape[1]
    copies = []
    for i, beside in enumerate(besides):
        rows = slice(i * size, (i + 1) * size)
        total[rows, :middle] = own[rows, :middle] + beside[:, :middle].astype(F32)
        right = own[rows, middle:] + beside[:, middle:].astype(F32)
        total[rows, middle:] = right + across_b[rows, :].astype(F32)
        copies.append(pltpu.make_async_copy(total.at[rows, :], out.at[rows, :], sems.at[i]))
        copies[-1].start()
    for copy in copies:
        copy.wait()


def back_mine(stack0, stack1, stack2, stack3, w, query, cols_h, out, states0, states1, states2, states3, *refs):
    attn, chunk_own, attn_vm, sem = refs
    for d, states in enumerate((states0, states1, states2, states3)):
        for j, cols, lead, _ in quarter_heads(d, states.shape[1], cols_h):
            attn_vm[:, cols] = (out[:, cols] + dot(query[:, cols], states[0, j], 1, 0) * lead) * (1.0 / DH)
    copy = pltpu.make_async_copy(attn_vm, attn, sem)
    copy.start()
    back(0, list(enumerate((stack0, stack1, stack2, stack3))), w, chunk_own)
    copy.wait()


def back_other(stack0, stack1, stack2, stack3, w, across_a, own_in, chunk_other, own):
    back(1, list(enumerate((stack0, stack1, stack2, stack3))), w, chunk_other)
    middle = across_a.shape[1]
    own[:, :middle] = own_in[:, :middle] + across_a[...].astype(F32)
    own[:, middle:] = own_in[:, middle:]


def per_head(scale, matrix):
    return scale[..., None, None] * matrix


def head_factors(rows):
    half = rows.shape[0] // 2
    return rows[:half].astype(F32) + rows[half:].astype(F32)


def join_kernel(own_through, mine, got1, got2, got3, to_group, inner, factors):
    quarter = mine.shape[1]
    place, group = group_place()
    odd = order_of(1) == 2

    def by_member(first, rows):
        one, two, three = [got[rows, :] for got in (got1, got2, got3)]
        return [first, jnp.where(odd, two, one), jnp.where(odd, one, two), three]

    through = [head_factors(rows) for rows in by_member(own_through[...], slice(2 * quarter * DH, got1.shape[0]))]
    ones = jnp.ones((1, DH), F32)
    for j in range(quarter):
        step = [pick(place, [t[c * quarter + j : c * quarter + j + 1] for c in range(4)]) for t in through]
        step = [pick(place, [step[k ^ p] for p in range(4)]) for k in range(4)]
        totals = []
        for i in range(2):
            first = (i * quarter + j) * DH
            own = [a.astype(F32) for a in by_member(mine[i, j], slice(first, first + DH))]
            own = [pick(place, [own[k ^ p] for p in range(4)]) for k in range(4)]
            order = (0, 1, 2, 3) if i == 0 else (3, 2, 1, 0)
            state, factor = jnp.zeros((DH, DH), F32), ones
            for k in order:
                inner[i, k, j], factors[i, k, j] = state, factor
                state, factor = own[k] + step[k] * state, step[k] * factor
            totals.append(state)
        to_group[j * DH : (j + 1) * DH, :] = jnp.where(group == 0, totals[0], totals[1]).astype(BF16)


def spread_kernel(inner, factors, other, *outs):
    quarter = inner.shape[2]
    place, group = group_place()
    for j in range(quarter):
        arrived = other[j * DH : (j + 1) * DH, :].astype(F32)
        for turn, out in enumerate(outs):
            k = place ^ order_of(turn)
            for i in range(2):
                factor = jnp.where(group == 1 - i, factors[i, k, j], 0.0)
                out[i, j] = (inner[i, k, j] + factor * arrived).astype(BF16)


def to_other_group(a):
    return lax.ppermute(a, "seq", [(i, i ^ 4) for i in range(8)])


def to_member(a, turn):
    seqs, tps = lax.axis_size("seq"), lax.axis_size("tp")
    pairs = []
    for i in range(seqs):
        for t in range(tps):
            partner = i ^ (0, 1 + t % 2, 2 - t % 2, 3)[turn]
            pairs.append((i * tps + t, partner * tps + t))
    return lax.ppermute(a, ("seq", "tp"), pairs)


def states_direct(own_through, mine, messages, inside):
    quarter = mine.shape[1]
    got = [to_member(message, turn) for turn, message in zip((1, 2, 3), messages)]
    inside, mine = lax.optimization_barrier((inside, mine))
    to_group, inner, factors = call(
        join_kernel,
        "join",
        [((quarter * DH, DH), BF16), ((2, 4, quarter, DH, DH), F32), ((2, 4, quarter, 1, DH), F32)],
        [own_through, mine] + got,
    )
    other = to_other_group(to_group)
    states = call(spread_kernel, "spread", [(mine.shape, BF16)] * 4, [inner, factors, other])
    return [states[0]] + [to_member(states[turn], turn) for turn in (1, 2, 3)], inside


def states_gathered(own, through):
    count = lax.axis_size("seq")
    place = lax.axis_index("seq")
    all_own = lax.all_gather(own, "seq")
    all_through = lax.all_gather(through, "seq")

    def pick(a, i):
        return lax.dynamic_index_in_dim(a, i, 0, False)

    def ahead(step, state):
        return per_head(pick(all_through, step), state) + pick(all_own, step)[0]

    def behind(step, state):
        source = count - 1 - step
        return per_head(pick(all_through, source), state) + pick(all_own, source)[1]

    zero = jnp.zeros_like(own[0])
    state = lax.fori_loop(0, place, ahead, zero)
    grad = lax.fori_loop(0, count - 1 - place, behind, zero)
    return jnp.stack([state, grad]).astype(BF16)


def local(tokens, w_qkv, forget, out_grad, doc_lengths):
    length, part = tokens.shape
    width = w_qkv.shape[2]
    heads = width // DH
    tps = lax.axis_size("tp")
    seqs = lax.axis_size("seq")
    by_hand = tps == 4 and seqs == 8 and heads % 4 == 0
    decays = [((length, 3 * heads + 1), F32), ((3 * heads, length), F32), ((2 * heads, DH), BF16)]
    rows_shape = ((length, width), BF16)
    sum_shape = ((length, width), F32)
    intra_flops = 16 * length * length * width
    forget = forget.T
    if not by_hand:
        gathered = lax.all_gather(tokens, "tp", axis=1, tiled=True)
        projected = jnp.einsum("td,mdc->mtc", gathered, w_qkv, preferred_element_type=F32).astype(BF16)
        qkv = [projected[m] for m in range(3)]
        cols_h, rows_h, through = call(prepare, "prepare", decays, [doc_lengths, forget], "sv")
        through = jnp.sum(through.astype(F32).reshape(2, heads, DH), axis=0)[:, 0]
        (own,) = call(own_states, "own_states", [((2, heads, DH, DH), F32)], qkv + [out_grad, rows_h])
        both = states_gathered(own, through)
        inside = call(intra, "intra", [sum_shape] * 4, qkv + [out_grad, cols_h, rows_h], flops=intra_flops)
        attn, gstack = call(
            finish_whole,
            "finish",
            [sum_shape, ((3, length, width), BF16)],
            qkv + [out_grad, cols_h] + list(inside) + [both],
        )
        grad_terms = jnp.einsum("mtc,mdc->td", gstack, w_qkv, preferred_element_type=F32)
        return attn, lax.psum_scatter(grad_terms, "tp", scatter_dimension=1, tiled=True)

    quarter = heads // 4
    core = [(i, i ^ 1) for i in range(4)]
    chip = [(i, i ^ 2) for i in range(4)]
    step_flops = 2 * 3 * length * part * width
    across = lax.ppermute(tokens, "tp", chip)
    beside = lax.ppermute(tokens, "tp", core)
    w_vm, acc, cols_h, rows_h, through = call(
        load_and_project,
        "load_and_project",
        [(w_qkv.shape, BF16), ((3, length, width), F32)] + decays,
        [doc_lengths, forget, tokens, w_qkv],
        "hhhh",
        flops=8 * step_flops,
        scratch=[
            pltpu.SMEM(doc_lengths.shape, jnp.int32),
            pltpu.VMEM(forget.shape, F32),
            pltpu.VMEM(tokens.shape, BF16),
            pltpu.SemaphoreType.DMA((tps + 3,)),
        ],
    )

    def project(name, acc, *pieces):
        kernel = functools.partial(project_chunks, [place for place, _ in pieces])
        return call(kernel, name, [(acc.shape, F32)], [x for _, x in pieces] + [w_vm, acc])[0]

    acc = project("project_beside", acc, ((1, 0), beside))
    across, acc = lax.optimization_barrier((across, acc))
    across_beside = lax.ppermute(across, "tp", core)
    acc = project("project_across", acc, ((2, 0), across))
    last = (3, 0)
    message_shape = ((2 * quarter * DH + through.shape[0], DH), BF16)
    query, key, value, mine, *messages = call(
        functools.partial(project_last, last),
        "project_last",
        [rows_shape] * 3 + [((2, quarter, DH, DH), F32)] + [message_shape] * 3,
        [across_beside, w_vm, acc, rows_h, through, out_grad],
        scratch=[pltpu.VMEM((2, heads, DH, DH), F32)],
    )
    inside = call(
        intra, "intra", [sum_shape] * 4, [query, key, value, out_grad, cols_h, rows_h], flops=intra_flops
    )
    states, inside = states_direct(through, mine, messages, inside)

    part_a = part // 2
    part_b = part - part_a
    stack_shape = ((3, length, width // 4), BF16)
    chunk_shape = ((length, part), F32)
    common = [key, value, out_grad, cols_h] + list(inside[1:])
    stack0, start3, start2 = call(
        back_own, "back_own", [stack_shape, chunk_shape, chunk_shape], common + [states[0], w_vm]
    )
    stack1, stack2, start3 = call(
        back_sides,
        "back_sides",
        [stack_shape, stack_shape, chunk_shape],
        common + [states[1], states[2], w_vm, start3],
        aliases={10: 2},
    )
    stack3, chunk3_a = call(
        back_first, "back_first", [stack_shape, ((length, part_a), BF16)], common + [states[3], w_vm, start3]
    )
    beside_a = lax.ppermute(chunk3_a, "tp", core)
    late = [stack1, stack2, stack3, w_vm]
    chunk3_b, chunk_a = call(
        back_second, "back_second", [((length, part_b), BF16), ((length, part_a), F32)], late + [start3, start2]
    )
    beside_b = lax.ppermute(chunk3_b, "tp", core)
    chunk_a = (chunk_a + beside_a.astype(F32)).astype(BF16)
    chunk_a, start2 = lax.optimization_barrier((chunk_a, start2))
    across_a = lax.ppermute(chunk_a, "tp", chip)
    (chunk_b,) = call(back_third, "back_third", [((length, part_b), F32)], late + [start2])
    chunk_b = (chunk_b + beside_b.astype(F32)).astype(BF16)
    chunk_b, stack0 = lax.optimization_barrier((chunk_b, stack0))
    across_b = lax.ppermute(chunk_b, "tp", chip)
    attn, chunk_own = call(
        back_mine,
        "back_mine",
        [sum_shape, chunk_shape],
        [stack0] + late + [query, cols_h, inside[0]] + states,
        out_spaces="hv",
        scratch=[pltpu.VMEM(sum_shape[0], F32), pltpu.SemaphoreType.DMA],
    )
    chunk_other, chunk_own = call(
        back_other,
        "back_other",
        [((length, part), BF16), chunk_shape],
        [stack0] + late + [across_a, chunk_own],
        flops=step_flops,
        aliases={6: 1},
    )
    beside = [lax.ppermute(c, "tp", core) for c in jnp.split(chunk_other, 4)]
    (across_b,) = call(
        hand_on, "hand_on", [(across_b.shape, BF16)], [across_b], flops=8 * step_flops, aliases={0: 0}
    )
    (input_grad,) = call(
        last_sum,
        "last_sum",
        [chunk_shape],
        [chunk_own, across_b] + beside,
        out_spaces="h",
        scratch=[pltpu.VMEM(chunk_shape[0], F32), pltpu.SemaphoreType.DMA((len(beside),))],
    )
    return attn, input_grad


def solution(mesh):
    placed = (P("seq", "tp"), P(None, None, "tp"), P("seq", "tp"), P("seq", "tp"), P())
    return jax.shard_map(
        local,
        mesh=mesh,
        in_specs=placed,
        out_specs=(P("seq", "tp"), P("seq", "tp")),
        check_vma=False,
    )
```

```python
import functools

import jax
import jax.numpy as jnp
from jax import lax
from jax.experimental import pallas as pl
from jax.experimental.pallas import tpu as pltpu
from jax.sharding import PartitionSpec as P

DH = 128
F32 = jnp.float32
BF16 = jnp.bfloat16
MIB = 1 << 20


def dot(a, b, ca, cb):
    return lax.dot_general(a, b, (((ca,), (cb,)), ((), ())), preferred_element_type=F32)


def split(a):
    high = a.astype(BF16)
    return high, (a - high.astype(F32)).astype(BF16)


def dot_split(a, b, ca, cb):
    high, low = split(a)
    return dot(high, b, ca, cb) + dot(low, b, ca, cb)


def call(kernel, name, outs, args, spaces=None, flops=0, limit=4, aliases=None, scratch=(), out_spaces=None):
    spaces = spaces or "v" * len(args)
    out_spaces = out_spaces or "v" * len(outs)
    kinds = {"v": pltpu.VMEM, "s": pltpu.SMEM, "h": pltpu.HBM}
    placed = [
        a if s == "s" else pltpu.with_memory_space_constraint(a, kinds[s])
        for a, s in zip(args, spaces)
    ]
    return pl.pallas_call(
        kernel,
        name=name,
        out_shape=[kinds[s](shape, dtype) for s, (shape, dtype) in zip(out_spaces, outs)],
        in_specs=[pl.BlockSpec(memory_space=kinds[s]) for s in spaces],
        out_specs=[pl.BlockSpec(memory_space=kinds[s]) for s in out_spaces],
        input_output_aliases=aliases or {},
        scratch_shapes=scratch,
        compiler_params=pltpu.CompilerParams(vmem_limit_bytes=limit * MIB),
        cost_estimate=pl.CostEstimate(flops=flops, bytes_accessed=0, transcendentals=0),
    )(*placed)


def tiles(width):
    tile = 256 if width % 256 == 0 else 128
    return [slice(i, i + tile) for i in range(0, width, tile)]


def rows_of(which, part, offset=0, size=None):
    size = size or part
    return pl.ds(pl.multiple_of((lax.axis_index("tp") ^ which) * part + offset, size), size)


def group_place():
    place = lax.axis_index("seq")
    return place % 4, place // 4


def order_of(turn):
    odd = lax.axis_index("tp") % 2
    return (0, 1 + odd, 2 - odd, 3)[turn]


def pick(index, values):
    out = values[-1]
    for i in reversed(range(len(values) - 1)):
        out = jnp.where(index == i, values[i], out)
    return out


def prepare(lengths, forget, cols_h, rows_h, through):
    heads, count = forget.shape
    offset = lax.axis_index("seq") * count
    t = lax.broadcasted_iota(jnp.int32, (count, count), 0)
    s = lax.broadcasted_iota(jnp.int32, (count, count), 1)
    lower = jnp.where(s <= t, 1.0, 0.0).astype(BF16)
    high, rest = split(forget[...])
    rest = forget[...] - high.astype(F32)
    middle, low = split(rest)

    def weights(axis):
        if axis:
            total = dot(high, lower, 1, 1) + (dot(middle, lower, 1, 1) + dot(low, lower, 1, 1))
        else:
            total = dot(lower, high, 1, 1) + (dot(lower, middle, 1, 1) + dot(lower, low, 1, 1))
        shape = (1, count) if axis else (count, 1)
        position = offset + lax.broadcasted_iota(jnp.int32, shape, axis)
        first, end = jnp.zeros(shape, jnp.int32), jnp.int32(0)
        for j in range(lengths.shape[0]):
            end = end + lengths[j]
            first = jnp.where(position >= end, end, first)
        first = first - offset
        last = lax.slice_in_dim(first, count - 1, count, axis=axis)
        final = lax.slice_in_dim(total, count - 1, count, axis=axis)
        lead = jnp.where(first < 0, jnp.exp(total), 0.0)
        tail = jnp.where(first == last, jnp.exp(jnp.where(first == last, final - total, 0.0)), 0.0)
        return total, lead, tail, first

    total, lead, tail, first = weights(0)
    cols_h[:, :heads] = total
    cols_h[:, heads : 2 * heads] = lead
    cols_h[:, 2 * heads : 3 * heads] = tail
    cols_h[:, 3 * heads : 3 * heads + 1] = first.astype(F32)
    total, lead, tail, first = weights(1)
    rows_h[:heads, :] = total
    rows_h[heads : 2 * heads, :] = lead
    rows_h[2 * heads :, :] = tail
    factor = jnp.broadcast_to(lead[:, count - 1 :], (heads, DH))
    through[...] = jnp.concatenate(split(factor), axis=0)


def load_and_project(lengths, forget, tokens, w, w_vm, acc, cols_h, rows_h, through, lengths_sm, forget_vm, own, sems):
    part = tokens.shape[1]
    count = w.shape[1] // part
    small = [
        pltpu.make_async_copy(lengths, lengths_sm, sems.at[count]),
        pltpu.make_async_copy(forget, forget_vm, sems.at[count + 1]),
        pltpu.make_async_copy(tokens, own, sems.at[count + 2]),
    ]
    copies = []
    for j in range(count):
        rows = rows_of(j, part)
        copies.append(pltpu.make_async_copy(w.at[:, rows, :], w_vm.at[:, rows, :], sems.at[j]))
    for copy in small + copies:
        copy.start()
    for copy in small:
        copy.wait()
    prepare(lengths_sm, forget_vm, cols_h, rows_h, through)
    copies[0].wait()
    for m in range(3):
        for cols in tiles(w.shape[2]):
            acc[m, :, cols] = dot(own[...], w_vm[m, rows_of(0, part), cols], 1, 0)
    for copy in copies[1:]:
        copy.wait()


def project_chunks(pieces, *refs):
    xs, (w, acc_in, acc) = refs[: len(pieces)], refs[len(pieces) :]
    for m in range(3):
        for cols in tiles(w.shape[2]):
            acc[m, :, cols] = acc_in[m, :, cols] + products(pieces, xs, w, m, cols)


def products(pieces, xs, w, m, cols):
    part = w.shape[1] // 4
    total = None
    for (which, offset), x in zip(pieces, xs):
        term = dot(x[...], w[m, rows_of(which, part, offset, x.shape[1]), cols], 1, 0)
        total = term if total is None else total + term
    return total


def project_last(piece, x, w, acc_in, rows_h, own_through, grads, query, key, value, mine, to1, to2, to3, states):
    for m, out in ((1, key), (2, value), (0, query)):
        for cols in tiles(w.shape[2]):
            out[:, cols] = (acc_in[m, :, cols] + products([piece], [x], w, m, cols)).astype(BF16)
    own_states(query, key, value, grads, rows_h, states)
    quarter = mine.shape[1]
    place = group_place()[0]
    for d, to in enumerate((mine, to1, to2, to3)):
        for i in range(2):
            for j in range(quarter):
                state = states[i, (place ^ order_of(d)) * quarter + j]
                if d:
                    first = (i * quarter + j) * DH
                    to[first : first + DH, :] = state.astype(BF16)
                else:
                    to[i, j] = state
        if d:
            to[2 * quarter * DH :, :] = own_through[...]


def columns(cols_h, h):
    heads = cols_h.shape[1] // 3
    return [cols_h[:, i * heads + h : i * heads + h + 1] for i in range(3)]


def state_end(key, value, rows_h, h):
    cols = slice(h * DH, (h + 1) * DH)
    heads = rows_h.shape[0] // 3
    return dot_split(key[:, cols].T.astype(F32) * rows_h[2 * heads + h : 2 * heads + h + 1, :], value[:, cols], 1, 0)


def grad_start(query, grads, rows_h, h):
    cols = slice(h * DH, (h + 1) * DH)
    heads = rows_h.shape[0] // 3
    weight = rows_h[heads + h : heads + h + 1, :] * (1.0 / DH)
    return dot_split(query[:, cols].T.astype(F32) * weight, grads[:, cols], 1, 0)


def own_states(query, key, value, grads, rows_h, states):
    for h in range(states.shape[1]):
        states[0, h] = state_end(key, value, rows_h, h)
        states[1, h] = grad_start(query, grads, rows_h, h)


def intra(query, key, value, grads, cols_h, rows_h, out, gq, gk, gv):
    length, heads = query.shape[0], rows_h.shape[0] // 3
    t = lax.broadcasted_iota(jnp.int32, (length, length), 0)
    s = lax.broadcasted_iota(jnp.int32, (length, length), 1)
    mask = (s <= t) & (s.astype(F32) >= cols_h[:, 3 * heads : 3 * heads + 1])
    for h in range(heads):
        cols = slice(h * DH, (h + 1) * DH)
        gap = jnp.where(mask, columns(cols_h, h)[0] - rows_h[h : h + 1, :], 0.0)
        weight = jnp.where(mask, jnp.exp(gap), 0.0)
        q, k, v, g = query[:, cols], key[:, cols], value[:, cols], grads[:, cols]
        scores = split(dot(q, k, 1, 1) * weight)
        dots = split(dot(g, v, 1, 1) * weight)
        out[:, cols] = dot(scores[0], v, 1, 0) + dot(scores[1], v, 1, 0)
        gq[:, cols] = dot(dots[0], k, 1, 0) + dot(dots[1], k, 1, 0)
        gk[:, cols] = dot(dots[0], q, 0, 0) + dot(dots[1], q, 0, 0)
        gv[:, cols] = dot(scores[0], g, 0, 0) + dot(scores[1], g, 0, 0)


def finish_grads(key, value, grads, gq, gk, gv, cols, lead, tail, state, end, gstack, at):
    gstack[0, :, at] = ((gq[:, cols] + dot(grads[:, cols], state, 1, 1) * lead) * (1.0 / DH)).astype(BF16)
    gstack[1, :, at] = (gk[:, cols] * (1.0 / DH) + dot(value[:, cols], end, 1, 1) * tail).astype(BF16)
    gstack[2, :, at] = (gv[:, cols] * (1.0 / DH) + dot(key[:, cols], end, 1, 0) * tail).astype(BF16)


def finish_whole(query, key, value, grads, cols_h, out, gq, gk, gv, both, attn, gstack):
    for h in range(query.shape[1] // DH):
        cols = slice(h * DH, (h + 1) * DH)
        lead, tail = columns(cols_h, h)[1:]
        finish_grads(key, value, grads, gq, gk, gv, cols, lead, tail, both[0, h], both[1, h], gstack, cols)
        attn[:, cols] = (out[:, cols] + dot(query[:, cols], both[0, h], 1, 0) * lead) * (1.0 / DH)


def quarter_heads(d, quarter, cols_h):
    member = group_place()[0] ^ order_of(d)
    for j in range(quarter):
        lead, tail = [pick(member, [columns(cols_h, c * quarter + j)[i] for c in range(4)]) for i in (1, 2)]
        yield j, pl.ds(pl.multiple_of((member * quarter + j) * DH, DH), DH), lead, tail


def quarter_columns(d, w):
    width = w.shape[2] // 4
    return pl.ds(pl.multiple_of((group_place()[0] ^ order_of(d)) * width, width), width)


def finish_quarter(d, key, value, grads, cols_h, gq, gk, gv, states, stack):
    for j, cols, lead, tail in quarter_heads(d, states.shape[1], cols_h):
        at = slice(j * DH, (j + 1) * DH)
        finish_grads(key, value, grads, gq, gk, gv, cols, lead, tail, states[0, j], states[1, j], stack, at)


def back(which, stacks, w, out, offset=0, start=None):
    part = w.shape[1] // 4
    size = out.shape[1]
    rows = rows_of(which, part, offset, size)
    total = None if start is None else start[:, offset : offset + size]
    for d, stack in stacks:
        for m in range(3):
            term = dot(stack[m], w[m, rows, quarter_columns(d, w)], 1, 1)
            total = term if total is None else total + term
    out[...] = total.astype(out.dtype)


def back_own(key, value, grads, cols_h, gq, gk, gv, states, w, stack, out3, out2):
    finish_quarter(0, key, value, grads, cols_h, gq, gk, gv, states, stack)
    back(3, [(0, stack)], w, out3)
    back(2, [(0, stack)], w, out2)


def back_sides(key, value, grads, cols_h, gq, gk, gv, states1, states2, w, start3, stack1, stack2, out3):
    finish_quarter(1, key, value, grads, cols_h, gq, gk, gv, states1, stack1)
    finish_quarter(2, key, value, grads, cols_h, gq, gk, gv, states2, stack2)
    back(3, [(1, stack1), (2, stack2)], w, out3, 0, start3)


def back_first(key, value, grads, cols_h, gq, gk, gv, states, w, start3, stack, chunk3_a):
    finish_quarter(3, key, value, grads, cols_h, gq, gk, gv, states, stack)
    back(3, [(3, stack)], w, chunk3_a, 0, start3)


def back_second(stack1, stack2, stack3, w, start3, start2, chunk3_b, chunk2_a):
    back(3, [(3, stack3)], w, chunk3_b, start3.shape[1] - chunk3_b.shape[1], start3)
    back(2, [(1, stack1), (2, stack2), (3, stack3)], w, chunk2_a, 0, start2)


def back_third(stack1, stack2, stack3, w, start2, chunk2_b):
    back(2, [(1, stack1), (2, stack2), (3, stack3)], w, chunk2_b, start2.shape[1] - chunk2_b.shape[1], start2)


def hand_on(*refs):
    pass


def last_sum(own, across_b, *refs):
    besides, (out, total, sems) = refs[:-3], refs[-3:]
    size, middle = besides[0].shape[0], own.shape[1] - across_b.shape[1]
    copies = []
    for i, beside in enumerate(besides):
        rows = slice(i * size, (i + 1) * size)
        total[rows, :middle] = own[rows, :middle] + beside[:, :middle].astype(F32)
        right = own[rows, middle:] + beside[:, middle:].astype(F32)
        total[rows, middle:] = right + across_b[rows, :].astype(F32)
        copies.append(pltpu.make_async_copy(total.at[rows, :], out.at[rows, :], sems.at[i]))
        copies[-1].start()
    for copy in copies:
        copy.wait()


def back_mine(stack0, stack1, stack2, stack3, w, query, cols_h, out, states0, states1, states2, states3, *refs):
    attn, chunk_own, attn_vm, sem = refs
    for d, states in enumerate((states0, states1, states2, states3)):
        for j, cols, lead, _ in quarter_heads(d, states.shape[1], cols_h):
            attn_vm[:, cols] = (out[:, cols] + dot(query[:, cols], states[0, j], 1, 0) * lead) * (1.0 / DH)
    copy = pltpu.make_async_copy(attn_vm, attn, sem)
    copy.start()
    back(0, list(enumerate((stack0, stack1, stack2, stack3))), w, chunk_own)
    copy.wait()


def back_other(stack0, stack1, stack2, stack3, w, across_a, own_in, chunk_other, own):
    back(1, list(enumerate((stack0, stack1, stack2, stack3))), w, chunk_other)
    middle = across_a.shape[1]
    own[:, :middle] = own_in[:, :middle] + across_a[...].astype(F32)
    own[:, middle:] = own_in[:, middle:]


def per_head(scale, matrix):
    return scale[..., None, None] * matrix


def head_factors(rows):
    half = rows.shape[0] // 2
    return rows[:half].astype(F32) + rows[half:].astype(F32)


def join_kernel(own_through, mine, got1, got2, got3, to_group, inner, factors):
    quarter = mine.shape[1]
    place, group = group_place()
    odd = order_of(1) == 2

    def by_member(first, rows):
        one, two, three = [got[rows, :] for got in (got1, got2, got3)]
        return [first, jnp.where(odd, two, one), jnp.where(odd, one, two), three]

    through = [head_factors(rows) for rows in by_member(own_through[...], slice(2 * quarter * DH, got1.shape[0]))]
    ones = jnp.ones((1, DH), F32)
    for j in range(quarter):
        step = [pick(place, [t[c * quarter + j : c * quarter + j + 1] for c in range(4)]) for t in through]
        step = [pick(place, [step[k ^ p] for p in range(4)]) for k in range(4)]
        totals = []
        for i in range(2):
            first = (i * quarter + j) * DH
            own = [a.astype(F32) for a in by_member(mine[i, j], slice(first, first + DH))]
            own = [pick(place, [own[k ^ p] for p in range(4)]) for k in range(4)]
            order = (0, 1, 2, 3) if i == 0 else (3, 2, 1, 0)
            state, factor = jnp.zeros((DH, DH), F32), ones
            for k in order:
                inner[i, k, j], factors[i, k, j] = state, factor
                state, factor = own[k] + step[k] * state, step[k] * factor
            totals.append(state)
        to_group[j * DH : (j + 1) * DH, :] = jnp.where(group == 0, totals[0], totals[1]).astype(BF16)


def spread_kernel(inner, factors, other, *outs):
    quarter = inner.shape[2]
    place, group = group_place()
    for j in range(quarter):
        arrived = other[j * DH : (j + 1) * DH, :].astype(F32)
        for turn, out in enumerate(outs):
            k = place ^ order_of(turn)
            for i in range(2):
                factor = jnp.where(group == 1 - i, factors[i, k, j], 0.0)
                out[i, j] = (inner[i, k, j] + factor * arrived).astype(BF16)


def to_other_group(a):
    return lax.ppermute(a, "seq", [(i, i ^ 4) for i in range(8)])


def to_member(a, turn):
    seqs, tps = lax.axis_size("seq"), lax.axis_size("tp")
    pairs = []
    for i in range(seqs):
        for t in range(tps):
            partner = i ^ (0, 1 + t % 2, 2 - t % 2, 3)[turn]
            pairs.append((i * tps + t, partner * tps + t))
    return lax.ppermute(a, ("seq", "tp"), pairs)


def states_direct(own_through, mine, messages, inside):
    quarter = mine.shape[1]
    got = [to_member(message, turn) for turn, message in zip((1, 2, 3), messages)]
    inside, mine = lax.optimization_barrier((inside, mine))
    to_group, inner, factors = call(
        join_kernel,
        "join",
        [((quarter * DH, DH), BF16), ((2, 4, quarter, DH, DH), F32), ((2, 4, quarter, 1, DH), F32)],
        [own_through, mine] + got,
    )
    other = to_other_group(to_group)
    states = call(spread_kernel, "spread", [(mine.shape, BF16)] * 4, [inner, factors, other])
    return [states[0]] + [to_member(states[turn], turn) for turn in (1, 2, 3)], inside


def states_gathered(own, through):
    count = lax.axis_size("seq")
    place = lax.axis_index("seq")
    all_own = lax.all_gather(own, "seq")
    all_through = lax.all_gather(through, "seq")

    def pick(a, i):
        return lax.dynamic_index_in_dim(a, i, 0, False)

    def ahead(step, state):
        return per_head(pick(all_through, step), state) + pick(all_own, step)[0]

    def behind(step, state):
        source = count - 1 - step
        return per_head(pick(all_through, source), state) + pick(all_own, source)[1]

    zero = jnp.zeros_like(own[0])
    state = lax.fori_loop(0, place, ahead, zero)
    grad = lax.fori_loop(0, count - 1 - place, behind, zero)
    return jnp.stack([state, grad]).astype(BF16)


def local(tokens, w_qkv, forget, out_grad, doc_lengths):
    length, part = tokens.shape
    width = w_qkv.shape[2]
    heads = width // DH
    tps = lax.axis_size("tp")
    seqs = lax.axis_size("seq")
    by_hand = tps == 4 and seqs == 8 and heads % 4 == 0
    decays = [((length, 3 * heads + 1), F32), ((3 * heads, length), F32), ((2 * heads, DH), BF16)]
    rows_shape = ((length, width), BF16)
    sum_shape = ((length, width), F32)
    intra_flops = 16 * length * length * width
    forget = forget.T
    if not by_hand:
        gathered = lax.all_gather(tokens, "tp", axis=1, tiled=True)
        projected = jnp.einsum("td,mdc->mtc", gathered, w_qkv, preferred_element_type=F32).astype(BF16)
        qkv = [projected[m] for m in range(3)]
        cols_h, rows_h, through = call(prepare, "prepare", decays, [doc_lengths, forget], "sv")
        through = jnp.sum(through.astype(F32).reshape(2, heads, DH), axis=0)[:, 0]
        (own,) = call(own_states, "own_states", [((2, heads, DH, DH), F32)], qkv + [out_grad, rows_h])
        both = states_gathered(own, through)
        inside = call(intra, "intra", [sum_shape] * 4, qkv + [out_grad, cols_h, rows_h], flops=intra_flops)
        attn, gstack = call(
            finish_whole,
            "finish",
            [sum_shape, ((3, length, width), BF16)],
            qkv + [out_grad, cols_h] + list(inside) + [both],
        )
        grad_terms = jnp.einsum("mtc,mdc->td", gstack, w_qkv, preferred_element_type=F32)
        return attn, lax.psum_scatter(grad_terms, "tp", scatter_dimension=1, tiled=True)

    quarter = heads // 4
    core = [(i, i ^ 1) for i in range(4)]
    chip = [(i, i ^ 2) for i in range(4)]
    step_flops = 2 * 3 * length * part * width
    across = lax.ppermute(tokens, "tp", chip)
    beside = lax.ppermute(tokens, "tp", core)
    w_vm, acc, cols_h, rows_h, through = call(
        load_and_project,
        "load_and_project",
        [(w_qkv.shape, BF16), ((3, length, width), F32)] + decays,
        [doc_lengths, forget, tokens, w_qkv],
        "hhhh",
        flops=8 * step_flops,
        scratch=[
            pltpu.SMEM(doc_lengths.shape, jnp.int32),
            pltpu.VMEM(forget.shape, F32),
            pltpu.VMEM(tokens.shape, BF16),
            pltpu.SemaphoreType.DMA((tps + 3,)),
        ],
    )

    def project(name, acc, *pieces):
        kernel = functools.partial(project_chunks, [place for place, _ in pieces])
        return call(kernel, name, [(acc.shape, F32)], [x for _, x in pieces] + [w_vm, acc])[0]

    acc = project("project_beside", acc, ((1, 0), beside))
    across, acc = lax.optimization_barrier((across, acc))
    across_beside = lax.ppermute(across, "tp", core)
    acc = project("project_across", acc, ((2, 0), across))
    last = (3, 0)
    message_shape = ((2 * quarter * DH + through.shape[0], DH), BF16)
    query, key, value, mine, *messages = call(
        functools.partial(project_last, last),
        "project_last",
        [rows_shape] * 3 + [((2, quarter, DH, DH), F32)] + [message_shape] * 3,
        [across_beside, w_vm, acc, rows_h, through, out_grad],
        scratch=[pltpu.VMEM((2, heads, DH, DH), F32)],
    )
    inside = call(
        intra, "intra", [sum_shape] * 4, [query, key, value, out_grad, cols_h, rows_h], flops=intra_flops
    )
    states, inside = states_direct(through, mine, messages, inside)

    part_a = part // 2
    part_b = part - part_a
    stack_shape = ((3, length, width // 4), BF16)
    chunk_shape = ((length, part), F32)
    common = [key, value, out_grad, cols_h] + list(inside[1:])
    stack0, start3, start2 = call(
        back_own, "back_own", [stack_shape, chunk_shape, chunk_shape], common + [states[0], w_vm]
    )
    stack1, stack2, start3 = call(
        back_sides,
        "back_sides",
        [stack_shape, stack_shape, chunk_shape],
        common + [states[1], states[2], w_vm, start3],
        aliases={10: 2},
    )
    stack3, chunk3_a = call(
        back_first, "back_first", [stack_shape, ((length, part_a), BF16)], common + [states[3], w_vm, start3]
    )
    beside_a = lax.ppermute(chunk3_a, "tp", core)
    late = [stack1, stack2, stack3, w_vm]
    chunk3_b, chunk_a = call(
        back_second, "back_second", [((length, part_b), BF16), ((length, part_a), F32)], late + [start3, start2]
    )
    beside_b = lax.ppermute(chunk3_b, "tp", core)
    chunk_a = (chunk_a + beside_a.astype(F32)).astype(BF16)
    chunk_a, start2 = lax.optimization_barrier((chunk_a, start2))
    across_a = lax.ppermute(chunk_a, "tp", chip)
    (chunk_b,) = call(back_third, "back_third", [((length, part_b), F32)], late + [start2])
    chunk_b = (chunk_b + beside_b.astype(F32)).astype(BF16)
    chunk_b, stack0 = lax.optimization_barrier((chunk_b, stack0))
    across_b = lax.ppermute(chunk_b, "tp", chip)
    attn, chunk_own = call(
        back_mine,
        "back_mine",
        [sum_shape, chunk_shape],
        [stack0] + late + [query, cols_h, inside[0]] + states,
        out_spaces="hv",
        scratch=[pltpu.VMEM(sum_shape[0], F32), pltpu.SemaphoreType.DMA],
    )
    chunk_other, chunk_own = call(
        back_other,
        "back_other",
        [((length, part), BF16), chunk_shape],
        [stack0] + late + [across_a, chunk_own],
        flops=step_flops,
        aliases={6: 1},
    )
    beside = [lax.ppermute(c, "tp", core) for c in jnp.split(chunk_other, 4)]
    (across_b,) = call(
        hand_on, "hand_on", [(across_b.shape, BF16)], [across_b], flops=8 * step_flops, aliases={0: 0}
    )
    (input_grad,) = call(
        last_sum,
        "last_sum",
        [chunk_shape],
        [chunk_own, across_b] + beside,
        out_spaces="h",
        scratch=[pltpu.VMEM(chunk_shape[0], F32), pltpu.SemaphoreType.DMA((len(beside),))],
    )
    return attn, input_grad


def solution(mesh):
    placed = (P("seq", "tp"), P(None, None, "tp"), P("seq", "tp"), P("seq", "tp"), P())
    return jax.shard_map(
        local,
        mesh=mesh,
        in_specs=placed,
        out_specs=(P("seq", "tp"), P("seq", "tp")),
        check_vma=False,
    )
```
